128 devices in a mesh: dp: 64 (over z_lo, y, x, core), tensor: 2 (over z_hi).
Axes of the slice: x: 4, y: 4, z: 4 (z_hi: 2, z_lo: 2; z = z_hi * 2 + z_lo), core: 2. Of those that a mesh axis runs over, the one named last changes fastest.
Arguments:
- tokens: bfloat16 [16384, 768], P(('dp', 'tensor')), may hold values from -24 to 24
- clip_bounds: int32 [2, 16384], P(None, 'dp'), may hold values from 0 to 16384, as said below
- attn_in: bfloat16 [1, 3, 768, 768], P(None, None, 'dp', 'tensor'), may hold values from -0.21875 to 0.21875
- qv_bias: bfloat16 [1, 2, 12, 64], P(None, None, 'tensor', 'dp'), may hold values from -3 to 3
- out_proj: bfloat16 [1, 768, 768], P(None, 'tensor', 'dp'), may hold values from -4 to 4
- fc_in: bfloat16 [1, 768, 3072], P(None, 'dp', 'tensor'), may hold values from -0.21875 to 0.21875
- fc_bias: bfloat16 [1, 12, 256], P(None, 'tensor', 'dp'), may hold values from -3 to 3
- fc_out: bfloat16 [1, 3072, 768], P(None, 'tensor', 'dp'), may hold values from -0.109375 to 0.109375
- ln_gain: bfloat16 [1, 2, 768], P(None, None, ('dp', 'tensor')), may hold values from 0.5 to 1.5
- row_bias: bfloat16 [1, 4, 768], P(None, None, ('dp', 'tensor')), may hold values from -2 to 2
- cotangent: bfloat16 [16384, 768], P(('dp', 'tensor')), may hold values from -24 to 24
Outputs:
- output: bfloat16 [16384, 768], P(('dp', 'tensor'))
- grad_tokens: float32 [16384, 768], P(('dp', 'tensor'))
- grad_attn_in: float32 [1, 3, 768, 768], P(None, None, 'dp', 'tensor')
- grad_qv_bias: float32 [1, 2, 12, 64], P(None, None, 'tensor', 'dp')
- grad_out_proj: float32 [1, 768, 768], P(None, 'tensor', 'dp')
- grad_fc_in: float32 [1, 768, 3072], P(None, 'dp', 'tensor')
- grad_fc_bias: float32 [1, 12, 256], P(None, 'tensor', 'dp')
- grad_fc_out: float32 [1, 3072, 768], P(None, 'tensor', 'dp')
- grad_ln_gain: float32 [1, 2, 768], P(None, None, ('dp', 'tensor'))
- grad_row_bias: float32 [1, 4, 768], P(None, None, ('dp', 'tensor'))
The draws below stay inside these ranges and needn't reach their ends.
Inputs may be any that keep to these rules, and one draw needn't show every extreme that they name: `clip_bounds`: row 0 holds the position of the first token of each token's clip and row 1 the position one past its last; clips are runs of consecutive tokens of at most 1500 tokens, and one clip has exactly 1500.
All inputs are finite; a program needn't handle non-finite values.
Results may differ from the reference program's by a relative error of at most 0.017.
Values may be sent and summed in bfloat16 or wider, within the bound.
A program may use at most 128 MiB of HBM per device.

```python
import math
import jax
import jax.numpy as jnp
from jax import lax

D = 768
H = 12
HD = 64
FF = 3072
CLIP = 1500
BLOCK = 256
LAYERS = 1
TOKENS = 16384
FGRP = 256
N_DP = 64


def draw_clip_bounds(key, part):
    key = jax.random.fold_in(key, 7)
    reach = (CLIP + BLOCK - 2) // BLOCK
    least = max(1, reach * BLOCK - CLIP + 1)
    count = TOKENS // (CLIP // 2) + 3
    first_key, other_key = jax.random.split(key)
    leading = jax.random.randint(first_key, (1,), least, BLOCK).astype(jnp.int32)
    others = jax.random.randint(other_key, (count,), CLIP // 2, CLIP + 1).astype(jnp.int32)
    lengths = jnp.concatenate([leading, jnp.full((1,), CLIP, jnp.int32), others]).astype(jnp.int32)
    ends = jnp.cumsum(lengths).astype(jnp.int32)
    starts = (ends - lengths).astype(jnp.int32)
    positions = jnp.arange(TOKENS, dtype=jnp.int32)
    which = jnp.sum((positions[:, None] >= ends[None, :]).astype(jnp.int32), axis=1).astype(jnp.int32)
    first = starts[which]
    beyond = jnp.minimum(ends[which], TOKENS)
    return jnp.stack([first, beyond]).astype(jnp.int32)


def spiked(drawn, key, source, target, shards_of, factor):
    owner, partner = [(jnp.arange(drawn.shape[axis_at]) // (drawn.shape[axis_at] // shards_of)).reshape([-1 if axis == axis_at else 1 for axis in range(drawn.ndim)]) for axis_at in (source, target)]
    chosen = jax.random.permutation(key, shards_of)[partner]
    strong = (owner == chosen) | (owner == (partner + shards_of // 2) % shards_of)
    return jnp.where(strong, factor * drawn, drawn)


def block_levels(rng, dims, shards, low, largest):
    loudness, own = 1.0, jax.random.fold_in(rng, 6)
    for dim, shards_of in shards:
        steps = jnp.exp(jax.random.uniform(jax.random.fold_in(own, dim), (shards_of,), jnp.float32, low / len(shards), largest / len(shards)))
        loudness = loudness * jnp.repeat(steps, dims[dim] // shards_of).reshape([-1 if axis == dim else 1 for axis in range(len(dims))])
    return loudness


def gaussian(own_key, dims, width, limit, pieces=(), held_as=jnp.bfloat16):
    entries = width * jax.random.normal(own_key, dims, jnp.float32)
    if pieces:
        entries = entries * block_levels(own_key, dims, pieces, -0.22, 0.18)
    return jnp.clip(entries, -limit, limit).astype(held_as)


def heavy_noise(key, extent, scale, bound, cuts, heavy, kind=jnp.bfloat16):
    values = scale * jax.random.normal(key, extent, jnp.float32)
    if cuts:
        values = values * block_levels(key, extent, cuts, -0.22, 0.18)
    return jnp.clip(spiked(values, jax.random.fold_in(key, 3), *heavy), -bound, bound).astype(kind)


def setup_inputs(seed: int = 0) -> dict:
    key_list = jax.random.split(jax.random.key(seed), 12)
    tokens = heavy_noise(key_list[0], (TOKENS, D), 1.0, 24.0, ((0, 128),), (0, 1, 128, 5.5))
    clip_bounds = draw_clip_bounds(jax.random.fold_in(key_list[11], 71), 0)
    attn_in = gaussian(key_list[2], (LAYERS, 3, D, D), D ** -0.5, 0.21875, ((2, 64), (3, 2)))
    qv_bias = gaussian(key_list[3], (LAYERS, 2, H, HD), 0.5, 3.0, ((2, 2), (3, 64)))
    out_proj = gaussian(key_list[4], (LAYERS, D, D), (max(1, D * 4 // CLIP)) ** -0.5, 4.0, ((1, 2), (2, 64)))
    fc_in = gaussian(key_list[5], (LAYERS, D, FF), D ** -0.5, 0.21875, ((1, 64), (2, 2)))
    fc_bias = gaussian(key_list[6], (LAYERS, H, FGRP), 0.5, 3.0, ((1, 2), (2, 64)))
    fc_out = gaussian(key_list[7], (LAYERS, FF, D), FF ** -0.5, 0.109375, ((1, 2), (2, 64)))
    ln_gain = jnp.clip(1.0 + 0.1 * jax.random.normal(key_list[8], (LAYERS, 2, D), jnp.float32), 0.5, 1.5).astype(jnp.bfloat16)
    row_bias = gaussian(key_list[9], (LAYERS, 4, D), 0.3, 2.0, ((2, 128),))
    cotangent = heavy_noise(key_list[10], (TOKENS, D), 1.0, 24.0, ((0, 128),), (0, 1, 128, 5.5))
    return dict(tokens=tokens, clip_bounds=clip_bounds, attn_in=attn_in, qv_bias=qv_bias, out_proj=out_proj, fc_in=fc_in, fc_bias=fc_bias, fc_out=fc_out, ln_gain=ln_gain, row_bias=row_bias, cotangent=cotangent)


@jax.custom_vjp
def low(v):
    return lax.optimization_barrier(v.astype(jnp.bfloat16)).astype(jnp.float32)

@jax.custom_vjp
def low_back(v):
    return v

def low_keep(v):
    return (low(v), None)

def low_pass(kept, grad):
    return (grad,)

def back_keep(v):
    return (v, None)

def back_low(kept, grad):
    return (low(grad),)
low.defvjp(low_keep, low_pass)
low_back.defvjp(back_keep, back_low)
EPS = 1e-05
HIGHEST = lax.Precision.HIGHEST
NEGATIVE = -1e+30

def dense(left, right):
    return jnp.dot(left, right, precision=HIGHEST)

def layer_norm(hidden, gain, offset):
    average = lax.optimization_barrier(jnp.mean(hidden, axis=-1, keepdims=True))
    centred = hidden - average
    spread = lax.optimization_barrier(jnp.mean(centred * centred, axis=-1, keepdims=True))
    return centred * lax.rsqrt(spread + EPS) * gain + offset

def attention(query, keys, values, bounds):
    total = query.shape[0]
    reach = (CLIP + BLOCK - 2) // BLOCK
    margin = reach * BLOCK
    group = BLOCK * math.gcd(N_DP, max(1, 512 // BLOCK))
    padded_keys = jnp.pad(keys, ((margin, margin), (0, 0), (0, 0)))
    padded_values = jnp.pad(values, ((margin, margin), (0, 0), (0, 0)))
    positions = jnp.arange(total + 2 * margin, dtype=jnp.int32) - margin

    def one_group(index):
        begin = (index * group).astype(jnp.int32)
        rows = lax.dynamic_slice_in_dim(query, begin, group, 0)
        first = lax.dynamic_slice_in_dim(bounds[0], begin, group, 0)
        beyond = lax.dynamic_slice_in_dim(bounds[1], begin, group, 0)
        near_keys = lax.dynamic_slice_in_dim(padded_keys, begin, group + 2 * margin, 0)
        near_values = lax.dynamic_slice_in_dim(padded_values, begin, group + 2 * margin, 0)
        near_positions = lax.dynamic_slice_in_dim(positions, begin, group + 2 * margin, 0)
        scores = low_back(0.125 * jnp.einsum('qhd,khd->hqk', rows, near_keys, precision=HIGHEST))
        allowed = (near_positions[None, :] >= first[:, None]) & (near_positions[None, :] < beyond[:, None])
        scores = jnp.where(allowed[None], scores, NEGATIVE)
        weights = jax.nn.softmax(scores, axis=-1)
        return jnp.einsum('hqk,khd->qhd', low(weights), near_values, precision=HIGHEST)
    blocks = lax.map(jax.checkpoint(one_group), jnp.arange(total // group, dtype=jnp.int32))
    return blocks.reshape(total, H * HD)

def forward(stream_in, attn_in, qv_bias, out_proj, fc_in, fc_bias, fc_out, ln_gain, row_bias, bounds):
    total = stream_in.shape[0]
    hidden = stream_in
    for layer in range(LAYERS):
        normed = low(layer_norm(hidden, ln_gain[layer, 0], row_bias[layer, 0]))
        query = low(low_back(dense(normed, attn_in[layer, 0]) + qv_bias[layer, 0].reshape(-1)))
        keys = low(low_back(dense(normed, attn_in[layer, 1])))
        values = low(low_back(dense(normed, attn_in[layer, 2]) + qv_bias[layer, 1].reshape(-1)))
        mixed = attention(query.reshape(total, H, HD), keys.reshape(total, H, HD), values.reshape(total, H, HD), bounds)
        mixed = low(low_back(mixed))
        hidden = hidden + low_back(dense(mixed, out_proj[layer]) + row_bias[layer, 1])
        normed = low(layer_norm(hidden, ln_gain[layer, 1], row_bias[layer, 2]))
        inner = low_back(dense(normed, fc_in[layer]) + fc_bias[layer].reshape(-1))
        active = low(jax.nn.gelu(inner, approximate=False))
        hidden = hidden + low_back(dense(active, fc_out[layer]) + row_bias[layer, 3])
    return hidden

def reference(tokens, clip_bounds, attn_in, qv_bias, out_proj, fc_in, fc_bias, fc_out, ln_gain, row_bias, cotangent):
    floats = (tokens.astype(jnp.float32), attn_in.astype(jnp.float32), qv_bias.astype(jnp.float32), out_proj.astype(jnp.float32), fc_in.astype(jnp.float32), fc_bias.astype(jnp.float32), fc_out.astype(jnp.float32), ln_gain.astype(jnp.float32), row_bias.astype(jnp.float32))

    def wrapped(*params):
        return forward(*params, clip_bounds)
    result, pullback = jax.vjp(wrapped, *floats)
    grads = pullback(cotangent.astype(jnp.float32))
    return (result.astype(jnp.bfloat16), grads[0], grads[1], grads[2], grads[3], grads[4], grads[5], grads[6], grads[7], grads[8])
```

```python
import jax
import jax.numpy as jnp
from jax import lax
import jax.experimental.pallas as pl
import jax.experimental.pallas.tpu as pltpu
from jax.sharding import PartitionSpec as P

EPS = 1e-05
NEGATIVE = -1e30
SCORE_SCALE = 0.125
BF = jnp.bfloat16
F32 = jnp.float32
MESH = pl.DeviceIdType.MESH
VM = pl.BlockSpec(memory_space=pltpu.VMEM)
SM = pl.BlockSpec(memory_space=pltpu.SMEM)
DMA = pltpu.SemaphoreType.DMA
LIMIT = 56 * 2**20
NT = (((1,), (1,)), ((), ()))
TN = (((0,), (0,)), ((), ()))


def coords():
    dp = lax.axis_index("dp")
    return dp // 32, (dp // 8) % 4, (dp // 2) % 4, dp % 2, lax.axis_index("tensor")


def device(z, y, x, k, t):
    return (((z * 4 + y) * 4 + x) * 2 + k, t)


def chip(c, k, t):
    return (c * 2 + k, t)


def greet(peers):
    bar = pltpu.get_barrier_semaphore()
    for peer in peers:
        pl.semaphore_signal(bar, inc=1, device_id=peer, device_id_type=MESH)
    pl.semaphore_wait(bar, len(peers))


def remote(src, dst, sems, index, peer):
    send, recv = sems
    return pltpu.make_async_remote_copy(
        src, dst, send.at[index], recv.at[index], device_id=peer, device_id_type=MESH
    )


def comm_call(kernel, out_shape, scratch, cid, name, args):
    single = not isinstance(out_shape, (list, tuple))
    return pl.pallas_call(
        kernel,
        out_shape=out_shape,
        in_specs=[VM] * len(args),
        out_specs=VM if single else [VM] * len(out_shape),
        scratch_shapes=scratch,
        compiler_params=pltpu.CompilerParams(
            collective_id=cid, has_side_effects=True, vmem_limit_bytes=LIMIT
        ),
        name=name,
    )(*args)


def gather_kernel(pay, tile, clip, cot, w, clip_out, cot_out, pay_s, tile_in, send, recv):
    sems = (send, recv)
    z, y, x, k, t = coords()
    xs = [device(z, y, (x + d) % 4, k, t) for d in (1, 2, 3)]
    ys = [device(z, (y + d) % 4, x, k, t) for d in (1, 2, 3)]
    core = device(z, y, x, 1 - k, t)
    far = device(z, y, x, k, 1 - t)
    both = device(z, y, x, 1 - k, 1 - t)
    low = device(1 - z, y, x, k, t)
    greet(xs + ys + [core, far, both, low])
    c_tile = remote(tile, tile_in, sems, 0, far)
    c_tile.start()
    c_clip = remote(clip, clip_out.at[k], sems, 1, core)
    c_clip.start()
    mine = k * 2 + t
    c_cot = [remote(cot, cot_out.at[mine], sems, 2 + i, p) for i, p in enumerate((core, far, both))]
    clip_out[k] = clip[...]
    cot_out[mine] = cot[...]
    c_tile.wait()
    pay_s[...] = pay[...]
    for q in range(2):
        pay_s[q, :, 0:128] = pay[q, :, 0:128] + tile_in[...]
    swap = remote(pay_s.at[1 - k], w.at[z, y, x, k], sems, 5, core)
    swap.start()
    w[z, y, x, k] = pay_s[k]
    swap.wait()
    c_z = remote(w.at[z, y, x], w.at[z, y, x], sems, 6, low)
    c_z.start()
    c_z.wait()
    h0, h1 = pl.ds(0, 1152), pl.ds(1152, 1152)
    phase = []
    for i in range(3):
        a = w.at[:, y, x, :, :, h0]
        phase.append(remote(a, a, sems, 7 + i, xs[i]))
        b = w.at[:, y, x, :, :, h1]
        phase.append(remote(b, b, sems, 10 + i, ys[i]))
    for c in phase:
        c.start()
    for c in c_cot:
        c.start()
    for c in phase:
        c.wait()
    phase = []
    for i in range(3):
        a = w.at[:, y, :, :, :, h0]
        phase.append(remote(a, a, sems, 13 + i, ys[i]))
        b = w.at[:, :, x, :, :, h1]
        phase.append(remote(b, b, sems, 16 + i, xs[i]))
    for c in phase:
        c.start()
    for c in phase:
        c.wait()
    c_clip.wait()
    for c in c_cot:
        c.wait()


def gather_all(pay, tile, clip, cot):
    return comm_call(
        gather_kernel,
        [
            jax.ShapeDtypeStruct((2, 4, 4, 2, 16, 2304), BF),
            jax.ShapeDtypeStruct((2, 2, 256), jnp.int32),
            jax.ShapeDtypeStruct((4, 128, 768), BF),
        ],
        [pltpu.VMEM((2, 16, 2304), BF), pltpu.VMEM((16, 128), BF), DMA((19,)), DMA((19,))],
        0,
        "gather_weights",
        (pay, tile, clip, cot),
    )


def rows_kernel(a, out, send, recv):
    sems = (send, recv)
    z, y, x, k, t = coords()
    core = device(z, y, x, 1 - k, t)
    far = device(z, y, x, k, 1 - t)
    greet([core, far])
    mine, other = k * 2 + t, k * 2 + 1 - t
    c_far = remote(a, out.at[mine], sems, 0, far)
    c_far.start()
    c_core = remote(a, out.at[mine], sems, 1, core)
    c_core.start()
    out[mine] = a[...]
    c_far.wait_recv()
    c_pass = remote(out.at[other], out.at[other], sems, 2, core)
    c_pass.start()
    c_far.wait_send()
    c_core.wait()
    c_pass.wait()


def gather_rows(a, cid, name):
    full = comm_call(
        rows_kernel,
        jax.ShapeDtypeStruct((4, 128, 768), BF),
        [DMA((3,)), DMA((3,))],
        cid,
        name,
        (a,),
    )
    return full.reshape(512, 768)


def sum_kernel(p, out, got, send, recv):
    sems = (send, recv)
    z, y, x, k, t = coords()
    flips = ((0, 1), (1, 1), (1, 0))
    peers = [((k + dk) % 2, (t + dt) % 2) for dk, dt in flips]
    greet([device(z, y, x, pk, pt) for pk, pt in peers])
    copies = []
    for i, (pk, pt) in enumerate(peers):
        copies.append(
            remote(p.at[:, pk * 2 + pt], got.at[i], sems, i, device(z, y, x, pk, pt))
        )
        copies[-1].start()
    for c in copies:
        c.wait()
    total = p[:, k * 2 + t].astype(F32)
    for i in range(3):
        total = total + got[i].astype(F32)
    out[...] = total


def sum_rows(p, cid, name):
    n = p.shape[0]
    return comm_call(
        sum_kernel,
        jax.ShapeDtypeStruct((n, 128, 768), F32),
        [pltpu.VMEM((3, n, 128, 768), BF), DMA((3,)), DMA((3,))],
        cid,
        name,
        (p,),
    )


def ring(c, k, t):
    return [chip((c + d) % 32, k, t) for d in (1, 2, 3, 29, 30, 31)]


SLOTS = (4, 5, 6, 0, 1, 2)


def halo_kernel(kv, out, send, recv):
    sems = (send, recv)
    dp = lax.axis_index("dp")
    c, k, t = dp // 2, dp % 2, lax.axis_index("tensor")
    peers = ring(c, k, t)
    greet(peers)
    copies = []
    for i in (1, 4, 0, 5, 2, 3):
        copies.append(remote(kv, out.at[6 - SLOTS[i]], sems, i, peers[i]))
        copies[-1].start()
    out[3] = kv[...]
    for cp in copies:
        cp.wait()


def halo(kv):
    return comm_call(
        halo_kernel,
        jax.ShapeDtypeStruct((7, 512, 384), BF),
        [DMA((6,)), DMA((6,))],
        1,
        "halo_kv",
        (kv,),
    )


def halo_back_kernel(d, out, got, send, recv):
    sems = (send, recv)
    dp = lax.axis_index("dp")
    c, k, t = dp // 2, dp % 2, lax.axis_index("tensor")
    peers = ring(c, k, t)
    greet(peers)
    copies = []
    for i in (1, 4, 0, 5, 2, 3):
        copies.append(remote(d.at[SLOTS[i]], got.at[i], sems, i, peers[i]))
        copies[-1].start()
    for cp in copies:
        cp.wait()

    @pl.loop(0, 8)
    def _(r):
        rows = pl.ds(pl.multiple_of(r * 64, 64), 64)
        total = d[3, rows, :].astype(F32)
        for i in range(6):
            total = total + got[i, rows, :].astype(F32)
        out[rows, :] = total.astype(BF)


def halo_back(d):
    return comm_call(
        halo_back_kernel,
        jax.ShapeDtypeStruct((512, 384), BF),
        [pltpu.VMEM((6, 512, 384), BF), DMA((6,)), DMA((6,))],
        2,
        "halo_back",
        (d,),
    )


def reduce_kernel(g, out, tile_out, b0, b1, s0, s1, a0, a1, u0, u1, f0, f1, res, tile, send, recv):
    sems = (send, recv)
    z, y, x, k, t = coords()
    px = [(x + d) % 4 for d in (1, 2, 3)]
    py = [(y + d) % 4 for d in (1, 2, 3)]
    xs = [device(z, y, p, k, t) for p in px]
    ys = [device(z, p, x, k, t) for p in py]
    core = device(z, y, x, 1 - k, t)
    far = device(z, y, x, k, 1 - t)
    low = device(1 - z, y, x, k, t)
    greet(xs + ys + [core, far, low])
    h0, h1 = pl.ds(0, 1152), pl.ds(1152, 1152)
    first, second = [], []
    for i in range(3):
        first.append(remote(g.at[:, py[i], :, :, :, h0], b0.at[i], sems, i, ys[i]))
        second.append(remote(g.at[:, :, px[i], :, :, h1], b1.at[i], sems, 3 + i, xs[i]))
        first[-1].start()
        second[-1].start()
    for c in first:
        c.wait()

    @pl.loop(0, 8)
    def _(n):
        zz, m = n // 4, n % 4
        v = g[zz, y, m, :, :, 0:1152].astype(F32)
        for i in range(3):
            v = v + b0[i, zz, m].astype(F32)
        s0[zz, m] = v.astype(BF)

    first = []
    for i in range(3):
        first.append(remote(s0.at[:, px[i]], a0.at[i], sems, 6 + i, xs[i]))
        first[-1].start()
    for c in second:
        c.wait()

    @pl.loop(0, 8)
    def _(n):
        zz, m = n // 4, n % 4
        v = g[zz, m, x, :, :, 1152:2304].astype(F32)
        for i in range(3):
            v = v + b1[i, zz, m].astype(F32)
        s1[zz, m] = v.astype(BF)

    second = []
    for i in range(3):
        second.append(remote(s1.at[:, py[i]], a1.at[i], sems, 9 + i, ys[i]))
        second[-1].start()
    for c in first:
        c.wait()
    for zz in range(2):
        v = s0[zz, x].astype(F32)
        for i in range(3):
            v = v + a0[i, zz].astype(F32)
        u0[zz] = v.astype(BF)
    z0 = remote(u0.at[1 - z], f0, sems, 12, low)
    z0.start()
    for c in second:
        c.wait()
    for zz in range(2):
        v = s1[zz, y].astype(F32)
        for i in range(3):
            v = v + a1[i, zz].astype(F32)
        u1[zz] = v.astype(BF)
    z1 = remote(u1.at[1 - z], f1, sems, 13, low)
    z1.start()
    z0.wait()
    res[:, :, 0:1152] = u0[z].astype(F32) + f0[...].astype(F32)
    z1.wait()
    res[:, :, 1152:2304] = u1[z].astype(F32) + f1[...].astype(F32)
    swap = remote(res.at[1 - k], out.at[k], sems, 14, core)
    swap.start()
    out[k] = res[k]
    swap.wait()
    tile[...] = out[0, :, 0:128] + out[1, :, 0:128]
    c_tile = remote(tile, tile_out, sems, 15, far)
    c_tile.start()
    c_tile.wait()


def reduce_all(g):
    big = (3, 2, 4, 2, 16, 1152)
    return comm_call(
        reduce_kernel,
        [jax.ShapeDtypeStruct((2, 16, 2304), F32), jax.ShapeDtypeStruct((16, 128), F32)],
        [
            pltpu.VMEM(big, BF),
            pltpu.VMEM(big, BF),
            pltpu.VMEM(big[1:], BF),
            pltpu.VMEM(big[1:], BF),
            pltpu.VMEM((3, 2, 2, 16, 1152), BF),
            pltpu.VMEM((3, 2, 2, 16, 1152), BF),
            pltpu.VMEM((2, 2, 16, 1152), BF),
            pltpu.VMEM((2, 2, 16, 1152), BF),
            pltpu.VMEM((2, 16, 1152), BF),
            pltpu.VMEM((2, 16, 1152), BF),
            pltpu.VMEM((2, 16, 2304), F32),
            pltpu.VMEM((16, 128), F32),
            DMA((16,)),
            DMA((16,)),
        ],
        3,
        "reduce_grads",
        (g,),
    )


def allowed_pairs(lim, clip, qb, j):
    cols = pl.ds(qb * 256, 256)
    pos = lim[4] + j * 256 + lax.broadcasted_iota(jnp.int32, (256, 256), 0)
    return (pos >= clip[0:1, cols]) & (pos < clip[1:2, cols])


def attend_kernel(lim, clip, q, kv, of, lse):
    lane = lax.broadcasted_iota(jnp.int32, (256, 128), 1)
    for qb in range(2):
        rows = slice(qb * 256, qb * 256 + 256)

        def step(j, carry):
            ok = allowed_pairs(lim, clip, qb, j)
            new = []
            for h in range(3):
                m, l, acc = carry[h]
                cols = slice(h * 128, h * 128 + 128)
                keys = kv[j, :, cols]
                s = lax.dot_general(keys, q[rows, cols], NT, preferred_element_type=F32)
                s = jnp.where(ok, s, NEGATIVE)
                top = jnp.maximum(m, jnp.max(s, axis=0, keepdims=True))
                p = jnp.exp(s - top)
                fade = jnp.exp(m - top)
                l = l * fade + jnp.sum(p, axis=0, keepdims=True)
                acc = acc * fade + lax.dot_general(
                    keys, p.astype(BF), TN, preferred_element_type=F32
                )
                new.append((top, l, acc))
            return tuple(new)

        start = tuple(
            (
                jnp.full((1, 256), NEGATIVE, F32),
                jnp.zeros((1, 256), F32),
                jnp.zeros((128, 256), F32),
            )
            for _ in range(3)
        )
        final = lax.fori_loop(lim[2 * qb], lim[2 * qb + 1], step, start)
        for h in range(3):
            m, l, acc = final[h]
            o = (acc / l).T
            of[rows, h * 128 : h * 128 + 128] = jnp.where(lane >= 64, o, 0.0)
            lse[h : h + 1, rows] = m + jnp.log(l)


def attend(lim, clip, q, kv):
    return pl.pallas_call(
        attend_kernel,
        out_shape=[
            jax.ShapeDtypeStruct((512, 384), F32),
            jax.ShapeDtypeStruct((3, 512), F32),
        ],
        in_specs=[SM, VM, VM, VM],
        out_specs=[VM, VM],
        compiler_params=pltpu.CompilerParams(vmem_limit_bytes=LIMIT),
        name="attend",
    )(lim, clip, q, kv)


def attend_back_kernel(lim, clip, q, dox, kv, lse, delta, dq, dkv, total):
    lane = lax.broadcasted_iota(jnp.int32, (256, 128), 1)

    @pl.loop(0, 14)
    def _(j):
        total[j] = jnp.zeros((256, 384), F32)

    for qb in range(2):
        rows = slice(qb * 256, qb * 256 + 256)

        def step(j, carry):
            ok = allowed_pairs(lim, clip, qb, j)
            new = []
            for h in range(3):
                cols = slice(h * 128, h * 128 + 128)
                keys = kv[j, :, cols]
                qh, dh = q[rows, cols], dox[rows, cols]
                s = lax.dot_general(keys, qh, NT, preferred_element_type=F32)
                p = jnp.exp(jnp.where(ok, s, NEGATIVE) - lse[h : h + 1, rows])
                dp = lax.dot_general(keys, dh, NT, preferred_element_type=F32)
                ds = (p * (dp - delta[h : h + 1, rows])).astype(BF)
                new.append(
                    carry[h] + lax.dot_general(keys, ds, TN, preferred_element_type=F32)
                )
                total[j, :, cols] += jnp.dot(
                    ds, qh, preferred_element_type=F32
                ) + jnp.dot(p.astype(BF), dh, preferred_element_type=F32)
            return tuple(new)

        start = tuple(jnp.zeros((128, 256), F32) for _ in range(3))
        final = lax.fori_loop(lim[2 * qb], lim[2 * qb + 1], step, start)
        for h in range(3):
            back = jnp.where(lane < 64, SCORE_SCALE * final[h].T, 0.0)
            dq[rows, h * 128 : h * 128 + 128] = back.astype(BF)

    @pl.loop(0, 14)
    def _(j):
        dkv[j] = total[j].astype(BF)


def attend_back(lim, clip, q, dox, kv, lse, delta):
    return pl.pallas_call(
        attend_back_kernel,
        out_shape=[
            jax.ShapeDtypeStruct((512, 384), BF),
            jax.ShapeDtypeStruct((14, 256, 384), BF),
        ],
        in_specs=[SM] + [VM] * 6,
        out_specs=[VM, VM],
        scratch_shapes=[pltpu.VMEM((14, 256, 384), F32)],
        compiler_params=pltpu.CompilerParams(vmem_limit_bytes=LIMIT),
        name="attend_back",
    )(lim, clip, q, dox, kv, lse, delta)


def matmul(left, right):
    return jnp.dot(left, right, preferred_element_type=F32)


def matmul_nt(left, right):
    return lax.dot_general(left, right, NT, preferred_element_type=F32)


def matmul_tn(left, right):
    return lax.dot_general(left, right, TN, preferred_element_type=F32)


def normalize(hidden, gain, offset):
    average = jnp.mean(hidden, axis=-1, keepdims=True)
    centred = hidden - average
    spread = jnp.mean(centred * centred, axis=-1, keepdims=True)
    scale = lax.rsqrt(spread + EPS)
    unit = centred * scale
    return unit * gain + offset, unit, scale


def normalize_back(grad_out, unit, scale, gain):
    grad_unit = grad_out * gain
    first = jnp.mean(grad_unit, axis=-1, keepdims=True)
    second = jnp.mean(grad_unit * unit, axis=-1, keepdims=True)
    return scale * (grad_unit - first - unit * second)


def body(
    tokens,
    clip_bounds,
    attn_in,
    qv_bias,
    out_proj,
    fc_in,
    fc_bias,
    fc_out,
    ln_gain,
    row_bias,
    cotangent,
):
    dp = lax.axis_index("dp")
    c, k, t = dp // 2, dp % 2, lax.axis_index("tensor")
    feature = lax.broadcasted_iota(jnp.int32, (768, 1024), 0)
    place = lax.broadcasted_iota(jnp.int32, (768, 1024), 1)
    select = (place == (feature // 12) * 16 + feature % 12).astype(BF)

    def widen(rows):
        return matmul(rows, select).astype(BF)

    def narrow(rows):
        return matmul_nt(rows.astype(BF), select).astype(BF)

    parts = attn_in[0].reshape(3, 12, 6, 64)
    proj = out_proj[0].T.reshape(12, 6, 64)
    kv_w = jnp.stack([parts[1], parts[2]], axis=2).reshape(12, 2, 384)
    qo_w = jnp.stack([parts[0], proj], axis=2).reshape(12, 2, 384)
    up_w = fc_in[0].reshape(12, 2, 768)
    down_w = fc_out[0].T.reshape(12, 2, 768)
    pay = jnp.concatenate([kv_w, qo_w, up_w, down_w], axis=-1).transpose(1, 0, 2)
    small = jnp.concatenate(
        [ln_gain.reshape(-1), row_bias.reshape(-1), qv_bias.reshape(-1), fc_bias.reshape(-1)]
    )
    small = jnp.pad(small, (0, 56))
    extra = jnp.pad(small.reshape(1, 1, 128), ((0, 0), (0, 3), (0, 2176)))
    extra = jnp.concatenate([extra, extra], axis=0)
    pay = jnp.concatenate([pay, extra], axis=1)
    tile = jnp.pad(small.reshape(1, 128), ((13, 2), (0, 0)))
    w, clip, cot = gather_all(pay, tile, clip_bounds, cotangent)
    clip = clip.transpose(1, 0, 2).reshape(2, 512)
    w = w.reshape(1024, 2304)
    w_kv, w_qo, w_up, w_down = w[:, 0:384], w[:, 384:768], w[:, 768:1536], w[:, 1536:2304]

    smalls = w.reshape(64, 16, 2304)[:, 12:14, 0:128].astype(F32)
    pair = jnp.where(t == 0, smalls, smalls[:, ::-1])
    gains = pair[:, :, 0:12].reshape(64, 2, 2, 6).transpose(2, 0, 1, 3).reshape(2, 768)
    biases = pair[:, :, 12:36].reshape(64, 2, 4, 6).transpose(2, 0, 1, 3).reshape(4, 768)
    heads = smalls[:, 0, 36:48].reshape(64, 2, 2, 3)
    heads = jnp.where(k == 0, heads[:, :, 0], heads[:, :, 1]).transpose(1, 2, 0)
    blank = jnp.zeros((3, 64), F32)
    qo_bias = jnp.concatenate([heads[0], blank], axis=1).reshape(384)
    kv_bias = jnp.concatenate([blank, heads[1]], axis=1).reshape(384)
    up_bias = smalls[:, 0, 48:72].reshape(64, 2, 3, 4)
    up_bias = jnp.where(k == 0, up_bias[:, 0], up_bias[:, 1]).transpose(1, 0, 2).reshape(768)
    low_lanes = (jnp.arange(384, dtype=jnp.int32) % 128) < 64

    hidden = tokens.astype(F32)
    normed, unit_one, scale_one = normalize(hidden, gains[0], biases[0])
    full_one = widen(gather_rows(normed.astype(BF), 4, "rows_one"))
    kv = (matmul(full_one, w_kv) + kv_bias).astype(BF)
    query = (matmul(full_one, w_qo) + qo_bias).astype(BF)
    query = jnp.where(low_lanes, query * BF(SCORE_SCALE), BF(0))
    near = halo(kv).reshape(14, 256, 384)
    base = (c - 3) * 512
    lim = jnp.stack(
        [
            (clip[0, 0] - base) // 256,
            (clip[1, 255] - base + 255) // 256,
            (clip[0, 256] - base) // 256,
            (clip[1, 511] - base + 255) // 256,
            base,
        ]
    ).astype(jnp.int32)
    mixed, lse = attend(lim, clip, query, near)
    mixed_low = mixed.astype(BF)
    attn = narrow(matmul_nt(mixed_low, w_qo))
    attn = sum_rows(attn.reshape(1, 4, 128, 768), 5, "sum_attn")[0]
    hidden_one = hidden + attn + biases[1]
    normed_two, unit_two, scale_two = normalize(hidden_one, gains[1], biases[2])
    full_two = widen(gather_rows(normed_two.astype(BF), 6, "rows_two"))
    inner = matmul(full_two, w_up) + up_bias
    gelu = lambda v: jax.nn.gelu(v, approximate=False)
    active = gelu(inner).astype(BF)
    mlp = narrow(matmul_nt(active, w_down))
    full_mlp = widen(cot.reshape(512, 768))
    grad_active = matmul(full_mlp, w_down)
    _, gelu_back = jax.vjp(gelu, inner)
    grad_inner = gelu_back(grad_active)[0].astype(BF)
    back_two = narrow(matmul_nt(grad_inner, w_up))
    pair_sum = sum_rows(jnp.stack([mlp, back_two]).reshape(2, 4, 128, 768), 7, "sum_mlp")
    output = (hidden_one + pair_sum[0] + biases[3]).astype(BF)
    grad_normed_two = pair_sum[1]
    grad_hidden_one = cotangent.astype(F32) + normalize_back(
        grad_normed_two, unit_two, scale_two, gains[1]
    )
    grad_attn = grad_hidden_one.astype(BF)
    full_attn = widen(gather_rows(grad_attn, 8, "rows_back"))
    grad_mixed = jnp.where(low_lanes, 0.0, matmul(full_attn, w_qo)).astype(BF)
    delta = (grad_mixed.astype(F32) * mixed).reshape(512, 3, 128).sum(axis=-1).T
    grad_query, grad_near = attend_back(lim, clip, query, grad_mixed, near, lse, delta)
    grad_kv = halo_back(grad_near.reshape(7, 512, 384))
    back_one = narrow(matmul_nt(grad_query, w_qo) + matmul_nt(grad_kv, w_kv))
    grad_normed_one = sum_rows(back_one.reshape(1, 4, 128, 768), 9, "sum_back")[0]
    grad_tokens = grad_hidden_one + normalize_back(
        grad_normed_one, unit_one, scale_one, gains[0]
    )

    sums = jnp.stack(
        [
            jnp.sum(grad_normed_one * unit_one, axis=0),
            jnp.sum(grad_normed_two * unit_two, axis=0),
            jnp.sum(grad_normed_one, axis=0),
            jnp.sum(grad_attn.astype(F32), axis=0),
            jnp.sum(grad_normed_two, axis=0),
            jnp.sum(cotangent.astype(F32), axis=0),
        ]
    )
    sums = sums.reshape(6, 64, 12).transpose(1, 0, 2).reshape(64, 72)
    q_sum = jnp.sum(grad_query.astype(F32), axis=0).reshape(3, 128)[:, :64]
    v_sum = jnp.sum(grad_kv.astype(F32), axis=0).reshape(3, 128)[:, 64:]
    qv_sum = jnp.concatenate([q_sum, v_sum], axis=0).T
    up_sum = jnp.sum(grad_inner.astype(F32), axis=0)
    up_sum = up_sum.reshape(3, 64, 4).transpose(1, 0, 2).reshape(64, 12)
    smalls = jnp.concatenate([sums, qv_sum, up_sum], axis=1)
    smalls = jnp.pad(smalls.reshape(64, 1, 90), ((0, 0), (12, 3), (0, 294))).reshape(1024, 384)
    grads = jnp.concatenate(
        [
            (matmul_tn(full_one, grad_kv) + smalls).astype(BF),
            (matmul_tn(full_one, grad_query) + matmul_tn(full_attn, mixed_low)).astype(BF),
            matmul_tn(full_two, grad_inner).astype(BF),
            matmul_tn(full_mlp, active).astype(BF),
        ],
        axis=1,
    )
    own, far = reduce_all(grads.reshape(2, 4, 4, 2, 16, 2304))
    vec = own[0, 12, 0:128] + own[1, 12, 0:128] + far[12]
    vec = vec[0:72].reshape(6, 2, 6)
    vec = jnp.where(t == 0, vec[:, 0], vec[:, 1])
    grad_gain, grad_row = vec[0:2].reshape(1, 2, 6), vec[2:6].reshape(1, 4, 6)
    grad_qv = own[:, 12, 72:78].reshape(2, 2, 3).transpose(1, 0, 2).reshape(1, 2, 6, 1)
    grad_up_bias = own[:, 12, 78:90].reshape(1, 6, 4)
    main = own[:, 0:12].transpose(1, 0, 2)
    g_kv = main[:, :, 0:384].reshape(12, 6, 2, 64)
    g_qo = main[:, :, 384:768].reshape(12, 6, 2, 64)
    grad_in = jnp.stack(
        [
            g_qo[:, :, 0].reshape(12, 384),
            g_kv[:, :, 0].reshape(12, 384),
            g_kv[:, :, 1].reshape(12, 384),
        ]
    )[None]
    grad_out = g_qo[:, :, 1].reshape(12, 384).T[None]
    grad_up = main[:, :, 768:1536].reshape(1, 12, 1536)
    grad_down = main[:, :, 1536:2304].reshape(12, 1536).T[None]
    return (
        output,
        grad_tokens,
        grad_in,
        grad_qv,
        grad_out,
        grad_up,
        grad_up_bias,
        grad_down,
        grad_gain,
        grad_row,
    )


def solution(mesh):
    return jax.shard_map(
        body,
        mesh=mesh,
        in_specs=(
            P(("dp", "tensor"), None),
            P(None, "dp"),
            P(None, None, "dp", "tensor"),
            P(None, None, "tensor", "dp"),
            P(None, "tensor", "dp"),
            P(None, "dp", "tensor"),
            P(None, "tensor", "dp"),
            P(None, "tensor", "dp"),
            P(None, None, ("dp", "tensor")),
            P(None, None, ("dp", "tensor")),
            P(("dp", "tensor"), None),
        ),
        out_specs=(
            P(("dp", "tensor"), None),
            P(("dp", "tensor"), None),
            P(None, None, "dp", "tensor"),
            P(None, None, "tensor", "dp"),
            P(None, "tensor", "dp"),
            P(None, "dp", "tensor"),
            P(None, "tensor", "dp"),
            P(None, "tensor", "dp"),
            P(None, None, ("dp", "tensor")),
            P(None, None, ("dp", "tensor")),
        ),
        check_vma=False,
    )
```

```python
import jax
import jax.numpy as jnp
from jax import lax
import jax.experimental.pallas as pl
import jax.experimental.pallas.tpu as pltpu
from jax.sharding import PartitionSpec as P

EPS = 1e-05
NEGATIVE = -1e30
SCORE_SCALE = 0.125
BF = jnp.bfloat16
F32 = jnp.float32
MESH = pl.DeviceIdType.MESH
VM = pl.BlockSpec(memory_space=pltpu.VMEM)
SM = pl.BlockSpec(memory_space=pltpu.SMEM)
DMA = pltpu.SemaphoreType.DMA
LIMIT = 56 * 2**20
NT = (((1,), (1,)), ((), ()))
TN = (((0,), (0,)), ((), ()))


def coords():
    dp = lax.axis_index("dp")
    return dp // 32, (dp // 8) % 4, (dp // 2) % 4, dp % 2, lax.axis_index("tensor")


def device(z, y, x, k, t):
    return (((z * 4 + y) * 4 + x) * 2 + k, t)


def chip(c, k, t):
    return (c * 2 + k, t)


def greet(peers):
    bar = pltpu.get_barrier_semaphore()
    for peer in peers:
        pl.semaphore_signal(bar, inc=1, device_id=peer, device_id_type=MESH)
    pl.semaphore_wait(bar, len(peers))


def remote(src, dst, sems, index, peer):
    send, recv = sems
    return pltpu.make_async_remote_copy(
        src, dst, send.at[index], recv.at[index], device_id=peer, device_id_type=MESH
    )


def comm_call(kernel, out_shape, scratch, cid, name, args):
    single = not isinstance(out_shape, (list, tuple))
    return pl.pallas_call(
        kernel,
        out_shape=out_shape,
        in_specs=[VM] * len(args),
        out_specs=VM if single else [VM] * len(out_shape),
        scratch_shapes=scratch,
        compiler_params=pltpu.CompilerParams(
            collective_id=cid, has_side_effects=True, vmem_limit_bytes=LIMIT
        ),
        name=name,
    )(*args)


def spots():
    z, y, x, k, t = coords()
    xs = [device(z, y, (x + d) % 4, k, t) for d in (1, 2, 3)]
    ys = [device(z, (y + d) % 4, x, k, t) for d in (1, 2, 3)]
    core = device(z, y, x, 1 - k, t)
    far = device(z, y, x, k, 1 - t)
    low = device(1 - z, y, x, k, t)
    ring = [chip(((z * 4 + y) * 4 + x + d) % 32, k, t) for d in RING]
    return (z, y, x, k, t), xs, ys, core, far, low, ring


RING = (2, -2, 3, -3, 1, -1)


class Copies:
    def __init__(self, send, recv):
        self.sems, self.count = (send, recv), 0

    def __call__(self, src, dst, peer):
        made = remote(src, dst, self.sems, self.count, peer)
        self.count += 1
        made.start()
        return made


def gather_kernel(
    pay, tile, clip, cot, tok, w, f0, f1, clip_out, cot_out, tk, pay_s, tile_in, ws, send, recv
):
    (z, y, x, k, t), xs, ys, core, far, low, ring = spots()
    copy = Copies(send, recv)
    mine, other = k * 2 + t, k * 2 + 1 - t
    greet(xs + ys + [core, far, low] + ring)
    c_tile = copy(tile, tile_in, far)
    cot_far = copy(cot, cot_out.at[mine], far)
    own_far = copy(tok, tk.at[3, mine], far)
    order = (4, 5, 2, 3, 0, 1)
    pushes = {i: copy(tok, tk.at[3 - RING[i], mine], ring[i]) for i in order}
    done = [
        copy(cot, cot_out.at[mine], core),
        copy(tok, tk.at[3, mine], core),
        copy(clip, clip_out.at[k], core),
    ]
    clip_out[k] = clip[...]
    cot_out[mine] = cot[...]
    tk[3, mine] = tok[...]
    c_tile.wait()
    pay_s[...] = pay[...]
    for q in range(2):
        pay_s[q, :, 0:128] = pay[q, :, 0:128] + tile_in[...]
    swap = copy(pay_s.at[1 - k], ws.at[z, k], core)
    ws[z, k] = pay_s[k]
    swap.wait()
    copy(ws.at[z], ws.at[z], low).wait()
    w[:, y, x] = ws[:, :, :, 0:768]
    f0[:, x] = ws[:, :, :, 768:1536]
    f1[:, y] = ws[:, :, :, 1536:2304]
    h0, h1 = pl.ds(0, 384), pl.ds(384, 384)
    phase = []
    for i in range(3):
        phase.append(copy(ws.at[:, :, :, h0], w.at[:, y, x, :, :, h0], xs[i]))
        phase.append(copy(ws.at[:, :, :, h1], w.at[:, y, x, :, :, h1], ys[i]))
    rest = []
    for i in range(3):
        rest.append(copy(ws.at[:, :, :, pl.ds(768, 768)], f0.at[:, x], xs[i]))
        rest.append(copy(ws.at[:, :, :, pl.ds(1536, 768)], f1.at[:, y], ys[i]))
    for c in phase:
        c.wait()
    for i in range(3):
        a = w.at[:, y, :, :, :, h0]
        rest.append(copy(a, a, ys[i]))
        b = w.at[:, :, x, :, :, h1]
        rest.append(copy(b, b, xs[i]))
    to_far = {}
    for i in order:
        pushes[i].wait_recv()
        a = tk.at[3 - RING[i], mine]
        to_far[i] = copy(a, a, far)
        done.append(copy(a, a, core))
    cot_far.wait_recv()
    done.append(copy(cot_out.at[other], cot_out.at[other], core))
    own_far.wait_recv()
    done.append(copy(tk.at[3, other], tk.at[3, other], core))
    for i in order:
        to_far[i].wait_recv()
        a = tk.at[3 - RING[i], other]
        done.append(copy(a, a, core))
    for i in order:
        pushes[i].wait_send()
        to_far[i].wait_send()
    cot_far.wait_send()
    own_far.wait_send()
    for c in rest + done:
        c.wait()


def gather_all(pay, tile, clip, cot, tok):
    return comm_call(
        gather_kernel,
        [
            jax.ShapeDtypeStruct((2, 4, 4, 2, 16, 768), BF),
            jax.ShapeDtypeStruct((2, 4, 2, 16, 768), BF),
            jax.ShapeDtypeStruct((2, 4, 2, 16, 768), BF),
            jax.ShapeDtypeStruct((2, 2, 256), jnp.int32),
            jax.ShapeDtypeStruct((4, 128, 768), BF),
            jax.ShapeDtypeStruct((7, 4, 128, 768), BF),
        ],
        [
            pltpu.VMEM((2, 16, 2304), BF),
            pltpu.VMEM((16, 128), BF),
            pltpu.VMEM((2, 2, 16, 2304), BF),
            DMA((56,)),
            DMA((56,)),
        ],
        0,
        "gather_first",
        (pay, tile, clip, cot, tok),
    )


def piece_copies(copy, f0, f1, p0, p1, p, x, y, xs, ys):
    made = []
    for i in range(3):
        made.append(copy(f0.at[p], p0.at[y], ys[i]))
        made.append(copy(f1.at[p], p1.at[:, x], xs[i]))
    p0[y] = f0[p]
    p1[:, x] = f1[p]
    return made


PIECE = [jax.ShapeDtypeStruct((4, 4, 2, 16, 768), BF)] * 2


def exchange_rows(copy, a, out, k, t, core, far):
    mine, other = k * 2 + t, k * 2 + 1 - t
    c_far = copy(a, out.at[mine], far)
    c_core = copy(a, out.at[mine], core)
    out[mine] = a[...]

    def finish():
        c_far.wait_recv()
        c_pass = copy(out.at[other], out.at[other], core)
        c_far.wait_send()
        c_core.wait()
        c_pass.wait()

    return finish


def exchange_sums(copy, p, out, got_core, mid, got_far, k, t, core, far):
    n = p.shape[0]
    to_core = [copy(p.at[i, pl.ds((1 - k) * 2, 2)], got_core.at[i], core) for i in range(n)]

    def finish():
        to_far = []
        for i in range(n):
            to_core[i].wait()
            mid[i] = (p[i, k * 2 + 1 - t].astype(F32) + got_core[i, 1 - t].astype(F32)).astype(BF)
            to_far.append(copy(mid.at[i], got_far.at[i], far))
        for i in range(n):
            part = p[i, k * 2 + t].astype(F32) + got_core[i, t].astype(F32)
            to_far[i].wait()
            out[i] = part + got_far[i].astype(F32)

    return finish


def sum_scratch(n):
    return [
        pltpu.VMEM((n, 2, 128, 768), BF),
        pltpu.VMEM((n, 128, 768), BF),
        pltpu.VMEM((n, 128, 768), BF),
    ]


def sum_attn_kernel(p, f0, f1, out, p0, p1, got_core, mid, got_far, send, recv):
    (z, y, x, k, t), xs, ys, core, far, low, ring = spots()
    copy = Copies(send, recv)
    greet(xs + ys + [core, far])
    finish = exchange_sums(copy, p, out, got_core, mid, got_far, k, t, core, far)
    made = piece_copies(copy, f0, f1, p0, p1, 0, x, y, xs, ys)
    finish()
    for c in made:
        c.wait()


def sum_attn(p, f0, f1):
    return comm_call(
        sum_attn_kernel,
        [jax.ShapeDtypeStruct((1, 128, 768), F32)] + PIECE,
        sum_scratch(1) + [DMA((8,)), DMA((8,))],
        1,
        "sum_attn",
        (p, f0, f1),
    )


def rows_two_kernel(a, f0, f1, out, p0, p1, send, recv):
    (z, y, x, k, t), xs, ys, core, far, low, ring = spots()
    copy = Copies(send, recv)
    greet(xs + ys + [core, far])
    finish = exchange_rows(copy, a, out, k, t, core, far)
    made = piece_copies(copy, f0, f1, p0, p1, 1, x, y, xs, ys)
    finish()
    for c in made:
        c.wait()


def rows_two(a, f0, f1):
    return comm_call(
        rows_two_kernel,
        [jax.ShapeDtypeStruct((4, 128, 768), BF)] + PIECE,
        [DMA((9,)), DMA((9,))],
        2,
        "rows_two",
        (a, f0, f1),
    )


def spread_first(copy, g0, g1, b0, b1, x, y, xs, ys):
    over_y, over_x = [], []
    for i in range(3):
        over_y.append(copy(g0.at[:, (y + i + 1) % 4], b0.at[i], ys[i]))
        over_x.append(copy(g1.at[:, :, (x + i + 1) % 4], b1.at[i], xs[i]))
    return over_y, over_x


def add_first(g0, g1, b0, b1, s0, s1, x, y, over_y, over_x):
    for c in over_y:
        c.wait()

    @pl.loop(0, 8)
    def _(n):
        zz, m = n // 4, n % 4
        v = g0[zz, y, m].astype(F32)
        for i in range(3):
            v = v + b0[i, zz, m].astype(F32)
        s0[zz, m] = v.astype(BF)

    for c in over_x:
        c.wait()

    @pl.loop(0, 8)
    def _(n):
        zz, m = n // 4, n % 4
        v = g1[zz, m, x].astype(F32)
        for i in range(3):
            v = v + b1[i, zz, m].astype(F32)
        s1[zz, m] = v.astype(BF)


def spread_second(copy, s0, s1, a0, a1, x, y, xs, ys):
    over_x, over_y = [], []
    for i in range(3):
        over_x.append(copy(s0.at[:, (x + i + 1) % 4], a0.at[i], xs[i]))
        over_y.append(copy(s1.at[:, (y + i + 1) % 4], a1.at[i], ys[i]))
    return over_x, over_y


def add_second(s0, s1, a0, a1, u0, u1, x, y, over_x, over_y):
    for c in over_x + over_y:
        c.wait()
    for zz in range(2):
        v = s0[zz, x].astype(F32)
        v1 = s1[zz, y].astype(F32)
        for i in range(3):
            v = v + a0[i, zz].astype(F32)
            v1 = v1 + a1[i, zz].astype(F32)
        u0[zz] = v.astype(BF)
        u1[zz] = v1.astype(BF)


def sum_mlp_kernel(p, g0, g1, out, s0, s1, got_core, mid, got_far, b0, b1, send, recv):
    (z, y, x, k, t), xs, ys, core, far, low, ring = spots()
    copy = Copies(send, recv)
    greet(xs + ys + [core, far])
    finish = exchange_sums(copy, p, out, got_core, mid, got_far, k, t, core, far)
    over = spread_first(copy, g0, g1, b0, b1, x, y, xs, ys)
    finish()
    add_first(g0, g1, b0, b1, s0, s1, x, y, *over)


def sum_mlp(p, g0, g1):
    return comm_call(
        sum_mlp_kernel,
        [jax.ShapeDtypeStruct((2, 128, 768), F32)]
        + [jax.ShapeDtypeStruct((2, 4, 2, 16, 768), BF)] * 2,
        sum_scratch(2)
        + [pltpu.VMEM((3, 2, 4, 2, 16, 768), BF)] * 2
        + [DMA((10,)), DMA((10,))],
        3,
        "sum_mlp",
        (p, g0, g1),
    )


def rows_back_kernel(a, s0, s1, out, u0, u1, a0, a1, send, recv):
    (z, y, x, k, t), xs, ys, core, far, low, ring = spots()
    copy = Copies(send, recv)
    greet(xs + ys + [core, far])
    finish = exchange_rows(copy, a, out, k, t, core, far)
    over = spread_second(copy, s0, s1, a0, a1, x, y, xs, ys)
    finish()
    add_second(s0, s1, a0, a1, u0, u1, x, y, *over)


def rows_back(a, s0, s1):
    return comm_call(
        rows_back_kernel,
        [jax.ShapeDtypeStruct((4, 128, 768), BF)]
        + [jax.ShapeDtypeStruct((2, 2, 16, 768), BF)] * 2,
        [pltpu.VMEM((3, 2, 2, 16, 768), BF)] * 2 + [DMA((9,)), DMA((9,))],
        4,
        "rows_back",
        (a, s0, s1),
    )


def return_kernel(
    d, g, u0, u1, out, own, tile_out,
    got_core, e_send, got_far, r_send, got_ring,
    b0, b1, s0, s1, a0, a1, v0, v1, z_in0, z_in1, z_in2, z_in3, res, tile, send, recv,
):
    (z, y, x, k, t), xs, ys, core, far, low, ring = spots()
    copy = Copies(send, recv)
    greet(xs + ys + [core, far, low] + ring)
    order = [3 + r for r in RING] + [3]
    to_core = {j: copy(d.at[j, pl.ds((1 - k) * 2, 2)], got_core.at[j], core) for j in order}
    g0, g1 = g.at[:, :, :, :, :, pl.ds(0, 384)], g.at[:, :, :, :, :, pl.ds(384, 384)]
    over = spread_first(copy, g0, g1, b0, b1, x, y, xs, ys)
    fc_z = [copy(u0.at[1 - z], z_in0, low), copy(u1.at[1 - z], z_in1, low)]
    to_far = {}
    for j in order:
        to_core[j].wait()
        e_send[j] = (d[j, k * 2 + 1 - t].astype(F32) + got_core[j, 1 - t].astype(F32)).astype(BF)
        to_far[j] = copy(e_send.at[j], got_far.at[j], far)
    add_first(g0, g1, b0, b1, s0, s1, x, y, *over)
    over = spread_second(copy, s0, s1, a0, a1, x, y, xs, ys)
    home = []

    def send_home(i):
        j = order[i]
        to_far[j].wait()
        v = d[j, k * 2 + t].astype(F32) + got_core[j, t].astype(F32) + got_far[j].astype(F32)
        r_send[i] = v.astype(BF)
        home.append(copy(r_send.at[i], got_ring.at[i], ring[i]))

    for i in range(3):
        send_home(i)
    add_second(s0, s1, a0, a1, v0, v1, x, y, *over)
    attn_z = [copy(v0.at[1 - z], z_in2, low), copy(v1.at[1 - z], z_in3, low)]
    for i in range(3, 6):
        send_home(i)
    for c in fc_z + attn_z:
        c.wait()
    res[:, :, 0:384] = v0[z].astype(F32) + z_in2[...].astype(F32)
    res[:, :, 384:768] = v1[z].astype(F32) + z_in3[...].astype(F32)
    res[:, :, 768:1536] = u0[z].astype(F32) + z_in0[...].astype(F32)
    res[:, :, 1536:2304] = u1[z].astype(F32) + z_in1[...].astype(F32)
    swap = copy(res.at[1 - k], own.at[k], core)
    own[k] = res[k]
    to_far[3].wait()
    total = d[3, k * 2 + t].astype(F32) + got_core[3, t].astype(F32) + got_far[3].astype(F32)
    swap.wait()
    tile[...] = own[0, :, 0:128] + own[1, :, 0:128]
    c_tile = copy(tile, tile_out, far)
    for i in range(6):
        home[i].wait()
        total = total + got_ring[i].astype(F32)
    out[...] = total
    c_tile.wait()


def return_all(d, g, u0, u1):
    return comm_call(
        return_kernel,
        [
            jax.ShapeDtypeStruct((128, 768), F32),
            jax.ShapeDtypeStruct((2, 16, 2304), F32),
            jax.ShapeDtypeStruct((16, 128), F32),
        ],
        [
            pltpu.VMEM((7, 2, 128, 768), BF),
            pltpu.VMEM((7, 128, 768), BF),
            pltpu.VMEM((7, 128, 768), BF),
            pltpu.VMEM((6, 128, 768), BF),
            pltpu.VMEM((6, 128, 768), BF),
        ]
        + [pltpu.VMEM((3, 2, 4, 2, 16, 384), BF)] * 2
        + [pltpu.VMEM((2, 4, 2, 16, 384), BF)] * 2
        + [pltpu.VMEM((3, 2, 2, 16, 384), BF)] * 2
        + [pltpu.VMEM((2, 2, 16, 384), BF)] * 2
        + [pltpu.VMEM((2, 16, 768), BF)] * 2
        + [pltpu.VMEM((2, 16, 384), BF)] * 2
        + [pltpu.VMEM((2, 16, 2304), F32), pltpu.VMEM((16, 128), F32), DMA((38,)), DMA((38,))],
        5,
        "return_all",
        (d, g, u0, u1),
    )


def allowed_pairs(lim, clip, qb, j):
    cols = pl.ds(qb * 256, 256)
    pos = lim[4] + j * 256 + lax.broadcasted_iota(jnp.int32, (256, 256), 0)
    return (pos >= clip[0:1, cols]) & (pos < clip[1:2, cols])


def attend_kernel(lim, clip, q, kv, of, lse):
    lane = lax.broadcasted_iota(jnp.int32, (256, 128), 1)
    for qb in range(2):
        rows = slice(qb * 256, qb * 256 + 256)

        def step(j, carry):
            ok = allowed_pairs(lim, clip, qb, j)
            new = []
            for h in range(3):
                m, l, acc = carry[h]
                cols = slice(h * 128, h * 128 + 128)
                keys = kv[j, :, cols]
                s = lax.dot_general(keys, q[rows, cols], NT, preferred_element_type=F32)
                s = jnp.where(ok, s, NEGATIVE)
                top = jnp.maximum(m, jnp.max(s, axis=0, keepdims=True))
                p = jnp.exp(s - top)
                fade = jnp.exp(m - top)
                l = l * fade + jnp.sum(p, axis=0, keepdims=True)
                acc = acc * fade + lax.dot_general(
                    keys, p.astype(BF), TN, preferred_element_type=F32
                )
                new.append((top, l, acc))
            return tuple(new)

        start = tuple(
            (
                jnp.full((1, 256), NEGATIVE, F32),
                jnp.zeros((1, 256), F32),
                jnp.zeros((128, 256), F32),
            )
            for _ in range(3)
        )
        final = lax.fori_loop(lim[2 * qb], lim[2 * qb + 1], step, start)
        for h in range(3):
            m, l, acc = final[h]
            o = (acc / l).T
            of[rows, h * 128 : h * 128 + 128] = jnp.where(lane >= 64, o, 0.0)
            lse[h : h + 1, rows] = m + jnp.log(l)


def attend(lim, clip, q, kv):
    return pl.pallas_call(
        attend_kernel,
        out_shape=[
            jax.ShapeDtypeStruct((512, 384), F32),
            jax.ShapeDtypeStruct((3, 512), F32),
        ],
        in_specs=[SM, VM, VM, VM],
        out_specs=[VM, VM],
        compiler_params=pltpu.CompilerParams(vmem_limit_bytes=LIMIT),
        name="attend",
    )(lim, clip, q, kv)


def attend_back_kernel(lim, clip, q, dox, kv, lse, delta, dz, total):
    lane = lax.broadcasted_iota(jnp.int32, (256, 128), 1)

    @pl.loop(0, 14)
    def _(j):
        total[j] = jnp.zeros((256, 384), F32)

    for qb in range(2):
        rows = slice(qb * 256, qb * 256 + 256)

        def step(j, carry):
            ok = allowed_pairs(lim, clip, qb, j)
            new = []
            for h in range(3):
                cols = slice(h * 128, h * 128 + 128)
                keys = kv[j, :, cols]
                qh, dh = q[rows, cols], dox[rows, cols]
                s = lax.dot_general(keys, qh, NT, preferred_element_type=F32)
                p = jnp.exp(jnp.where(ok, s, NEGATIVE) - lse[h : h + 1, rows])
                dp = lax.dot_general(keys, dh, NT, preferred_element_type=F32)
                ds = (p * (dp - delta[h : h + 1, rows])).astype(BF)
                new.append(
                    carry[h] + lax.dot_general(keys, ds, TN, preferred_element_type=F32)
                )
                total[j, :, cols] += jnp.dot(
                    ds, qh, preferred_element_type=F32
                ) + jnp.dot(p.astype(BF), dh, preferred_element_type=F32)
            return tuple(new)

        start = tuple(jnp.zeros((128, 256), F32) for _ in range(3))
        final = lax.fori_loop(lim[2 * qb], lim[2 * qb + 1], step, start)
        for h in range(3):
            back = jnp.where(lane < 64, SCORE_SCALE * final[h].T, 0.0)
            dz[6 + qb, :, 384 + h * 128 : 512 + h * 128] = back.astype(BF)

    @pl.loop(0, 14)
    def _(j):
        dz[j, :, 0:384] = total[j].astype(BF)

    for j in range(14):
        if j not in (6, 7):
            dz[j, :, 384:768] = jnp.zeros((256, 384), BF)


def attend_back(lim, clip, q, dox, kv, lse, delta):
    return pl.pallas_call(
        attend_back_kernel,
        out_shape=jax.ShapeDtypeStruct((14, 256, 768), BF),
        in_specs=[SM] + [VM] * 6,
        out_specs=VM,
        scratch_shapes=[pltpu.VMEM((14, 256, 384), F32)],
        compiler_params=pltpu.CompilerParams(vmem_limit_bytes=LIMIT),
        name="attend_back",
    )(lim, clip, q, dox, kv, lse, delta)


def matmul(left, right):
    return jnp.dot(left, right, preferred_element_type=F32)


def matmul_nt(left, right):
    return lax.dot_general(left, right, NT, preferred_element_type=F32)


def matmul_tn(left, right):
    return lax.dot_general(left, right, TN, preferred_element_type=F32)


def normalize(hidden, gain, offset):
    average = jnp.mean(hidden, axis=-1, keepdims=True)
    centred = hidden - average
    spread = jnp.mean(centred * centred, axis=-1, keepdims=True)
    scale = lax.rsqrt(spread + EPS)
    unit = centred * scale
    return unit * gain + offset, unit, scale


def normalize_back(grad_out, unit, scale, gain):
    grad_unit = grad_out * gain
    first = jnp.mean(grad_unit, axis=-1, keepdims=True)
    second = jnp.mean(grad_unit * unit, axis=-1, keepdims=True)
    return scale * (grad_unit - first - unit * second)


def body(
    tokens,
    clip_bounds,
    attn_in,
    qv_bias,
    out_proj,
    fc_in,
    fc_bias,
    fc_out,
    ln_gain,
    row_bias,
    cotangent,
):
    dp = lax.axis_index("dp")
    c, k, t = dp // 2, dp % 2, lax.axis_index("tensor")
    feature = lax.broadcasted_iota(jnp.int32, (384, 512), 0)
    place = lax.broadcasted_iota(jnp.int32, (384, 512), 1)
    select = (place == (feature // 12) * 16 + feature % 12).astype(BF)

    def narrow(padded):
        return matmul(select, padded.reshape(512, -1)).astype(BF)

    def widen(rows):
        halves = [matmul_tn(select, rows[i : i + 384]).astype(BF) for i in (0, 384)]
        return jnp.stack(halves).reshape(2, 4, 4, 2, 16, -1)

    parts = attn_in[0].reshape(3, 12, 6, 64)
    proj = out_proj[0].T.reshape(12, 6, 64)
    kv_w = jnp.stack([parts[1], parts[2]], axis=2).reshape(12, 2, 384)
    qo_w = jnp.stack([parts[0], proj], axis=2).reshape(12, 2, 384)
    up_w = fc_in[0].reshape(12, 2, 768)
    down_w = fc_out[0].T.reshape(12, 2, 768)
    pay = jnp.concatenate([kv_w, qo_w, up_w, down_w], axis=-1).transpose(1, 0, 2)
    small = jnp.concatenate(
        [ln_gain.reshape(-1), row_bias.reshape(-1), qv_bias.reshape(-1), fc_bias.reshape(-1)]
    )
    small = jnp.pad(small, (0, 56))
    extra = jnp.pad(small.reshape(1, 1, 128), ((0, 0), (0, 3), (0, 2176)))
    extra = jnp.concatenate([extra, extra], axis=0)
    pay = jnp.concatenate([pay, extra], axis=1)
    tile = jnp.pad(small.reshape(1, 128), ((13, 2), (0, 0)))
    w, f0, f1, clip, cot, near_tokens = gather_all(pay, tile, clip_bounds, cotangent, tokens)
    clip = clip.transpose(1, 0, 2).reshape(2, 512)
    w_attn = jnp.concatenate([narrow(w[0]), narrow(w[1])])
    w_kv, w_qo = w_attn[:, 0:384], w_attn[:, 384:768]

    smalls = w.reshape(64, 16, 768)[:, 12:14, 0:128].astype(F32)
    pair = jnp.where(t == 0, smalls, smalls[:, ::-1])
    gains = pair[:, :, 0:12].reshape(64, 2, 2, 6).transpose(2, 0, 1, 3).reshape(2, 768)
    biases = pair[:, :, 12:36].reshape(64, 2, 4, 6).transpose(2, 0, 1, 3).reshape(4, 768)
    heads = smalls[:, 0, 36:48].reshape(64, 2, 2, 3)
    heads = jnp.where(k == 0, heads[:, :, 0], heads[:, :, 1]).transpose(1, 2, 0)
    blank = jnp.zeros((3, 64), F32)
    qo_bias = jnp.concatenate([heads[0], blank], axis=1).reshape(384)
    kv_bias = jnp.concatenate([blank, heads[1]], axis=1).reshape(384)
    up_bias = smalls[:, 0, 48:72].reshape(64, 2, 3, 4)
    up_bias = jnp.where(k == 0, up_bias[:, 0], up_bias[:, 1]).transpose(1, 0, 2).reshape(768)
    low_lanes = (jnp.arange(384, dtype=jnp.int32) % 128) < 64

    hidden = tokens.astype(F32)
    near_one, near_unit, _ = normalize(
        near_tokens.reshape(3584, 768).astype(F32), gains[0], biases[0]
    )
    near_one, near_unit = near_one.astype(BF), near_unit.astype(BF)
    near = (matmul(near_one, w_kv) + kv_bias).astype(BF).reshape(14, 256, 384)
    query = (matmul(near_one[1536:2048], w_qo) + qo_bias).astype(BF)
    query = jnp.where(low_lanes, query * BF(SCORE_SCALE), BF(0))
    base = (c - 3) * 512
    lim = jnp.stack(
        [
            (clip[0, 0] - base) // 256,
            (clip[1, 255] - base + 255) // 256,
            (clip[0, 256] - base) // 256,
            (clip[1, 511] - base + 255) // 256,
            base,
        ]
    ).astype(jnp.int32)
    mixed, lse = attend(lim, clip, query, near)
    mixed_low = mixed.astype(BF)
    attn = matmul_nt(mixed_low, w_qo).astype(BF)
    attn, up_a, down_a = sum_attn(attn.reshape(1, 4, 128, 768), f0, f1)
    hidden_one = hidden + attn[0] + biases[1]
    normed_two, unit_two, scale_two = normalize(hidden_one, gains[1], biases[2])
    full_two, up_b, down_b = rows_two(normed_two.astype(BF), f0, f1)
    full_two = full_two.reshape(512, 768)
    w_up = jnp.concatenate([narrow(up_a), narrow(up_b)])
    w_down = jnp.concatenate([narrow(down_a), narrow(down_b)])
    inner = matmul(full_two, w_up) + up_bias
    gelu = lambda v: jax.nn.gelu(v, approximate=False)
    active = gelu(inner).astype(BF)
    mlp = matmul_nt(active, w_down).astype(BF)
    full_mlp = cot.reshape(512, 768)
    grad_active = matmul(full_mlp, w_down)
    _, gelu_back = jax.vjp(gelu, inner)
    grad_inner = gelu_back(grad_active)[0].astype(BF)
    back_two = matmul_nt(grad_inner, w_up).astype(BF)
    grad_up = widen(matmul_tn(full_two, grad_inner).astype(BF))
    grad_down = widen(matmul_tn(full_mlp, active).astype(BF))
    pair_sum, s0, s1 = sum_mlp(
        jnp.stack([mlp, back_two]).reshape(2, 4, 128, 768), grad_up, grad_down
    )
    output = (hidden_one + pair_sum[0] + biases[3]).astype(BF)
    grad_normed_two = pair_sum[1]
    grad_hidden_one = cotangent.astype(F32) + normalize_back(
        grad_normed_two, unit_two, scale_two, gains[1]
    )
    grad_attn = grad_hidden_one.astype(BF)
    full_attn, u0, u1 = rows_back(grad_attn, s0, s1)
    full_attn = full_attn.reshape(512, 768)
    grad_mixed = jnp.where(low_lanes, 0.0, matmul(full_attn, w_qo)).astype(BF)
    delta = (grad_mixed.astype(F32) * mixed).reshape(512, 3, 128).sum(axis=-1).T
    grad_near = attend_back(lim, clip, query, grad_mixed, near, lse, delta).reshape(3584, 768)
    near_back = matmul_nt(grad_near, w_attn).astype(BF).reshape(7, 4, 128, 768)
    near_sum = jnp.sum(grad_near.astype(F32), axis=0)
    unit_grad = matmul_tn(near_unit, grad_near)
    grad_w = unit_grad * gains[0][:, None] + biases[0][:, None] * near_sum[None, :]
    grad_w_out = matmul_tn(full_attn, mixed_low)
    w_full = w_attn.astype(F32)

    sums = jnp.stack(
        [
            jnp.sum(unit_grad * w_full, axis=1),
            jnp.sum(grad_normed_two * unit_two, axis=0),
            jnp.sum(w_full * near_sum[None, :], axis=1),
            jnp.sum(grad_attn.astype(F32), axis=0),
            jnp.sum(grad_normed_two, axis=0),
            jnp.sum(cotangent.astype(F32), axis=0),
        ]
    )
    sums = sums.reshape(6, 64, 12).transpose(1, 0, 2).reshape(64, 72)
    q_sum = near_sum[384:768].reshape(3, 128)[:, :64]
    v_sum = near_sum[0:384].reshape(3, 128)[:, 64:]
    qv_sum = jnp.concatenate([q_sum, v_sum], axis=0).T
    up_sum = jnp.sum(grad_inner.astype(F32), axis=0)
    up_sum = up_sum.reshape(3, 64, 4).transpose(1, 0, 2).reshape(64, 12)
    smalls = jnp.concatenate([sums, qv_sum, up_sum], axis=1)
    smalls = jnp.pad(smalls.reshape(64, 1, 90), ((0, 0), (12, 3), (0, 678)))
    grad_w = jnp.concatenate([grad_w[:, 0:384], grad_w[:, 384:768] + grad_w_out], axis=1)
    grad_w = widen(grad_w.astype(BF)) + smalls.astype(BF).reshape(2, 4, 4, 2, 16, 768)
    back_one, own, far = return_all(near_back, grad_w, u0, u1)
    _, unit_one, scale_one = normalize(hidden, gains[0], biases[0])
    grad_tokens = grad_hidden_one + normalize_back(back_one, unit_one, scale_one, gains[0])
    vec = own[0, 12, 0:128] + own[1, 12, 0:128] + far[12]
    vec = vec[0:72].reshape(6, 2, 6)
    vec = jnp.where(t == 0, vec[:, 0], vec[:, 1])
    grad_gain, grad_row = vec[0:2].reshape(1, 2, 6), vec[2:6].reshape(1, 4, 6)
    grad_qv = own[:, 12, 72:78].reshape(2, 2, 3).transpose(1, 0, 2).reshape(1, 2, 6, 1)
    grad_up_bias = own[:, 12, 78:90].reshape(1, 6, 4)
    main = own[:, 0:12].transpose(1, 0, 2)
    g_kv = main[:, :, 0:384].reshape(12, 6, 2, 64)
    g_qo = main[:, :, 384:768].reshape(12, 6, 2, 64)
    grad_in = jnp.stack(
        [
            g_qo[:, :, 0].reshape(12, 384),
            g_kv[:, :, 0].reshape(12, 384),
            g_kv[:, :, 1].reshape(12, 384),
        ]
    )[None]
    grad_out = g_qo[:, :, 1].reshape(12, 384).T[None]
    grad_fc_in = main[:, :, 768:1536].reshape(1, 12, 1536)
    grad_fc_out = main[:, :, 1536:2304].reshape(12, 1536).T[None]
    return (
        output,
        grad_tokens,
        grad_in,
        grad_qv,
        grad_out,
        grad_fc_in,
        grad_up_bias,
        grad_fc_out,
        grad_gain,
        grad_row,
    )


def solution(mesh):
    return jax.shard_map(
        body,
        mesh=mesh,
        in_specs=(
            P(("dp", "tensor"), None),
            P(None, "dp"),
            P(None, None, "dp", "tensor"),
            P(None, None, "tensor", "dp"),
            P(None, "tensor", "dp"),
            P(None, "dp", "tensor"),
            P(None, "tensor", "dp"),
            P(None, "tensor", "dp"),
            P(None, None, ("dp", "tensor")),
            P(None, None, ("dp", "tensor")),
            P(("dp", "tensor"), None),
        ),
        out_specs=(
            P(("dp", "tensor"), None),
            P(("dp", "tensor"), None),
            P(None, None, "dp", "tensor"),
            P(None, None, "tensor", "dp"),
            P(None, "tensor", "dp"),
            P(None, "dp", "tensor"),
            P(None, "tensor", "dp"),
            P(None, "tensor", "dp"),
            P(None, None, ("dp", "tensor")),
            P(None, None, ("dp", "tensor")),
        ),
        check_vma=False,
    )
```

```python
import jax
import jax.numpy as jnp
import numpy as np
from jax import lax
import jax.experimental.pallas as pl
import jax.experimental.pallas.tpu as pltpu
from jax.sharding import PartitionSpec as P

EPS = 1e-05
NEGATIVE = -1e30
SCORE_SCALE = 0.125
BF = jnp.bfloat16
F32 = jnp.float32
MESH = pl.DeviceIdType.MESH
VM = pl.BlockSpec(memory_space=pltpu.VMEM)
SM = pl.BlockSpec(memory_space=pltpu.SMEM)
DMA = pltpu.SemaphoreType.DMA
LIMIT = 56 * 2**20
NT = (((1,), (1,)), ((), ()))
TN = (((0,), (0,)), ((), ()))


def coords():
    dp = lax.axis_index("dp")
    return dp // 32, (dp // 8) % 4, (dp // 2) % 4, dp % 2, lax.axis_index("tensor")


def device(z, y, x, k, t):
    return (((z * 4 + y) * 4 + x) * 2 + k, t)


def chip(c, k, t):
    return (c * 2 + k, t)


def greet(peers):
    bar = pltpu.get_barrier_semaphore()
    for peer in peers:
        pl.semaphore_signal(bar, inc=1, device_id=peer, device_id_type=MESH)
    pl.semaphore_wait(bar, len(peers))


def remote(src, dst, sems, index, peer):
    send, recv = sems
    return pltpu.make_async_remote_copy(
        src, dst, send.at[index], recv.at[index], device_id=peer, device_id_type=MESH
    )


def comm_call(kernel, out_shape, scratch, cid, name, args):
    single = not isinstance(out_shape, (list, tuple))
    return pl.pallas_call(
        kernel,
        out_shape=out_shape,
        in_specs=[VM] * len(args),
        out_specs=VM if single else [VM] * len(out_shape),
        scratch_shapes=scratch,
        compiler_params=pltpu.CompilerParams(
            collective_id=cid, has_side_effects=True, vmem_limit_bytes=LIMIT
        ),
        name=name,
    )(*args)


def spots():
    z, y, x, k, t = coords()
    xs = [device(z, y, (x + d) % 4, k, t) for d in (1, 2, 3)]
    ys = [device(z, (y + d) % 4, x, k, t) for d in (1, 2, 3)]
    core = device(z, y, x, 1 - k, t)
    far = device(z, y, x, k, 1 - t)
    low = device(1 - z, y, x, k, t)
    ring = [chip(((z * 4 + y) * 4 + x + d) % 32, k, t) for d in RING]
    return (z, y, x, k, t), xs, ys, core, far, low, ring


RING = (2, -2, 3, -3, 1, -1)


class Copies:
    def __init__(self, send, recv):
        self.sems, self.count = (send, recv), 0

    def __call__(self, src, dst, peer):
        made = remote(src, dst, self.sems, self.count, peer)
        self.count += 1
        made.start()
        return made


def gather_kernel(
    pay, tile, clip, tok, w, f0, f1, clip_out, tk, pay_s, tile_in, ws, send, recv
):
    (z, y, x, k, t), xs, ys, core, far, low, ring = spots()
    copy = Copies(send, recv)
    mine, other = k * 2 + t, k * 2 + 1 - t
    greet(xs + ys + [core, far, low] + ring)
    c_tile = copy(tile, tile_in, far)
    own_far = copy(tok, tk.at[3, mine], far)
    order = (4, 5, 2, 3, 0, 1)
    pushes = {i: copy(tok, tk.at[3 - RING[i], mine], ring[i]) for i in order}
    done = [copy(tok, tk.at[3, mine], core), copy(clip, clip_out.at[k], core)]
    clip_out[k] = clip[...]
    tk[3, mine] = tok[...]
    c_tile.wait()
    pay_s[...] = pay[...]
    for q in range(2):
        pay_s[q, :, 0:128] = pay[q, :, 0:128] + tile_in[...]
    swap = copy(pay_s.at[1 - k], ws.at[z, k], core)
    ws[z, k] = pay_s[k]
    swap.wait()
    c_low = copy(ws.at[z], ws.at[z], low)
    to_far = {}

    def pass_on(i):
        pushes[i].wait_recv()
        a = tk.at[3 - RING[i], mine]
        to_far[i] = copy(a, a, far)
        done.append(copy(a, a, core))

    pass_on(4)
    pass_on(5)
    c_low.wait()
    w[:, y, x] = ws[:, :, :, 0:768]
    f0[:, x] = ws[:, :, :, 768:1536]
    f1[:, y] = ws[:, :, :, 1536:2304]
    h0, h1 = pl.ds(0, 384), pl.ds(384, 384)
    phase = []
    for i in range(3):
        phase.append(copy(ws.at[:, :, :, h0], w.at[:, y, x, :, :, h0], xs[i]))
        phase.append(copy(ws.at[:, :, :, h1], w.at[:, y, x, :, :, h1], ys[i]))
    pass_on(2)
    pass_on(3)
    for c in phase:
        c.wait()
    rest = []
    for i in range(3):
        a = w.at[:, y, :, :, :, h0]
        rest.append(copy(a, a, ys[i]))
        b = w.at[:, :, x, :, :, h1]
        rest.append(copy(b, b, xs[i]))
    pass_on(0)
    pass_on(1)
    for i in range(3):
        rest.append(copy(ws.at[:, :, :, pl.ds(768, 768)], f0.at[:, x], xs[i]))
        rest.append(copy(ws.at[:, :, :, pl.ds(1536, 768)], f1.at[:, y], ys[i]))
    own_far.wait_recv()
    done.append(copy(tk.at[3, other], tk.at[3, other], core))
    for i in order:
        to_far[i].wait_recv()
        a = tk.at[3 - RING[i], other]
        done.append(copy(a, a, core))
    for i in order:
        pushes[i].wait_send()
        to_far[i].wait_send()
    own_far.wait_send()
    for c in rest + done:
        c.wait()


def gather_all(pay, tile, clip, tok):
    return comm_call(
        gather_kernel,
        [
            jax.ShapeDtypeStruct((2, 4, 4, 2, 16, 768), BF),
            jax.ShapeDtypeStruct((2, 4, 2, 16, 768), BF),
            jax.ShapeDtypeStruct((2, 4, 2, 16, 768), BF),
            jax.ShapeDtypeStruct((2, 2, 256), jnp.int32),
            jax.ShapeDtypeStruct((7, 4, 128, 768), BF),
        ],
        [
            pltpu.VMEM((2, 16, 2304), BF),
            pltpu.VMEM((16, 128), BF),
            pltpu.VMEM((2, 2, 16, 2304), BF),
            DMA((53,)),
            DMA((53,)),
        ],
        0,
        "gather_first",
        (pay, tile, clip, tok),
    )


def piece_copies(copy, f0, f1, p0, p1, p, x, y, xs, ys):
    made = []
    for i in range(3):
        made.append(copy(f0.at[p], p0.at[y], ys[i]))
        made.append(copy(f1.at[p], p1.at[:, x], xs[i]))
    p0[y] = f0[p]
    p1[:, x] = f1[p]
    return made


PIECE = [jax.ShapeDtypeStruct((4, 4, 2, 16, 768), BF)] * 2


def exchange_rows(copy, a, out, k, t, core, far):
    mine, other = k * 2 + t, k * 2 + 1 - t
    c_far = copy(a, out.at[mine], far)
    c_core = copy(a, out.at[mine], core)
    out[mine] = a[...]

    def finish():
        c_far.wait_recv()
        c_pass = copy(out.at[other], out.at[other], core)
        c_far.wait_send()
        c_core.wait()
        c_pass.wait()

    return finish


def exchange_sums(copy, p, out, got_core, mid, got_far, k, t, core, far):
    n = p.shape[0]
    to_core = [copy(p.at[i, pl.ds((1 - k) * 2, 2)], got_core.at[i], core) for i in range(n)]

    def finish():
        to_far = []
        for i in range(n):
            to_core[i].wait()
            mid[i] = (p[i, k * 2 + 1 - t].astype(F32) + got_core[i, 1 - t].astype(F32)).astype(BF)
            to_far.append(copy(mid.at[i], got_far.at[i], far))
        for i in range(n):
            part = p[i, k * 2 + t].astype(F32) + got_core[i, t].astype(F32)
            to_far[i].wait()
            out[i] = part + got_far[i].astype(F32)

    return finish


def sum_scratch(n):
    return [
        pltpu.VMEM((n, 2, 128, 768), BF),
        pltpu.VMEM((n, 128, 768), BF),
        pltpu.VMEM((n, 128, 768), BF),
    ]


def sum_attn_kernel(p, f0, f1, out, p0, p1, got_core, mid, got_far, send, recv):
    (z, y, x, k, t), xs, ys, core, far, low, ring = spots()
    copy = Copies(send, recv)
    greet(xs + ys + [core, far])
    finish = exchange_sums(copy, p, out, got_core, mid, got_far, k, t, core, far)
    made = piece_copies(copy, f0, f1, p0, p1, 0, x, y, xs, ys)
    finish()
    for c in made:
        c.wait()


def sum_attn(p, f0, f1):
    return comm_call(
        sum_attn_kernel,
        [jax.ShapeDtypeStruct((1, 128, 768), F32)] + PIECE,
        sum_scratch(1) + [DMA((8,)), DMA((8,))],
        1,
        "sum_attn",
        (p, f0, f1),
    )


def rows_two_kernel(a, cot, f0, f1, out, cot_out, p0, p1, send, recv):
    (z, y, x, k, t), xs, ys, core, far, low, ring = spots()
    copy = Copies(send, recv)
    greet(xs + ys + [core, far])
    finish = exchange_rows(copy, a, out, k, t, core, far)
    made = piece_copies(copy, f0, f1, p0, p1, 1, x, y, xs, ys)
    finish_cot = exchange_rows(copy, cot, cot_out, k, t, core, far)
    finish()
    finish_cot()
    for c in made:
        c.wait()


def rows_two(a, cot, f0, f1):
    return comm_call(
        rows_two_kernel,
        [jax.ShapeDtypeStruct((4, 128, 768), BF)] * 2 + PIECE,
        [DMA((12,)), DMA((12,))],
        2,
        "rows_two",
        (a, cot, f0, f1),
    )


def spread_first(copy, g0, g1, b0, b1, x, y, xs, ys):
    over_y, over_x = [], []
    for i in range(3):
        over_y.append(copy(g0.at[:, (y + i + 1) % 4], b0.at[i], ys[i]))
        over_x.append(copy(g1.at[:, :, (x + i + 1) % 4], b1.at[i], xs[i]))
    return over_y, over_x


def add_first(g0, g1, b0, b1, s0, s1, x, y, over_y, over_x):
    for c in over_y:
        c.wait()

    @pl.loop(0, 8)
    def _(n):
        zz, m = n // 4, n % 4
        v = g0[zz, y, m].astype(F32)
        for i in range(3):
            v = v + b0[i, zz, m].astype(F32)
        s0[zz, m] = v.astype(BF)

    for c in over_x:
        c.wait()

    @pl.loop(0, 8)
    def _(n):
        zz, m = n // 4, n % 4
        v = g1[zz, m, x].astype(F32)
        for i in range(3):
            v = v + b1[i, zz, m].astype(F32)
        s1[zz, m] = v.astype(BF)


def spread_second(copy, s0, s1, a0, a1, x, y, xs, ys):
    over_x, over_y = [], []
    for i in range(3):
        over_x.append(copy(s0.at[:, (x + i + 1) % 4], a0.at[i], xs[i]))
        over_y.append(copy(s1.at[:, (y + i + 1) % 4], a1.at[i], ys[i]))
    return over_x, over_y


def add_second(s0, s1, a0, a1, u0, u1, x, y, over_x, over_y):
    for c in over_x + over_y:
        c.wait()
    for zz in range(2):
        v = s0[zz, x].astype(F32)
        v1 = s1[zz, y].astype(F32)
        for i in range(3):
            v = v + a0[i, zz].astype(F32)
            v1 = v1 + a1[i, zz].astype(F32)
        u0[zz] = v.astype(BF)
        u1[zz] = v1.astype(BF)


def sum_mlp_kernel(p, g0, g1, out, s0, s1, got_core, mid, got_far, b0, b1, send, recv):
    (z, y, x, k, t), xs, ys, core, far, low, ring = spots()
    copy = Copies(send, recv)
    greet(xs + ys + [core, far])
    finish = exchange_sums(copy, p, out, got_core, mid, got_far, k, t, core, far)
    over = spread_first(copy, g0, g1, b0, b1, x, y, xs, ys)
    finish()
    add_first(g0, g1, b0, b1, s0, s1, x, y, *over)


def sum_mlp(p, g0, g1):
    return comm_call(
        sum_mlp_kernel,
        [jax.ShapeDtypeStruct((2, 128, 768), F32)]
        + [jax.ShapeDtypeStruct((2, 4, 2, 16, 768), BF)] * 2,
        sum_scratch(2)
        + [pltpu.VMEM((3, 2, 4, 2, 16, 768), BF)] * 2
        + [DMA((10,)), DMA((10,))],
        3,
        "sum_mlp",
        (p, g0, g1),
    )


def rows_back_kernel(a, s0, s1, out, u0, u1, a0, a1, send, recv):
    (z, y, x, k, t), xs, ys, core, far, low, ring = spots()
    copy = Copies(send, recv)
    greet(xs + ys + [core, far])
    finish = exchange_rows(copy, a, out, k, t, core, far)
    over = spread_second(copy, s0, s1, a0, a1, x, y, xs, ys)
    finish()
    add_second(s0, s1, a0, a1, u0, u1, x, y, *over)


def rows_back(a, s0, s1):
    return comm_call(
        rows_back_kernel,
        [jax.ShapeDtypeStruct((4, 128, 768), BF)]
        + [jax.ShapeDtypeStruct((2, 2, 16, 768), BF)] * 2,
        [pltpu.VMEM((3, 2, 2, 16, 768), BF)] * 2 + [DMA((9,)), DMA((9,))],
        4,
        "rows_back",
        (a, s0, s1),
    )


def return_kernel(
    d, g, u0, u1, out, own, tile_out,
    got_core, e_send, got_far, r_send, got_ring,
    b0, b1, s0, s1, a0, a1, v0, v1, z_in0, z_in1, z_in2, z_in3, res, tile, send, recv,
):
    (z, y, x, k, t), xs, ys, core, far, low, ring = spots()
    copy = Copies(send, recv)
    greet(xs + ys + [core, far, low] + ring)
    order = [3 + r for r in RING] + [3]
    to_core = {j: copy(d.at[j, pl.ds((1 - k) * 2, 2)], got_core.at[j], core) for j in order}
    g0, g1 = g.at[:, :, :, :, :, pl.ds(0, 384)], g.at[:, :, :, :, :, pl.ds(384, 384)]
    over = spread_first(copy, g0, g1, b0, b1, x, y, xs, ys)
    fc_z = [copy(u0.at[1 - z], z_in0, low), copy(u1.at[1 - z], z_in1, low)]
    to_far = {}
    for j in order:
        to_core[j].wait()
        e_send[j] = (d[j, k * 2 + 1 - t].astype(F32) + got_core[j, 1 - t].astype(F32)).astype(BF)
        to_far[j] = copy(e_send.at[j], got_far.at[j], far)
    add_first(g0, g1, b0, b1, s0, s1, x, y, *over)
    over = spread_second(copy, s0, s1, a0, a1, x, y, xs, ys)
    home = []

    def send_home(i):
        j = order[i]
        to_far[j].wait()
        v = d[j, k * 2 + t].astype(F32) + got_core[j, t].astype(F32) + got_far[j].astype(F32)
        r_send[i] = v.astype(BF)
        home.append(copy(r_send.at[i], got_ring.at[i], ring[i]))

    for i in range(3):
        send_home(i)
    add_second(s0, s1, a0, a1, v0, v1, x, y, *over)
    attn_z = [copy(v0.at[1 - z], z_in2, low), copy(v1.at[1 - z], z_in3, low)]
    for i in range(3, 6):
        send_home(i)
    for c in fc_z + attn_z:
        c.wait()
    res[:, :, 0:384] = v0[z].astype(F32) + z_in2[...].astype(F32)
    res[:, :, 384:768] = v1[z].astype(F32) + z_in3[...].astype(F32)
    res[:, :, 768:1536] = u0[z].astype(F32) + z_in0[...].astype(F32)
    res[:, :, 1536:2304] = u1[z].astype(F32) + z_in1[...].astype(F32)
    swap = copy(res.at[1 - k], own.at[k], core)
    own[k] = res[k]
    to_far[3].wait()
    total = d[3, k * 2 + t].astype(F32) + got_core[3, t].astype(F32) + got_far[3].astype(F32)
    swap.wait()
    tile[...] = own[0, :, 0:128] + own[1, :, 0:128]
    c_tile = copy(tile, tile_out, far)
    for i in range(6):
        home[i].wait()
        total = total + got_ring[i].astype(F32)
    out[...] = total
    c_tile.wait()


def return_all(d, g, u0, u1):
    return comm_call(
        return_kernel,
        [
            jax.ShapeDtypeStruct((128, 768), F32),
            jax.ShapeDtypeStruct((2, 16, 2304), F32),
            jax.ShapeDtypeStruct((16, 128), F32),
        ],
        [
            pltpu.VMEM((7, 2, 128, 768), BF),
            pltpu.VMEM((7, 128, 768), BF),
            pltpu.VMEM((7, 128, 768), BF),
            pltpu.VMEM((6, 128, 768), BF),
            pltpu.VMEM((6, 128, 768), BF),
        ]
        + [pltpu.VMEM((3, 2, 4, 2, 16, 384), BF)] * 2
        + [pltpu.VMEM((2, 4, 2, 16, 384), BF)] * 2
        + [pltpu.VMEM((3, 2, 2, 16, 384), BF)] * 2
        + [pltpu.VMEM((2, 2, 16, 384), BF)] * 2
        + [pltpu.VMEM((2, 16, 768), BF)] * 2
        + [pltpu.VMEM((2, 16, 384), BF)] * 2
        + [pltpu.VMEM((2, 16, 2304), F32), pltpu.VMEM((16, 128), F32), DMA((38,)), DMA((38,))],
        5,
        "return_all",
        (d, g, u0, u1),
    )


def layout_tables():
    d = np.arange(768)
    n64 = np.arange(64)[:, None]
    own = (d // 12 == n64).astype(np.float32)
    lane = d % 128
    high = d < 384
    column = np.where(high, lane - 64, lane)
    heads = ((column == n64) & (column >= 0) & (column < 64)).astype(np.float32)
    hidden = ((d % 256) // 4 == n64).astype(np.float32)
    spread = np.stack([own, heads, hidden])
    spot = 64 * ((d % 12) // 6) + d % 6
    head = (d % 384) // 128
    rows = [spot + 6 * p for p in range(6)]
    rows.append(np.where(high, 6, 0) + head)
    rows.append(12 + (d // 256) * 4 + d % 4)
    step = np.zeros((8, 768), np.int32)
    step[6], step[7] = 3, 12
    back = [12 * p + d % 12 for p in range(6)]
    back.append(72 + np.where(high, 3, 0) + head)
    back.append(78 + (d // 256) * 4 + d % 4)
    select = np.arange(512)[None, :] == (np.arange(384) // 12 * 16 + np.arange(384) % 12)[:, None]
    row12 = np.arange(512)[:, None] == np.arange(32)[None, :] * 16 + 12
    return (
        spread,
        np.stack(rows).astype(np.int32),
        step,
        np.stack(back).astype(np.int32),
        select.astype(np.float32),
        row12.astype(np.float32),
    )


SPREAD, FETCH, FETCH_STEP, PUT, SELECT, ROW12 = layout_tables()


def matmul(left, right):
    return jnp.dot(left, right, preferred_element_type=F32)


def matmul_nt(left, right):
    return lax.dot_general(left, right, NT, preferred_element_type=F32)


def matmul_tn(left, right):
    return lax.dot_general(left, right, TN, preferred_element_type=F32)


def allowed_pairs(lim, clip, qb, j):
    cols = pl.ds(qb * 256, 256)
    pos = lim[4] + j * 256 + lax.broadcasted_iota(jnp.int32, (256, 256), 0)
    return (pos >= clip[0:1, cols]) & (pos < clip[1:2, cols])


def front_kernel(
    lim, clip, w, row12, row13, spread, fetch, select, tk,
    vecs, w_attn, unit, kv, q, of, lse, attn,
):
    line = lax.broadcasted_iota(jnp.int32, (128, 768), 0)
    wide = matmul_tn(row12[...], spread[0])
    for p in range(6):
        hit = line == fetch[p : p + 1, :]
        vecs[p : p + 1, :] = jnp.sum(jnp.where(hit, wide, 0.0), axis=0, keepdims=True)
    for p in (6, 7):
        wide = matmul_tn(row13[...], spread[p - 5])
        hit = line == fetch[p : p + 1, :]
        vecs[p : p + 1, :] = jnp.sum(jnp.where(hit, wide, 0.0), axis=0, keepdims=True)
    for z in range(2):
        w_attn[z * 384 : z * 384 + 384, :] = matmul(select[...], w[z]).astype(BF)

    def norm_rows(j):
        v = tk[j].astype(F32)
        centred = v - jnp.mean(v, axis=-1, keepdims=True)
        spread_out = jnp.mean(centred * centred, axis=-1, keepdims=True)
        u = centred * lax.rsqrt(spread_out + EPS)
        return u, (u * vecs[0:1, :] + vecs[2:3, :]).astype(BF)

    @pl.loop(lim[0], lim[3])
    def _(j):
        u, a = norm_rows(j)
        unit[j] = u.astype(BF)
        kv[j] = (matmul(a, w_attn[:, 0:384]) + vecs[6:7, 0:384]).astype(BF)

    low = (lax.broadcasted_iota(jnp.int32, (256, 384), 1) & 127) < 64
    for qb in range(2):
        _, a = norm_rows(6 + qb)
        v = (matmul(a, w_attn[:, 384:768]) + vecs[6:7, 384:768]).astype(BF).astype(F32)
        q[qb * 256 : qb * 256 + 256, :] = jnp.where(low, v * SCORE_SCALE, 0.0).astype(BF)

    lane = lax.broadcasted_iota(jnp.int32, (256, 128), 1)
    for qb in range(2):
        rows = slice(qb * 256, qb * 256 + 256)

        def step(j, carry):
            ok = allowed_pairs(lim, clip, qb, j)
            new = []
            for h in range(3):
                m, l, acc = carry[h]
                cols = slice(h * 128, h * 128 + 128)
                keys = kv[j, :, cols]
                s = jnp.where(ok, matmul_nt(keys, q[rows, cols]), NEGATIVE)
                top = jnp.maximum(m, jnp.max(s, axis=0, keepdims=True))
                p = jnp.exp(s - top)
                fade = jnp.exp(m - top)
                l = l * fade + jnp.sum(p, axis=0, keepdims=True)
                acc = acc * fade + matmul_tn(keys, p.astype(BF))
                new.append((top, l, acc))
            return tuple(new)

        start = tuple(
            (
                jnp.full((1, 256), NEGATIVE, F32),
                jnp.zeros((1, 256), F32),
                jnp.zeros((128, 256), F32),
            )
            for _ in range(3)
        )
        final = lax.fori_loop(lim[2 * qb], lim[2 * qb + 1], step, start)
        for h in range(3):
            m, l, acc = final[h]
            o = (acc / l).T
            of[rows, h * 128 : h * 128 + 128] = jnp.where(lane >= 64, o, 0.0)
            lse[h : h + 1, rows] = m + jnp.log(l)
        attn[rows, :] = matmul_nt(of[rows, :].astype(BF), w_attn[:, 384:768]).astype(BF)


def front(lim, clip, w, row12, row13, spread, fetch, select, tk):
    return pl.pallas_call(
        front_kernel,
        out_shape=[
            jax.ShapeDtypeStruct((8, 768), F32),
            jax.ShapeDtypeStruct((768, 768), BF),
            jax.ShapeDtypeStruct((14, 256, 768), BF),
            jax.ShapeDtypeStruct((14, 256, 384), BF),
            jax.ShapeDtypeStruct((512, 384), BF),
            jax.ShapeDtypeStruct((512, 384), F32),
            jax.ShapeDtypeStruct((3, 512), F32),
            jax.ShapeDtypeStruct((512, 768), BF),
        ],
        in_specs=[SM] + [VM] * 8,
        out_specs=[VM] * 8,
        compiler_params=pltpu.CompilerParams(vmem_limit_bytes=LIMIT),
        name="front",
    )(lim, clip, w, row12, row13, spread, fetch, select, tk)


def middle_kernel(
    b, cot, up_a, up_b, down_a, down_b, vecs, select,
    pair, g0, g1, up_sum, w_up, w_down, active, inner_back,
):
    for i, (up, down) in enumerate(((up_a, down_a), (up_b, down_b))):
        rows = slice(i * 384, i * 384 + 384)
        w_up[rows, :] = matmul(select[...], up[...]).astype(BF)
        w_down[rows, :] = matmul(select[...], down[...]).astype(BF)
    up_sum[...] = jnp.zeros((1, 768), F32)

    @pl.loop(0, 4)
    def _(r):
        rows = pl.ds(pl.multiple_of(r * 128, 128), 128)
        u = matmul(b[rows, :], w_up[...]) + vecs[7:8, :]
        phi = 0.5 + 0.5 * lax.erf(u * 0.7071067811865476)
        gl = (u * phi).astype(BF)
        active[rows, :] = gl
        pair[0, rows, :] = matmul_nt(gl, w_down[...]).astype(BF)
        slope = phi + u * jnp.exp(-0.5 * u * u) * 0.3989422804014327
        du = (matmul(cot[rows, :], w_down[...]) * slope).astype(BF)
        inner_back[rows, :] = du
        up_sum[...] += jnp.sum(du.astype(F32), axis=0, keepdims=True)
        pair[1, rows, :] = matmul_nt(du, w_up[...]).astype(BF)

    for i in range(2):
        cols = slice(i * 384, i * 384 + 384)
        g = matmul_tn(b[:, cols], inner_back[...]).astype(BF)
        g0[i] = matmul_tn(select[...], g).astype(BF)
        g = matmul_tn(cot[:, cols], active[...]).astype(BF)
        g1[i] = matmul_tn(select[...], g).astype(BF)


def middle(b, cot, up_a, up_b, down_a, down_b, vecs, select):
    return pl.pallas_call(
        middle_kernel,
        out_shape=[
            jax.ShapeDtypeStruct((2, 512, 768), BF),
            jax.ShapeDtypeStruct((2, 512, 768), BF),
            jax.ShapeDtypeStruct((2, 512, 768), BF),
            jax.ShapeDtypeStruct((1, 768), F32),
        ],
        in_specs=[VM] * 8,
        out_specs=[VM] * 4,
        scratch_shapes=[
            pltpu.VMEM((768, 768), BF),
            pltpu.VMEM((768, 768), BF),
            pltpu.VMEM((512, 768), BF),
            pltpu.VMEM((512, 768), BF),
        ],
        compiler_params=pltpu.CompilerParams(vmem_limit_bytes=LIMIT),
        name="middle",
    )(b, cot, up_a, up_b, down_a, down_b, vecs, select)


def back_kernel(
    lim, clip, q, dr, of, kv, lse, unit, w_attn, vecs, sums, up_sum, spread, put, select, row12,
    d_out, grad, total, dox, delta, dq, ug,
):
    lane = lax.broadcasted_iota(jnp.int32, (256, 128), 1)
    high = (lax.broadcasted_iota(jnp.int32, (256, 384), 1) & 127) >= 64

    @pl.loop(0, 14)
    def _(j):
        total[j] = jnp.zeros((256, 384), F32)
        d_out[j] = jnp.zeros((256, 768), BF)

    for qb in range(2):
        rows = slice(qb * 256, qb * 256 + 256)
        g = jnp.where(high, matmul(dr[rows, :], w_attn[:, 384:768]), 0.0).astype(BF)
        dox[rows, :] = g
        prod = g.astype(F32) * of[rows, :]
        for h in range(3):
            part = prod[:, h * 128 : h * 128 + 128].T
            delta[h : h + 1, rows] = jnp.sum(part, axis=0, keepdims=True)

    for qb in range(2):
        rows = slice(qb * 256, qb * 256 + 256)

        def step(j, carry):
            ok = allowed_pairs(lim, clip, qb, j)
            new = []
            for h in range(3):
                cols = slice(h * 128, h * 128 + 128)
                keys = kv[j, :, cols]
                qh, dh = q[rows, cols], dox[rows, cols]
                s = jnp.where(ok, matmul_nt(keys, qh), NEGATIVE)
                p = jnp.exp(s - lse[h : h + 1, rows])
                ds = (p * (matmul_nt(keys, dh) - delta[h : h + 1, rows])).astype(BF)
                new.append(carry[h] + matmul_tn(keys, ds))
                total[j, :, cols] += matmul(ds, qh) + matmul(p.astype(BF), dh)
            return tuple(new)

        start = tuple(jnp.zeros((128, 256), F32) for _ in range(3))
        final = lax.fori_loop(lim[2 * qb], lim[2 * qb + 1], step, start)
        for h in range(3):
            part = jnp.where(lane < 64, SCORE_SCALE * final[h].T, 0.0)
            dq[rows, h * 128 : h * 128 + 128] = part.astype(BF)

    ug[...] = jnp.zeros((768, 768), F32)

    def chunk(j, kv_sum):
        z = total[j].astype(BF)
        d_out[j] = matmul_nt(z, w_attn[:, 0:384]).astype(BF)
        ug[:, 0:384] += matmul_tn(unit[j], z)
        return kv_sum + jnp.sum(z.astype(F32), axis=0, keepdims=True)

    kv_sum = lax.fori_loop(lim[0], lim[3], chunk, jnp.zeros((1, 384), F32))
    for qb in range(2):
        rows = slice(qb * 256, qb * 256 + 256)
        own = matmul_nt(total[6 + qb].astype(BF), w_attn[:, 0:384])
        d_out[6 + qb] = (own + matmul_nt(dq[rows, :], w_attn[:, 384:768])).astype(BF)
        ug[:, 384:768] += matmul_tn(unit[6 + qb], dq[rows, :])
    q_sum = jnp.sum(dq[...].astype(F32), axis=0, keepdims=True)
    z_sum = jnp.concatenate([kv_sum, q_sum], axis=1)

    line = lax.broadcasted_iota(jnp.int32, (128, 768), 0)

    def place(p, row):
        return jnp.where(line == put[p : p + 1, :], row, 0.0)

    columns = vecs[...].T
    gain_col, offset_col = columns[:, 0:1], columns[:, 2:3]
    w_full = w_attn[...].astype(F32)
    gain_sum = jnp.sum(ug[...] * w_full, axis=1, keepdims=True)
    offset_sum = jnp.sum(w_full * z_sum, axis=1, keepdims=True)
    flip = lax.broadcasted_iota(jnp.int32, (768, 128), 1)
    both = jnp.where(flip == 0, gain_sum, jnp.where(flip == 1, offset_sum, 0.0)).T
    own = place(0, both[0:1, :]) + place(2, both[1:2, :])
    for i, p in enumerate((1, 3, 4, 5)):
        own = own + place(p, sums[i : i + 1, :])
    small = matmul_nt(spread[0], own.astype(BF))
    small += matmul_nt(spread[1], place(6, z_sum).astype(BF))
    small += matmul_nt(spread[2], place(7, up_sum[...]).astype(BF))
    small = small.astype(BF)

    ug[...] = ug[...] * gain_col + offset_col * z_sum
    ug[:, 384:768] += matmul_tn(dr[...], of[...].astype(BF))
    for i in range(2):
        g = matmul_tn(select[...], ug[i * 384 : i * 384 + 384, :].astype(BF))
        grad[i] = g.astype(BF)
        extra = matmul(row12[...], small[i * 32 : i * 32 + 32, :])
        grad[i, :, 0:128] = (g[:, 0:128] + extra).astype(BF)


def back(lim, *args):
    return pl.pallas_call(
        back_kernel,
        out_shape=[
            jax.ShapeDtypeStruct((14, 256, 768), BF),
            jax.ShapeDtypeStruct((2, 512, 768), BF),
        ],
        in_specs=[SM] + [VM] * len(args),
        out_specs=[VM, VM],
        scratch_shapes=[
            pltpu.VMEM((14, 256, 384), F32),
            pltpu.VMEM((512, 384), BF),
            pltpu.VMEM((3, 512), F32),
            pltpu.VMEM((512, 384), BF),
            pltpu.VMEM((768, 768), F32),
        ],
        compiler_params=pltpu.CompilerParams(vmem_limit_bytes=LIMIT),
        name="back",
    )(lim, *args)


def normalize(hidden, gain, offset):
    average = jnp.mean(hidden, axis=-1, keepdims=True)
    centred = hidden - average
    spread = jnp.mean(centred * centred, axis=-1, keepdims=True)
    scale = lax.rsqrt(spread + EPS)
    unit = centred * scale
    return unit * gain + offset, unit, scale


def normalize_back(grad_out, unit, scale, gain):
    grad_unit = grad_out * gain
    first = jnp.mean(grad_unit, axis=-1, keepdims=True)
    second = jnp.mean(grad_unit * unit, axis=-1, keepdims=True)
    return scale * (grad_unit - first - unit * second)


def body(
    tokens,
    clip_bounds,
    attn_in,
    qv_bias,
    out_proj,
    fc_in,
    fc_bias,
    fc_out,
    ln_gain,
    row_bias,
    cotangent,
):
    dp = lax.axis_index("dp")
    c, k, t = dp // 2, dp % 2, lax.axis_index("tensor")
    spread, select, row12 = jnp.asarray(SPREAD, BF), jnp.asarray(SELECT, BF), jnp.asarray(ROW12, BF)
    put = jnp.asarray(PUT)
    fetch = jnp.asarray(FETCH) + k * jnp.asarray(FETCH_STEP)

    parts = attn_in[0].reshape(3, 12, 6, 64)
    proj = out_proj[0].T.reshape(12, 6, 64)
    kv_w = jnp.stack([parts[1], parts[2]], axis=2).reshape(12, 2, 384)
    qo_w = jnp.stack([parts[0], proj], axis=2).reshape(12, 2, 384)
    up_w = fc_in[0].reshape(12, 2, 768)
    down_w = fc_out[0].T.reshape(12, 2, 768)
    pay = jnp.concatenate([kv_w, qo_w, up_w, down_w], axis=-1).transpose(1, 0, 2)
    norms = jnp.concatenate([ln_gain.reshape(1, 12), row_bias.reshape(1, 24)], axis=1)
    blank = jnp.zeros((1, 64), BF)
    norms = jnp.pad(norms, ((0, 0), (0, 28)))
    norms = jnp.where(
        t == 0,
        jnp.concatenate([norms, blank], axis=1),
        jnp.concatenate([blank, norms], axis=1),
    )
    others = jnp.concatenate([qv_bias.reshape(1, 12), fc_bias.reshape(1, 24)], axis=1)
    others = jnp.pad(others, ((0, 0), (0, 92)))
    extra = jnp.pad(jnp.concatenate([norms, others]), ((0, 2), (0, 2176)))[None]
    pay = jnp.concatenate([pay, jnp.concatenate([extra, extra])], axis=1)
    tile = jnp.pad(norms, ((12, 3), (0, 0)))
    w, f0, f1, clip, near_tokens = gather_all(pay, tile, clip_bounds, tokens)
    clip = clip.transpose(1, 0, 2).reshape(2, 512)
    rows = w.reshape(64, 16, 768)[:, 12:14, 0:128]
    base = (c - 3) * 512
    lim = jnp.stack(
        [
            (clip[0, 0] - base) // 256,
            (clip[1, 255] - base + 255) // 256,
            (clip[0, 256] - base) // 256,
            (clip[1, 511] - base + 255) // 256,
            base,
        ]
    ).astype(jnp.int32)
    vecs, w_attn, unit, near, query, mixed, lse, attn = front(
        lim,
        clip,
        w.reshape(2, 512, 768),
        rows[:, 0],
        rows[:, 1],
        spread,
        fetch,
        select,
        near_tokens.reshape(14, 256, 768),
    )
    gains, biases = vecs[0:2], vecs[2:6]
    hidden = tokens.astype(F32)
    attn, up_a, down_a = sum_attn(attn.reshape(1, 4, 128, 768), f0, f1)
    hidden_one = hidden + attn[0] + biases[1]
    normed_two, unit_two, scale_two = normalize(hidden_one, gains[1], biases[2])
    full_two, cot, up_b, down_b = rows_two(normed_two.astype(BF), cotangent, f0, f1)
    pair, grad_up, grad_down, up_sum = middle(
        full_two.reshape(512, 768),
        cot.reshape(512, 768),
        up_a.reshape(512, 768),
        up_b.reshape(512, 768),
        down_a.reshape(512, 768),
        down_b.reshape(512, 768),
        vecs,
        select,
    )
    shape = (2, 4, 4, 2, 16, 768)
    pair_sum, s0, s1 = sum_mlp(
        pair.reshape(2, 4, 128, 768), grad_up.reshape(shape), grad_down.reshape(shape)
    )
    output = (hidden_one + pair_sum[0] + biases[3]).astype(BF)
    grad_normed_two = pair_sum[1]
    grad_hidden_one = cotangent.astype(F32) + normalize_back(
        grad_normed_two, unit_two, scale_two, gains[1]
    )
    grad_attn = grad_hidden_one.astype(BF)
    full_attn, u0, u1 = rows_back(grad_attn, s0, s1)
    sums = jnp.stack(
        [
            jnp.sum(grad_normed_two * unit_two, axis=0),
            jnp.sum(grad_attn.astype(F32), axis=0),
            jnp.sum(grad_normed_two, axis=0),
            jnp.sum(cotangent.astype(F32), axis=0),
        ]
    )
    near_back, grad_w = back(
        lim,
        clip,
        query,
        full_attn.reshape(512, 768),
        mixed,
        near,
        lse,
        unit,
        w_attn,
        vecs,
        sums,
        up_sum,
        spread,
        put,
        select,
        row12,
    )
    back_one, own, far = return_all(
        near_back.reshape(7, 4, 128, 768), grad_w.reshape(shape), u0, u1
    )
    _, unit_one, scale_one = normalize(hidden, gains[0], biases[0])
    grad_tokens = grad_hidden_one + normalize_back(back_one, unit_one, scale_one, gains[0])
    vec = own[0, 12, 0:128] + own[1, 12, 0:128] + far[12]
    vec = vec[0:72].reshape(6, 2, 6)
    vec = jnp.where(t == 0, vec[:, 0], vec[:, 1])
    grad_gain, grad_row = vec[0:2].reshape(1, 2, 6), vec[2:6].reshape(1, 4, 6)
    grad_qv = own[:, 12, 72:78].reshape(2, 2, 3).transpose(1, 0, 2).reshape(1, 2, 6, 1)
    grad_up_bias = own[:, 12, 78:90].reshape(1, 6, 4)
    main = own[:, 0:12].transpose(1, 0, 2)
    g_kv = main[:, :, 0:384].reshape(12, 6, 2, 64)
    g_qo = main[:, :, 384:768].reshape(12, 6, 2, 64)
    grad_in = jnp.stack(
        [
            g_qo[:, :, 0].reshape(12, 384),
            g_kv[:, :, 0].reshape(12, 384),
            g_kv[:, :, 1].reshape(12, 384),
        ]
    )[None]
    grad_out = g_qo[:, :, 1].reshape(12, 384).T[None]
    grad_fc_in = main[:, :, 768:1536].reshape(1, 12, 1536)
    grad_fc_out = main[:, :, 1536:2304].reshape(12, 1536).T[None]
    return (
        output,
        grad_tokens,
        grad_in,
        grad_qv,
        grad_out,
        grad_fc_in,
        grad_up_bias,
        grad_fc_out,
        grad_gain,
        grad_row,
    )


def solution(mesh):
    return jax.shard_map(
        body,
        mesh=mesh,
        in_specs=(
            P(("dp", "tensor"), None),
            P(None, "dp"),
            P(None, None, "dp", "tensor"),
            P(None, None, "tensor", "dp"),
            P(None, "tensor", "dp"),
            P(None, "dp", "tensor"),
            P(None, "tensor", "dp"),
            P(None, "tensor", "dp"),
            P(None, None, ("dp", "tensor")),
            P(None, None, ("dp", "tensor")),
            P(("dp", "tensor"), None),
        ),
        out_specs=(
            P(("dp", "tensor"), None),
            P(("dp", "tensor"), None),
            P(None, None, "dp", "tensor"),
            P(None, None, "tensor", "dp"),
            P(None, "tensor", "dp"),
            P(None, "dp", "tensor"),
            P(None, "tensor", "dp"),
            P(None, "tensor", "dp"),
            P(None, None, ("dp", "tensor")),
            P(None, None, ("dp", "tensor")),
        ),
        check_vma=False,
    )
```

```python
import jax
import jax.numpy as jnp
import numpy as np
from jax import lax
import jax.experimental.pallas as pl
import jax.experimental.pallas.tpu as pltpu
from jax.sharding import PartitionSpec as P

EPS = 1e-05
NEGATIVE = -1e30
SCORE_SCALE = 0.125
BF = jnp.bfloat16
F32 = jnp.float32
MESH = pl.DeviceIdType.MESH
VM = pl.BlockSpec(memory_space=pltpu.VMEM)
SM = pl.BlockSpec(memory_space=pltpu.SMEM)
DMA = pltpu.SemaphoreType.DMA
LIMIT = 56 * 2**20
NT = (((1,), (1,)), ((), ()))
TN = (((0,), (0,)), ((), ()))


def coords():
    dp = lax.axis_index("dp")
    return dp // 32, (dp // 8) % 4, (dp // 2) % 4, dp % 2, lax.axis_index("tensor")


def device(z, y, x, k, t):
    return (((z * 4 + y) * 4 + x) * 2 + k, t)


def chip(c, k, t):
    return (c * 2 + k, t)


def greet(peers):
    bar = pltpu.get_barrier_semaphore()
    for peer in peers:
        pl.semaphore_signal(bar, inc=1, device_id=peer, device_id_type=MESH)
    pl.semaphore_wait(bar, len(peers))


def remote(src, dst, sems, index, peer):
    send, recv = sems
    return pltpu.make_async_remote_copy(
        src, dst, send.at[index], recv.at[index], device_id=peer, device_id_type=MESH
    )


def comm_call(kernel, out_shape, scratch, cid, name, args):
    single = not isinstance(out_shape, (list, tuple))
    return pl.pallas_call(
        kernel,
        out_shape=out_shape,
        in_specs=[VM] * len(args),
        out_specs=VM if single else [VM] * len(out_shape),
        scratch_shapes=scratch,
        compiler_params=pltpu.CompilerParams(
            collective_id=cid, has_side_effects=True, vmem_limit_bytes=LIMIT
        ),
        name=name,
    )(*args)


def spots():
    z, y, x, k, t = coords()
    xs = [device(z, y, (x + d) % 4, k, t) for d in (1, 2, 3)]
    ys = [device(z, (y + d) % 4, x, k, t) for d in (1, 2, 3)]
    core = device(z, y, x, 1 - k, t)
    far = device(z, y, x, k, 1 - t)
    low = device(1 - z, y, x, k, t)
    ring = [chip(((z * 4 + y) * 4 + x + d) % 32, k, t) for d in RING]
    return (z, y, x, k, t), xs, ys, core, far, low, ring


RING = (2, -2, 3, -3, 1, -1)


class Copies:
    def __init__(self, send, recv):
        self.sems, self.count = (send, recv), 0

    def __call__(self, src, dst, peer):
        made = remote(src, dst, self.sems, self.count, peer)
        self.count += 1
        made.start()
        return made


def gather_kernel(
    pay, tile, clip, tok, w, f0, f1, clip_out, tk, pay_s, tile_in, ws, send, recv
):
    (z, y, x, k, t), xs, ys, core, far, low, ring = spots()
    copy = Copies(send, recv)
    mine, other = k * 2 + t, k * 2 + 1 - t
    greet(xs + ys + [core, far, low] + ring)
    c_tile = copy(tile, tile_in, far)
    own_far = copy(tok, tk.at[3, mine], far)
    order = (4, 5, 2, 3, 0, 1)
    pushes = {i: copy(tok, tk.at[3 - RING[i], mine], ring[i]) for i in order}
    done = [copy(tok, tk.at[3, mine], core), copy(clip, clip_out.at[k], core)]
    clip_out[k] = clip[...]
    tk[3, mine] = tok[...]
    c_tile.wait()
    pay_s[...] = pay[...]
    for q in range(2):
        pay_s[q, :, 0:128] = pay[q, :, 0:128] + tile_in[...]
    swap = copy(pay_s.at[1 - k], ws.at[z, k], core)
    ws[z, k] = pay_s[k]
    swap.wait()
    c_low = copy(ws.at[z], ws.at[z], low)
    to_far = {}

    def pass_on(i):
        pushes[i].wait_recv()
        a = tk.at[3 - RING[i], mine]
        to_far[i] = copy(a, a, far)
        done.append(copy(a, a, core))

    pass_on(4)
    pass_on(5)
    c_low.wait()
    w[:, y, x] = ws[:, :, :, 0:768]
    f0[:, x] = ws[:, :, :, 768:1536]
    f1[:, y] = ws[:, :, :, 1536:2304]
    h0, h1 = pl.ds(0, 384), pl.ds(384, 384)
    phase = []
    for i in range(3):
        phase.append(copy(ws.at[:, :, :, h0], w.at[:, y, x, :, :, h0], xs[i]))
        phase.append(copy(ws.at[:, :, :, h1], w.at[:, y, x, :, :, h1], ys[i]))
    pass_on(2)
    pass_on(3)
    for c in phase:
        c.wait()
    rest = []
    for i in range(3):
        a = w.at[:, y, :, :, :, h0]
        rest.append(copy(a, a, ys[i]))
        b = w.at[:, :, x, :, :, h1]
        rest.append(copy(b, b, xs[i]))
    pass_on(0)
    pass_on(1)
    for i in range(3):
        rest.append(copy(ws.at[:, :, :, pl.ds(768, 768)], f0.at[:, x], xs[i]))
        rest.append(copy(ws.at[:, :, :, pl.ds(1536, 768)], f1.at[:, y], ys[i]))
    own_far.wait_recv()
    done.append(copy(tk.at[3, other], tk.at[3, other], core))
    for i in order:
        to_far[i].wait_recv()
        a = tk.at[3 - RING[i], other]
        done.append(copy(a, a, core))
    for i in order:
        pushes[i].wait_send()
        to_far[i].wait_send()
    own_far.wait_send()
    for c in rest + done:
        c.wait()


def gather_all(pay, tile, clip, tok):
    return comm_call(
        gather_kernel,
        [
            jax.ShapeDtypeStruct((2, 4, 4, 2, 16, 768), BF),
            jax.ShapeDtypeStruct((2, 4, 2, 16, 768), BF),
            jax.ShapeDtypeStruct((2, 4, 2, 16, 768), BF),
            jax.ShapeDtypeStruct((2, 2, 256), jnp.int32),
            jax.ShapeDtypeStruct((7, 4, 128, 768), BF),
        ],
        [
            pltpu.VMEM((2, 16, 2304), BF),
            pltpu.VMEM((16, 128), BF),
            pltpu.VMEM((2, 2, 16, 2304), BF),
            DMA((53,)),
            DMA((53,)),
        ],
        0,
        "gather_first",
        (pay, tile, clip, tok),
    )


def exchange_rows(copy, a, out, k, t, core, far):
    mine, other = k * 2 + t, k * 2 + 1 - t
    c_far = copy(a, out.at[mine], far)
    c_core = copy(a, out.at[mine], core)
    out[mine] = a[...]

    def finish():
        c_far.wait_recv()
        c_pass = copy(out.at[other], out.at[other], core)
        c_far.wait_send()
        c_core.wait()
        c_pass.wait()

    return finish


def spread_first(copy, g0, g1, b0, b1, x, y, xs, ys):
    over_y, over_x = [], []
    for i in range(3):
        over_y.append(copy(g0.at[:, (y + i + 1) % 4], b0.at[i], ys[i]))
        over_x.append(copy(g1.at[:, :, (x + i + 1) % 4], b1.at[i], xs[i]))
    return over_y, over_x


def add_first(g0, g1, b0, b1, s0, s1, x, y, over_y, over_x):
    for c in over_y:
        c.wait()

    @pl.loop(0, 8)
    def _(n):
        zz, m = n // 4, n % 4
        v = g0[zz, y, m].astype(F32)
        for i in range(3):
            v = v + b0[i, zz, m].astype(F32)
        s0[zz, m] = v.astype(BF)

    for c in over_x:
        c.wait()

    @pl.loop(0, 8)
    def _(n):
        zz, m = n // 4, n % 4
        v = g1[zz, m, x].astype(F32)
        for i in range(3):
            v = v + b1[i, zz, m].astype(F32)
        s1[zz, m] = v.astype(BF)


def spread_second(copy, s0, s1, a0, a1, x, y, xs, ys):
    over_x, over_y = [], []
    for i in range(3):
        over_x.append(copy(s0.at[:, (x + i + 1) % 4], a0.at[i], xs[i]))
        over_y.append(copy(s1.at[:, (y + i + 1) % 4], a1.at[i], ys[i]))
    return over_x, over_y


def add_second(s0, s1, a0, a1, u0, u1, x, y, over_x, over_y):
    for c in over_x + over_y:
        c.wait()
    for zz in range(2):
        v = s0[zz, x].astype(F32)
        v1 = s1[zz, y].astype(F32)
        for i in range(3):
            v = v + a0[i, zz].astype(F32)
            v1 = v1 + a1[i, zz].astype(F32)
        u0[zz] = v.astype(BF)
        u1[zz] = v1.astype(BF)


def mid_kernel(
    p, f0, f1, cot, tok, vecs, select,
    output, e1, dr_full, sums, up_sum, u0, u1,
    got, mid, got_far, p0, p1, w_up, w_down, b_full, cot_full, dg, active, du_full,
    pr, got_two, mid_two, far_two, dr, g0, g1, b0, b1, s0, s1, a0, a1, send, recv,
):
    (z, y, x, k, t), xs, ys, core, far, low, ring = spots()
    copy = Copies(send, recv)
    greet(xs + ys + [core, far])
    mine, across, beside, both = k * 2 + t, k * 2 + 1 - t, 2 - 2 * k + t, 3 - 2 * k - t
    to_core = copy(p.at[pl.ds((1 - k) * 2, 2)], got, core)
    made = []
    for i in range(2):
        for j in range(3):
            made.append(copy(f0.at[i], p0.at[i, y], ys[j]))
            made.append(copy(f1.at[i], p1.at[i, :, x], xs[j]))
        p0[i, y] = f0[i]
        p1[i, :, x] = f1[i]
    to_core.wait()
    mid[...] = (p[across].astype(F32) + got[1 - t].astype(F32)).astype(BF)
    to_far = copy(mid, got_far, far)
    finish_cot = exchange_rows(copy, cot, cot_full, k, t, core, far)
    part = p[mine].astype(F32) + got[t].astype(F32) + tok[...].astype(F32) + vecs[3:4, :]
    to_far.wait()
    hidden = part + got_far[...].astype(F32)
    centred = hidden - jnp.mean(hidden, axis=-1, keepdims=True)
    scale = lax.rsqrt(jnp.mean(centred * centred, axis=-1, keepdims=True) + EPS)
    unit = centred * scale
    b_full[mine] = (unit * vecs[1:2, :] + vecs[4:5, :]).astype(BF)
    rows_far = copy(b_full.at[mine], b_full.at[mine], far)
    rows_core = copy(b_full.at[mine], b_full.at[mine], core)
    e1[...] = hidden
    finish_cot()
    for c in made:
        c.wait()
    for i in range(2):
        rows = slice(i * 384, i * 384 + 384)
        w_up[rows, :] = matmul(select[...], p0[i].reshape(512, 768)).astype(BF)
        w_down[rows, :] = matmul(select[...], p1[i].reshape(512, 768)).astype(BF)

    @pl.loop(0, 4)
    def _(i):
        dg[i] = matmul(cot_full[i], w_down[...])

    up_sum[...] = jnp.zeros((1, 768), F32)

    def feed(i):
        u = matmul(b_full[i], w_up[...]) + vecs[7:8, :]
        phi = 0.5 + 0.5 * lax.erf(u * 0.7071067811865476)
        gl = (u * phi).astype(BF)
        active[i] = gl
        pr[0, i] = matmul_nt(gl, w_down[...]).astype(BF)
        slope = phi + u * jnp.exp(-0.5 * u * u) * 0.3989422804014327
        du = (dg[i] * slope).astype(BF)
        du_full[i] = du
        up_sum[...] += jnp.sum(du.astype(F32), axis=0, keepdims=True)
        pr[1, i] = matmul_nt(du, w_up[...]).astype(BF)

    feed(mine)
    rows_core.wait()
    feed(beside)
    first = copy(pr.at[:, beside], got_two.at[:, t], core)
    rows_far.wait()
    rows_pass = copy(b_full.at[across], b_full.at[across], core)
    feed(across)
    rows_pass.wait()
    feed(both)
    second = copy(pr.at[:, both], got_two.at[:, 1 - t], core)
    second.wait()
    two = []
    for i in range(2):
        v = pr[i, across].astype(F32) + got_two[i, 1 - t].astype(F32)
        mid_two[i] = v.astype(BF)
        two.append(copy(mid_two.at[i], far_two.at[i], far))
    b_rows, du_rows = b_full[...].reshape(512, 768), du_full[...].reshape(512, 768)
    for i in range(2):
        cols = slice(i * 384, i * 384 + 384)
        g = matmul_tn(b_rows[:, cols], du_rows).astype(BF)
        g0[i] = matmul_tn(select[...], g).astype(BF).reshape(4, 4, 2, 16, 768)
    c_rows, a_rows = cot_full[...].reshape(512, 768), active[...].reshape(512, 768)
    for i in range(2):
        cols = slice(i * 384, i * 384 + 384)
        g = matmul_tn(c_rows[:, cols], a_rows).astype(BF)
        g1[i] = matmul_tn(select[...], g).astype(BF).reshape(4, 4, 2, 16, 768)
    over = spread_first(copy, g0, g1, b0, b1, x, y, xs, ys)
    first.wait()
    pair = []
    for i in range(2):
        v = pr[i, mine].astype(F32) + got_two[i, t].astype(F32)
        two[i].wait()
        pair.append(v + far_two[i].astype(F32))
    hidden = e1[...]
    output[...] = (hidden + pair[0] + vecs[5:6, :]).astype(BF)
    centred = hidden - jnp.mean(hidden, axis=-1, keepdims=True)
    scale = lax.rsqrt(jnp.mean(centred * centred, axis=-1, keepdims=True) + EPS)
    unit = centred * scale
    w = pair[1] * vecs[1:2, :]
    mean_w = jnp.mean(w, axis=-1, keepdims=True)
    mean_wu = jnp.mean(w * unit, axis=-1, keepdims=True)
    cot_f = cot[...].astype(F32)
    grad = cot_f + scale * (w - mean_w - unit * mean_wu)
    e1[...] = grad
    low_grad = grad.astype(BF)
    dr[...] = low_grad
    finish_rows = exchange_rows(copy, dr, dr_full, k, t, core, far)
    sums[0:1, :] = jnp.sum(pair[1] * unit, axis=0, keepdims=True)
    sums[1:2, :] = jnp.sum(low_grad.astype(F32), axis=0, keepdims=True)
    sums[2:3, :] = jnp.sum(pair[1], axis=0, keepdims=True)
    sums[3:4, :] = jnp.sum(cot_f, axis=0, keepdims=True)
    add_first(g0, g1, b0, b1, s0, s1, x, y, *over)
    over = spread_second(copy, s0, s1, a0, a1, x, y, xs, ys)
    finish_rows()
    add_second(s0, s1, a0, a1, u0, u1, x, y, *over)


def mid(p, f0, f1, cot, tok, vecs, select):
    rows = pltpu.VMEM((128, 768), BF)
    two = pltpu.VMEM((2, 128, 768), BF)
    four = pltpu.VMEM((4, 128, 768), BF)
    square = pltpu.VMEM((768, 768), BF)
    piece = pltpu.VMEM((2, 4, 4, 2, 16, 768), BF)
    return comm_call(
        mid_kernel,
        [
            jax.ShapeDtypeStruct((128, 768), BF),
            jax.ShapeDtypeStruct((128, 768), F32),
            jax.ShapeDtypeStruct((4, 128, 768), BF),
            jax.ShapeDtypeStruct((4, 768), F32),
            jax.ShapeDtypeStruct((1, 768), F32),
            jax.ShapeDtypeStruct((2, 2, 16, 768), BF),
            jax.ShapeDtypeStruct((2, 2, 16, 768), BF),
        ],
        [two, rows, rows, piece, piece, square, square, four, four]
        + [pltpu.VMEM((4, 128, 768), F32), four, four]
        + [pltpu.VMEM((2, 4, 128, 768), BF), pltpu.VMEM((2, 2, 128, 768), BF), two, two, rows]
        + [piece, piece]
        + [pltpu.VMEM((3, 2, 4, 2, 16, 768), BF)] * 2
        + [pltpu.VMEM((2, 4, 2, 16, 768), BF)] * 2
        + [pltpu.VMEM((3, 2, 2, 16, 768), BF)] * 2
        + [DMA((39,)), DMA((39,))],
        1,
        "mid",
        (p, f0, f1, cot, tok, vecs, select),
    )


def return_kernel(
    d, g, u0, u1, out, own, tile_out,
    got_core, e_send, got_far, r_send, got_ring,
    b0, b1, s0, s1, a0, a1, v0, v1, z_in0, z_in1, z_in2, z_in3, res, tile, send, recv,
):
    (z, y, x, k, t), xs, ys, core, far, low, ring = spots()
    copy = Copies(send, recv)
    greet(xs + ys + [core, far, low] + ring)
    order = [3 + r for r in RING] + [3]
    to_core = {j: copy(d.at[j, pl.ds((1 - k) * 2, 2)], got_core.at[j], core) for j in order}
    g0, g1 = g.at[:, :, :, :, :, pl.ds(0, 384)], g.at[:, :, :, :, :, pl.ds(384, 384)]
    over = spread_first(copy, g0, g1, b0, b1, x, y, xs, ys)
    fc_z = [copy(u0.at[1 - z], z_in0, low), copy(u1.at[1 - z], z_in1, low)]
    to_far = {}
    for j in order:
        to_core[j].wait()
        e_send[j] = (d[j, k * 2 + 1 - t].astype(F32) + got_core[j, 1 - t].astype(F32)).astype(BF)
        to_far[j] = copy(e_send.at[j], got_far.at[j], far)
    add_first(g0, g1, b0, b1, s0, s1, x, y, *over)
    over = spread_second(copy, s0, s1, a0, a1, x, y, xs, ys)
    home = []

    def send_home(i):
        j = order[i]
        to_far[j].wait()
        v = d[j, k * 2 + t].astype(F32) + got_core[j, t].astype(F32) + got_far[j].astype(F32)
        r_send[i] = v.astype(BF)
        home.append(copy(r_send.at[i], got_ring.at[i], ring[i]))

    for i in range(3):
        send_home(i)
    add_second(s0, s1, a0, a1, v0, v1, x, y, *over)
    attn_z = [copy(v0.at[1 - z], z_in2, low), copy(v1.at[1 - z], z_in3, low)]
    for i in range(3, 6):
        send_home(i)
    for c in fc_z + attn_z:
        c.wait()
    res[:, :, 0:384] = v0[z].astype(F32) + z_in2[...].astype(F32)
    res[:, :, 384:768] = v1[z].astype(F32) + z_in3[...].astype(F32)
    res[:, :, 768:1536] = u0[z].astype(F32) + z_in0[...].astype(F32)
    res[:, :, 1536:2304] = u1[z].astype(F32) + z_in1[...].astype(F32)
    swap = copy(res.at[1 - k], own.at[k], core)
    own[k] = res[k]
    to_far[3].wait()
    total = d[3, k * 2 + t].astype(F32) + got_core[3, t].astype(F32) + got_far[3].astype(F32)
    swap.wait()
    tile[...] = own[0, :, 0:128] + own[1, :, 0:128]
    c_tile = copy(tile, tile_out, far)
    for i in range(6):
        home[i].wait()
        total = total + got_ring[i].astype(F32)
    out[...] = total
    c_tile.wait()


def return_all(d, g, u0, u1):
    return comm_call(
        return_kernel,
        [
            jax.ShapeDtypeStruct((128, 768), F32),
            jax.ShapeDtypeStruct((2, 16, 2304), F32),
            jax.ShapeDtypeStruct((16, 128), F32),
        ],
        [
            pltpu.VMEM((7, 2, 128, 768), BF),
            pltpu.VMEM((7, 128, 768), BF),
            pltpu.VMEM((7, 128, 768), BF),
            pltpu.VMEM((6, 128, 768), BF),
            pltpu.VMEM((6, 128, 768), BF),
        ]
        + [pltpu.VMEM((3, 2, 4, 2, 16, 384), BF)] * 2
        + [pltpu.VMEM((2, 4, 2, 16, 384), BF)] * 2
        + [pltpu.VMEM((3, 2, 2, 16, 384), BF)] * 2
        + [pltpu.VMEM((2, 2, 16, 384), BF)] * 2
        + [pltpu.VMEM((2, 16, 768), BF)] * 2
        + [pltpu.VMEM((2, 16, 384), BF)] * 2
        + [pltpu.VMEM((2, 16, 2304), F32), pltpu.VMEM((16, 128), F32), DMA((38,)), DMA((38,))],
        5,
        "return_all",
        (d, g, u0, u1),
    )


def layout_tables():
    d = np.arange(768)
    n64 = np.arange(64)[:, None]
    own = (d // 12 == n64).astype(np.float32)
    lane = d % 128
    high = d < 384
    column = np.where(high, lane - 64, lane)
    heads = ((column == n64) & (column >= 0) & (column < 64)).astype(np.float32)
    hidden = ((d % 256) // 4 == n64).astype(np.float32)
    spread = np.stack([own, heads, hidden])
    spot = 64 * ((d % 12) // 6) + d % 6
    head = (d % 384) // 128
    rows = [spot + 6 * p for p in range(6)]
    rows.append(np.where(high, 6, 0) + head)
    rows.append(12 + (d // 256) * 4 + d % 4)
    step = np.zeros((8, 768), np.int32)
    step[6], step[7] = 3, 12
    back = [12 * p + d % 12 for p in range(6)]
    back.append(72 + np.where(high, 3, 0) + head)
    back.append(78 + (d // 256) * 4 + d % 4)
    select = np.arange(512)[None, :] == (np.arange(384) // 12 * 16 + np.arange(384) % 12)[:, None]
    row12 = np.arange(512)[:, None] == np.arange(32)[None, :] * 16 + 12
    return (
        spread,
        np.stack(rows).astype(np.int32),
        step,
        np.stack(back).astype(np.int32),
        select.astype(np.float32),
        row12.astype(np.float32),
    )


SPREAD, FETCH, FETCH_STEP, PUT, SELECT, ROW12 = layout_tables()


def matmul(left, right):
    return jnp.dot(left, right, preferred_element_type=F32)


def matmul_nt(left, right):
    return lax.dot_general(left, right, NT, preferred_element_type=F32)


def matmul_tn(left, right):
    return lax.dot_general(left, right, TN, preferred_element_type=F32)


def allowed_pairs(lim, clip, qb, j):
    cols = pl.ds(qb * 256, 256)
    pos = lim[4] + j * 256 + lax.broadcasted_iota(jnp.int32, (256, 256), 0)
    return (pos >= clip[0:1, cols]) & (pos < clip[1:2, cols])


def front_kernel(
    lim, clip, w, row12, row13, spread, fetch, select, tk,
    vecs, w_attn, unit, kv, q, of, lse, attn,
):
    line = lax.broadcasted_iota(jnp.int32, (128, 768), 0)
    wide = matmul_tn(row12[...], spread[0])
    for p in range(6):
        hit = line == fetch[p : p + 1, :]
        vecs[p : p + 1, :] = jnp.sum(jnp.where(hit, wide, 0.0), axis=0, keepdims=True)
    for p in (6, 7):
        wide = matmul_tn(row13[...], spread[p - 5])
        hit = line == fetch[p : p + 1, :]
        vecs[p : p + 1, :] = jnp.sum(jnp.where(hit, wide, 0.0), axis=0, keepdims=True)
    for z in range(2):
        w_attn[z * 384 : z * 384 + 384, :] = matmul(select[...], w[z]).astype(BF)

    def norm_rows(j):
        v = tk[j].astype(F32)
        centred = v - jnp.mean(v, axis=-1, keepdims=True)
        spread_out = jnp.mean(centred * centred, axis=-1, keepdims=True)
        u = centred * lax.rsqrt(spread_out + EPS)
        return u, (u * vecs[0:1, :] + vecs[2:3, :]).astype(BF)

    @pl.loop(lim[0], lim[3])
    def _(j):
        u, a = norm_rows(j)
        unit[j] = u.astype(BF)
        kv[j] = (matmul(a, w_attn[:, 0:384]) + vecs[6:7, 0:384]).astype(BF)

    low = (lax.broadcasted_iota(jnp.int32, (256, 384), 1) & 127) < 64
    for qb in range(2):
        _, a = norm_rows(6 + qb)
        v = (matmul(a, w_attn[:, 384:768]) + vecs[6:7, 384:768]).astype(BF).astype(F32)
        q[qb * 256 : qb * 256 + 256, :] = jnp.where(low, v * SCORE_SCALE, 0.0).astype(BF)

    lane = lax.broadcasted_iota(jnp.int32, (256, 128), 1)
    for qb in range(2):
        rows = slice(qb * 256, qb * 256 + 256)

        def step(j, carry):
            ok = allowed_pairs(lim, clip, qb, j)
            new = []
            for h in range(3):
                m, l, acc = carry[h]
                cols = slice(h * 128, h * 128 + 128)
                keys = kv[j, :, cols]
                s = jnp.where(ok, matmul_nt(keys, q[rows, cols]), NEGATIVE)
                top = jnp.maximum(m, jnp.max(s, axis=0, keepdims=True))
                p = jnp.exp(s - top)
                fade = jnp.exp(m - top)
                l = l * fade + jnp.sum(p, axis=0, keepdims=True)
                acc = acc * fade + matmul_tn(keys, p.astype(BF))
                new.append((top, l, acc))
            return tuple(new)

        start = tuple(
            (
                jnp.full((1, 256), NEGATIVE, F32),
                jnp.zeros((1, 256), F32),
                jnp.zeros((128, 256), F32),
            )
            for _ in range(3)
        )
        final = lax.fori_loop(lim[2 * qb], lim[2 * qb + 1], step, start)
        for h in range(3):
            m, l, acc = final[h]
            o = (acc / l).T
            of[rows, h * 128 : h * 128 + 128] = jnp.where(lane >= 64, o, 0.0)
            lse[h : h + 1, rows] = m + jnp.log(l)
        attn[rows, :] = matmul_nt(of[rows, :].astype(BF), w_attn[:, 384:768]).astype(BF)


def front(lim, clip, w, row12, row13, spread, fetch, select, tk):
    return pl.pallas_call(
        front_kernel,
        out_shape=[
            jax.ShapeDtypeStruct((8, 768), F32),
            jax.ShapeDtypeStruct((768, 768), BF),
            jax.ShapeDtypeStruct((14, 256, 768), BF),
            jax.ShapeDtypeStruct((14, 256, 384), BF),
            jax.ShapeDtypeStruct((512, 384), BF),
            jax.ShapeDtypeStruct((512, 384), F32),
            jax.ShapeDtypeStruct((3, 512), F32),
            jax.ShapeDtypeStruct((512, 768), BF),
        ],
        in_specs=[SM] + [VM] * 8,
        out_specs=[VM] * 8,
        compiler_params=pltpu.CompilerParams(vmem_limit_bytes=LIMIT),
        name="front",
    )(lim, clip, w, row12, row13, spread, fetch, select, tk)


def back_kernel(
    lim, clip, q, dr, of, kv, lse, unit, w_attn, vecs, sums, up_sum, spread, put, select, row12,
    d_out, grad, total, dox, delta, dq, ug,
):
    lane = lax.broadcasted_iota(jnp.int32, (256, 128), 1)
    high = (lax.broadcasted_iota(jnp.int32, (256, 384), 1) & 127) >= 64

    @pl.loop(0, 14)
    def _(j):
        total[j] = jnp.zeros((256, 384), F32)
        d_out[j] = jnp.zeros((256, 768), BF)

    for qb in range(2):
        rows = slice(qb * 256, qb * 256 + 256)
        g = jnp.where(high, matmul(dr[rows, :], w_attn[:, 384:768]), 0.0).astype(BF)
        dox[rows, :] = g
        prod = g.astype(F32) * of[rows, :]
        for h in range(3):
            part = prod[:, h * 128 : h * 128 + 128].T
            delta[h : h + 1, rows] = jnp.sum(part, axis=0, keepdims=True)

    for qb in range(2):
        rows = slice(qb * 256, qb * 256 + 256)

        def step(j, carry):
            ok = allowed_pairs(lim, clip, qb, j)
            new = []
            for h in range(3):
                cols = slice(h * 128, h * 128 + 128)
                keys = kv[j, :, cols]
                qh, dh = q[rows, cols], dox[rows, cols]
                s = jnp.where(ok, matmul_nt(keys, qh), NEGATIVE)
                p = jnp.exp(s - lse[h : h + 1, rows])
                ds = (p * (matmul_nt(keys, dh) - delta[h : h + 1, rows])).astype(BF)
                new.append(carry[h] + matmul_tn(keys, ds))
                total[j, :, cols] += matmul(ds, qh) + matmul(p.astype(BF), dh)
            return tuple(new)

        start = tuple(jnp.zeros((128, 256), F32) for _ in range(3))
        final = lax.fori_loop(lim[2 * qb], lim[2 * qb + 1], step, start)
        for h in range(3):
            part = jnp.where(lane < 64, SCORE_SCALE * final[h].T, 0.0)
            dq[rows, h * 128 : h * 128 + 128] = part.astype(BF)

    ug[...] = jnp.zeros((768, 768), F32)

    def chunk(j, kv_sum):
        z = total[j].astype(BF)
        d_out[j] = matmul_nt(z, w_attn[:, 0:384]).astype(BF)
        ug[:, 0:384] += matmul_tn(unit[j], z)
        return kv_sum + jnp.sum(z.astype(F32), axis=0, keepdims=True)

    kv_sum = lax.fori_loop(lim[0], lim[3], chunk, jnp.zeros((1, 384), F32))
    for qb in range(2):
        rows = slice(qb * 256, qb * 256 + 256)
        own = matmul_nt(total[6 + qb].astype(BF), w_attn[:, 0:384])
        d_out[6 + qb] = (own + matmul_nt(dq[rows, :], w_attn[:, 384:768])).astype(BF)
        ug[:, 384:768] += matmul_tn(unit[6 + qb], dq[rows, :])
    q_sum = jnp.sum(dq[...].astype(F32), axis=0, keepdims=True)
    z_sum = jnp.concatenate([kv_sum, q_sum], axis=1)

    line = lax.broadcasted_iota(jnp.int32, (128, 768), 0)

    def place(p, row):
        return jnp.where(line == put[p : p + 1, :], row, 0.0)

    columns = vecs[...].T
    gain_col, offset_col = columns[:, 0:1], columns[:, 2:3]
    w_full = w_attn[...].astype(F32)
    gain_sum = jnp.sum(ug[...] * w_full, axis=1, keepdims=True)
    offset_sum = jnp.sum(w_full * z_sum, axis=1, keepdims=True)
    flip = lax.broadcasted_iota(jnp.int32, (768, 128), 1)
    both = jnp.where(flip == 0, gain_sum, jnp.where(flip == 1, offset_sum, 0.0)).T
    own = place(0, both[0:1, :]) + place(2, both[1:2, :])
    for i, p in enumerate((1, 3, 4, 5)):
        own = own + place(p, sums[i : i + 1, :])
    small = matmul_nt(spread[0], own.astype(BF))
    small += matmul_nt(spread[1], place(6, z_sum).astype(BF))
    small += matmul_nt(spread[2], place(7, up_sum[...]).astype(BF))
    small = small.astype(BF)

    ug[...] = ug[...] * gain_col + offset_col * z_sum
    ug[:, 384:768] += matmul_tn(dr[...], of[...].astype(BF))
    for i in range(2):
        g = matmul_tn(select[...], ug[i * 384 : i * 384 + 384, :].astype(BF))
        grad[i] = g.astype(BF)
        extra = matmul(row12[...], small[i * 32 : i * 32 + 32, :])
        grad[i, :, 0:128] = (g[:, 0:128] + extra).astype(BF)


def back(lim, *args):
    return pl.pallas_call(
        back_kernel,
        out_shape=[
            jax.ShapeDtypeStruct((14, 256, 768), BF),
            jax.ShapeDtypeStruct((2, 512, 768), BF),
        ],
        in_specs=[SM] + [VM] * len(args),
        out_specs=[VM, VM],
        scratch_shapes=[
            pltpu.VMEM((14, 256, 384), F32),
            pltpu.VMEM((512, 384), BF),
            pltpu.VMEM((3, 512), F32),
            pltpu.VMEM((512, 384), BF),
            pltpu.VMEM((768, 768), F32),
        ],
        compiler_params=pltpu.CompilerParams(vmem_limit_bytes=LIMIT),
        name="back",
    )(lim, *args)


def normalize(hidden, gain, offset):
    average = jnp.mean(hidden, axis=-1, keepdims=True)
    centred = hidden - average
    spread = jnp.mean(centred * centred, axis=-1, keepdims=True)
    scale = lax.rsqrt(spread + EPS)
    unit = centred * scale
    return unit * gain + offset, unit, scale


def normalize_back(grad_out, unit, scale, gain):
    grad_unit = grad_out * gain
    first = jnp.mean(grad_unit, axis=-1, keepdims=True)
    second = jnp.mean(grad_unit * unit, axis=-1, keepdims=True)
    return scale * (grad_unit - first - unit * second)


def body(
    tokens,
    clip_bounds,
    attn_in,
    qv_bias,
    out_proj,
    fc_in,
    fc_bias,
    fc_out,
    ln_gain,
    row_bias,
    cotangent,
):
    dp = lax.axis_index("dp")
    c, k, t = dp // 2, dp % 2, lax.axis_index("tensor")
    spread, select, row12 = jnp.asarray(SPREAD, BF), jnp.asarray(SELECT, BF), jnp.asarray(ROW12, BF)
    put = jnp.asarray(PUT)
    fetch = jnp.asarray(FETCH) + k * jnp.asarray(FETCH_STEP)

    parts = attn_in[0].reshape(3, 12, 6, 64)
    proj = out_proj[0].T.reshape(12, 6, 64)
    kv_w = jnp.stack([parts[1], parts[2]], axis=2).reshape(12, 2, 384)
    qo_w = jnp.stack([parts[0], proj], axis=2).reshape(12, 2, 384)
    up_w = fc_in[0].reshape(12, 2, 768)
    down_w = fc_out[0].T.reshape(12, 2, 768)
    pay = jnp.concatenate([kv_w, qo_w, up_w, down_w], axis=-1).transpose(1, 0, 2)
    norms = jnp.concatenate([ln_gain.reshape(1, 12), row_bias.reshape(1, 24)], axis=1)
    blank = jnp.zeros((1, 64), BF)
    norms = jnp.pad(norms, ((0, 0), (0, 28)))
    norms = jnp.where(
        t == 0,
        jnp.concatenate([norms, blank], axis=1),
        jnp.concatenate([blank, norms], axis=1),
    )
    others = jnp.concatenate([qv_bias.reshape(1, 12), fc_bias.reshape(1, 24)], axis=1)
    others = jnp.pad(others, ((0, 0), (0, 92)))
    extra = jnp.pad(jnp.concatenate([norms, others]), ((0, 2), (0, 2176)))[None]
    pay = jnp.concatenate([pay, jnp.concatenate([extra, extra])], axis=1)
    tile = jnp.pad(norms, ((12, 3), (0, 0)))
    w, f0, f1, clip, near_tokens = gather_all(pay, tile, clip_bounds, tokens)
    clip = clip.transpose(1, 0, 2).reshape(2, 512)
    rows = w.reshape(64, 16, 768)[:, 12:14, 0:128]
    base = (c - 3) * 512
    lim = jnp.stack(
        [
            (clip[0, 0] - base) // 256,
            (clip[1, 255] - base + 255) // 256,
            (clip[0, 256] - base) // 256,
            (clip[1, 511] - base + 255) // 256,
            base,
        ]
    ).astype(jnp.int32)
    vecs, w_attn, unit, near, query, mixed, lse, attn = front(
        lim,
        clip,
        w.reshape(2, 512, 768),
        rows[:, 0],
        rows[:, 1],
        spread,
        fetch,
        select,
        near_tokens.reshape(14, 256, 768),
    )
    output, grad_hidden_one, full_attn, sums, up_sum, u0, u1 = mid(
        attn.reshape(4, 128, 768), f0, f1, cotangent, tokens, vecs, select
    )
    near_back, grad_w = back(
        lim,
        clip,
        query,
        full_attn.reshape(512, 768),
        mixed,
        near,
        lse,
        unit,
        w_attn,
        vecs,
        sums,
        up_sum,
        spread,
        put,
        select,
        row12,
    )
    back_one, own, far = return_all(
        near_back.reshape(7, 4, 128, 768), grad_w.reshape(2, 4, 4, 2, 16, 768), u0, u1
    )
    _, unit_one, scale_one = normalize(tokens.astype(F32), vecs[0], vecs[2])
    grad_tokens = grad_hidden_one + normalize_back(back_one, unit_one, scale_one, vecs[0])
    vec = own[0, 12, 0:128] + own[1, 12, 0:128] + far[12]
    vec = vec[0:72].reshape(6, 2, 6)
    vec = jnp.where(t == 0, vec[:, 0], vec[:, 1])
    grad_gain, grad_row = vec[0:2].reshape(1, 2, 6), vec[2:6].reshape(1, 4, 6)
    grad_qv = own[:, 12, 72:78].reshape(2, 2, 3).transpose(1, 0, 2).reshape(1, 2, 6, 1)
    grad_up_bias = own[:, 12, 78:90].reshape(1, 6, 4)
    main = own[:, 0:12].transpose(1, 0, 2)
    g_kv = main[:, :, 0:384].reshape(12, 6, 2, 64)
    g_qo = main[:, :, 384:768].reshape(12, 6, 2, 64)
    grad_in = jnp.stack(
        [
            g_qo[:, :, 0].reshape(12, 384),
            g_kv[:, :, 0].reshape(12, 384),
            g_kv[:, :, 1].reshape(12, 384),
        ]
    )[None]
    grad_out = g_qo[:, :, 1].reshape(12, 384).T[None]
    grad_fc_in = main[:, :, 768:1536].reshape(1, 12, 1536)
    grad_fc_out = main[:, :, 1536:2304].reshape(12, 1536).T[None]
    return (
        output,
        grad_tokens,
        grad_in,
        grad_qv,
        grad_out,
        grad_fc_in,
        grad_up_bias,
        grad_fc_out,
        grad_gain,
        grad_row,
    )


def solution(mesh):
    return jax.shard_map(
        body,
        mesh=mesh,
        in_specs=(
            P(("dp", "tensor"), None),
            P(None, "dp"),
            P(None, None, "dp", "tensor"),
            P(None, None, "tensor", "dp"),
            P(None, "tensor", "dp"),
            P(None, "dp", "tensor"),
            P(None, "tensor", "dp"),
            P(None, "tensor", "dp"),
            P(None, None, ("dp", "tensor")),
            P(None, None, ("dp", "tensor")),
            P(("dp", "tensor"), None),
        ),
        out_specs=(
            P(("dp", "tensor"), None),
            P(("dp", "tensor"), None),
            P(None, None, "dp", "tensor"),
            P(None, None, "tensor", "dp"),
            P(None, "tensor", "dp"),
            P(None, "dp", "tensor"),
            P(None, "tensor", "dp"),
            P(None, "tensor", "dp"),
            P(None, None, ("dp", "tensor")),
            P(None, None, ("dp", "tensor")),
        ),
        check_vma=False,
    )
```

```python
import jax
import jax.numpy as jnp
import numpy as np
from jax import lax
import jax.experimental.pallas as pl
import jax.experimental.pallas.tpu as pltpu
from jax.sharding import PartitionSpec as P

EPS = 1e-05
NEGATIVE = -1e30
SCORE_SCALE = 0.125
BF = jnp.bfloat16
F32 = jnp.float32
MESH = pl.DeviceIdType.MESH
VM = pl.BlockSpec(memory_space=pltpu.VMEM)
SM = pl.BlockSpec(memory_space=pltpu.SMEM)
DMA = pltpu.SemaphoreType.DMA
LIMIT = 56 * 2**20
NT = (((1,), (1,)), ((), ()))
TN = (((0,), (0,)), ((), ()))


def coords():
    dp = lax.axis_index("dp")
    return dp // 32, (dp // 8) % 4, (dp // 2) % 4, dp % 2, lax.axis_index("tensor")


def device(z, y, x, k, t):
    return (((z * 4 + y) * 4 + x) * 2 + k, t)


def chip(c, k, t):
    return (c * 2 + k, t)


def greet(peers):
    bar = pltpu.get_barrier_semaphore()
    for peer in peers:
        pl.semaphore_signal(bar, inc=1, device_id=peer, device_id_type=MESH)
    pl.semaphore_wait(bar, len(peers))


def remote(src, dst, sems, index, peer):
    send, recv = sems
    return pltpu.make_async_remote_copy(
        src, dst, send.at[index], recv.at[index], device_id=peer, device_id_type=MESH
    )


def comm_call(kernel, out_shape, scratch, cid, name, args):
    single = not isinstance(out_shape, (list, tuple))
    return pl.pallas_call(
        kernel,
        out_shape=out_shape,
        in_specs=[VM] * len(args),
        out_specs=VM if single else [VM] * len(out_shape),
        scratch_shapes=scratch,
        compiler_params=pltpu.CompilerParams(
            collective_id=cid, has_side_effects=True, vmem_limit_bytes=LIMIT
        ),
        name=name,
    )(*args)


def spots():
    z, y, x, k, t = coords()
    xs = [device(z, y, (x + d) % 4, k, t) for d in (1, 2, 3)]
    ys = [device(z, (y + d) % 4, x, k, t) for d in (1, 2, 3)]
    core = device(z, y, x, 1 - k, t)
    far = device(z, y, x, k, 1 - t)
    low = device(1 - z, y, x, k, t)
    ring = [chip(((z * 4 + y) * 4 + x + d) % 32, k, t) for d in RING]
    return (z, y, x, k, t), xs, ys, core, far, low, ring


RING = (2, -2, 3, -3, 1, -1)


class Copies:
    def __init__(self, send, recv):
        self.sems, self.count = (send, recv), 0

    def __call__(self, src, dst, peer):
        made = remote(src, dst, self.sems, self.count, peer)
        self.count += 1
        made.start()
        return made


def build_rows(attn_w, proj, up, down, gain, row, qv, fc, pads, place, masks, t, pay, tile):
    def tall(v):
        return matmul(pads[...], v)

    query, keys, values = [tall(attn_w[i]) for i in range(3)]
    mixed, up_rows, down_rows = tall(proj[...]), tall(up[...]), tall(down[...])
    norms = jnp.sum(matmul(gain[...], place[0:6, :]) * masks[0:2, :], axis=0, keepdims=True)
    norms += jnp.sum(matmul(row[...], place[0:6, :]) * masks[2:6, :], axis=0, keepdims=True)
    lane = lax.broadcasted_iota(jnp.int32, (16, 128), 1)
    line = lax.broadcasted_iota(jnp.int32, (16, 128), 0)
    others = jnp.sum(matmul(qv[...], place[0:6, :]) * masks[6:8, :], axis=0, keepdims=True)
    others += jnp.sum(matmul(fc[...], place[8:14, :]) * masks[8:12, :], axis=0, keepdims=True)
    mine = (line == 12) & (lane >= 64 * t) & (lane < 64 * t + 64)
    small = jnp.where(mine, norms, 0.0)
    tile[...] = small.astype(BF)
    small = small + jnp.where(line == 13, others, 0.0)
    for q in range(2):
        for h in range(3):
            n = slice((q * 3 + h) * 64, (q * 3 + h) * 64 + 64)
            first = jnp.concatenate([keys[:, n], values[:, n]], axis=1)
            if h == 0:
                first = first + small
            pay[q, :, h * 128 : h * 128 + 128] = first.astype(BF)
            second = jnp.concatenate([query[:, n], mixed[:, n]], axis=1)
            pay[q, :, 384 + h * 128 : 512 + h * 128] = second.astype(BF)
        pay[q, :, 768:1536] = up_rows[:, q * 768 : q * 768 + 768].astype(BF)
        pay[q, :, 1536:2304] = down_rows[:, q * 768 : q * 768 + 768].astype(BF)


H0, H1 = pl.ds(0, 512), pl.ds(512, 256)


def gather_kernel(
    clip, tok, attn_w, proj, up, down, gain, row, qv, fc, pads, place, masks,
    w, f0, f1, clip_out, tk, pay_s, tile, tile_in, ws, send, recv,
):
    (z, y, x, k, t), xs, ys, core, far, low, ring = spots()
    copy = Copies(send, recv)
    mine, other = k * 2 + t, k * 2 + 1 - t
    greet(xs + ys + [core, far, low] + ring)
    own_far = copy(tok, tk.at[3, mine], far)
    order = (4, 5, 2, 3, 0, 1)
    pushes = {i: copy(tok, tk.at[3 - RING[i], mine], ring[i]) for i in order}
    done = [copy(tok, tk.at[3, mine], core), copy(clip, clip_out.at[k], core)]
    build_rows(attn_w, proj, up, down, gain, row, qv, fc, pads, place, masks, t, pay_s, tile)
    c_tile = copy(tile, tile_in, far)
    clip_out[k] = clip[...]
    tk[3, mine] = tok[...]
    to_far = {}

    def pass_on(i):
        pushes[i].wait_recv()
        a = tk.at[3 - RING[i], mine]
        to_far[i] = copy(a, a, far)
        done.append(copy(a, a, core))

    c_tile.wait()
    for q in range(2):
        pay_s[q, :, 0:128] = pay_s[q, :, 0:128] + tile_in[...]
    swap = copy(pay_s.at[1 - k], ws.at[z, k], core)
    ws[z, k] = pay_s[k]
    swap.wait()
    c_low = copy(ws.at[z], ws.at[z], low)
    pass_on(4)
    pass_on(5)
    c_low.wait()
    w[:, y, x] = ws[:, :, :, 0:768]
    f0[:, x] = ws[:, :, :, 768:1536]
    f1[:, y] = ws[:, :, :, 1536:2304]
    phase = []
    for i in range(3):
        phase.append(copy(ws.at[:, :, :, H0], w.at[:, y, x, :, :, H0], xs[i]))
        phase.append(copy(ws.at[:, :, :, H1], w.at[:, y, x, :, :, H1], ys[i]))
    pass_on(2)
    pass_on(3)
    for c in phase:
        c.wait()
    rest = []
    for i in range(3):
        a = w.at[:, y, :, :, :, H0]
        rest.append(copy(a, a, ys[i]))
        b = w.at[:, :, x, :, :, H1]
        rest.append(copy(b, b, xs[i]))
    pass_on(0)
    pass_on(1)
    for i in range(3):
        rest.append(copy(ws.at[:, :, :, pl.ds(768, 768)], f0.at[:, x], xs[i]))
        rest.append(copy(ws.at[:, :, :, pl.ds(1536, 768)], f1.at[:, y], ys[i]))
    own_far.wait_recv()
    done.append(copy(tk.at[3, other], tk.at[3, other], core))
    for i in order:
        to_far[i].wait_recv()
        a = tk.at[3 - RING[i], other]
        done.append(copy(a, a, core))
    for i in order:
        pushes[i].wait_send()
        to_far[i].wait_send()
    own_far.wait_send()
    for c in rest + done:
        c.wait()


def gather_all(*args):
    return comm_call(
        gather_kernel,
        [
            jax.ShapeDtypeStruct((2, 4, 4, 2, 16, 768), BF),
            jax.ShapeDtypeStruct((2, 4, 2, 16, 768), BF),
            jax.ShapeDtypeStruct((2, 4, 2, 16, 768), BF),
            jax.ShapeDtypeStruct((2, 2, 256), jnp.int32),
            jax.ShapeDtypeStruct((7, 4, 128, 768), BF),
        ],
        [
            pltpu.VMEM((2, 16, 2304), BF),
            pltpu.VMEM((16, 128), BF),
            pltpu.VMEM((16, 128), BF),
            pltpu.VMEM((2, 2, 16, 2304), BF),
            DMA((50,)),
            DMA((50,)),
        ],
        0,
        "gather_first",
        args,
    )


def exchange_rows(copy, a, out, k, t, core, far):
    mine, other = k * 2 + t, k * 2 + 1 - t
    c_far = copy(a, out.at[mine], far)
    c_core = copy(a, out.at[mine], core)
    out[mine] = a[...]

    def finish():
        c_far.wait_recv()
        c_pass = copy(out.at[other], out.at[other], core)
        c_far.wait_send()
        c_core.wait()
        c_pass.wait()

    return finish


def spread_first(copy, g0, g1, b0, b1, x, y, xs, ys):
    over_y, over_x = [], []
    for i in range(3):
        over_y.append(copy(g0.at[:, (y + i + 1) % 4], b0.at[i], ys[i]))
        over_x.append(copy(g1.at[:, :, (x + i + 1) % 4], b1.at[i], xs[i]))
    return over_y, over_x


def add_first(g0, g1, b0, b1, s0, s1, x, y, over_y, over_x):
    for c in over_y:
        c.wait()

    @pl.loop(0, 8)
    def _(n):
        zz, m = n // 4, n % 4
        v = g0[zz, y, m].astype(F32)
        for i in range(3):
            v = v + b0[i, zz, m].astype(F32)
        s0[zz, m] = v.astype(BF)

    for c in over_x:
        c.wait()

    @pl.loop(0, 8)
    def _(n):
        zz, m = n // 4, n % 4
        v = g1[zz, m, x].astype(F32)
        for i in range(3):
            v = v + b1[i, zz, m].astype(F32)
        s1[zz, m] = v.astype(BF)


def spread_second(copy, s0, s1, a0, a1, x, y, xs, ys):
    over_x, over_y = [], []
    for i in range(3):
        over_x.append(copy(s0.at[:, (x + i + 1) % 4], a0.at[i], xs[i]))
        over_y.append(copy(s1.at[:, (y + i + 1) % 4], a1.at[i], ys[i]))
    return over_x, over_y


def add_second(s0, s1, a0, a1, u0, u1, x, y, over_x, over_y):
    for c in over_x + over_y:
        c.wait()
    for zz in range(2):
        v = s0[zz, x].astype(F32)
        v1 = s1[zz, y].astype(F32)
        for i in range(3):
            v = v + a0[i, zz].astype(F32)
            v1 = v1 + a1[i, zz].astype(F32)
        u0[zz] = v.astype(BF)
        u1[zz] = v1.astype(BF)


def mid_kernel(
    p, f0, f1, cot, tok, vecs, select,
    output, e1, dr_full, sums, up_sum, u0, u1,
    got, mid, got_far, p0, p1, w_up, w_down, b_full, cot_full, dg, active, du_full,
    pr, got_two, mid_two, far_two, dr, g0, g1, b0, b1, s0, s1, a0, a1, send, recv,
):
    (z, y, x, k, t), xs, ys, core, far, low, ring = spots()
    copy = Copies(send, recv)
    greet(xs + ys + [core, far])
    mine, across, beside, both = k * 2 + t, k * 2 + 1 - t, 2 - 2 * k + t, 3 - 2 * k - t
    to_core = copy(p.at[pl.ds((1 - k) * 2, 2)], got, core)
    made = []
    for i in range(2):
        for j in range(3):
            made.append(copy(f0.at[i], p0.at[i, y], ys[j]))
            made.append(copy(f1.at[i], p1.at[i, :, x], xs[j]))
        p0[i, y] = f0[i]
        p1[i, :, x] = f1[i]
    to_core.wait()
    mid[...] = (p[across].astype(F32) + got[1 - t].astype(F32)).astype(BF)
    to_far = copy(mid, got_far, far)
    finish_cot = exchange_rows(copy, cot, cot_full, k, t, core, far)
    part = p[mine].astype(F32) + got[t].astype(F32) + tok[...].astype(F32) + vecs[3:4, :]
    to_far.wait()
    hidden = part + got_far[...].astype(F32)
    centred = hidden - jnp.mean(hidden, axis=-1, keepdims=True)
    scale = lax.rsqrt(jnp.mean(centred * centred, axis=-1, keepdims=True) + EPS)
    unit = centred * scale
    b_full[mine] = (unit * vecs[1:2, :] + vecs[4:5, :]).astype(BF)
    rows_far = copy(b_full.at[mine], b_full.at[mine], far)
    rows_core = copy(b_full.at[mine], b_full.at[mine], core)
    e1[...] = hidden
    finish_cot()
    for c in made:
        c.wait()
    for i in range(2):
        rows = slice(i * 384, i * 384 + 384)
        w_up[rows, :] = matmul(select[...], p0[i].reshape(512, 768)).astype(BF)
        w_down[rows, :] = matmul(select[...], p1[i].reshape(512, 768)).astype(BF)

    @pl.loop(0, 4)
    def _(i):
        dg[i] = matmul(cot_full[i], w_down[...])

    up_sum[...] = jnp.zeros((1, 768), F32)

    def feed(i):
        u = matmul(b_full[i], w_up[...]) + vecs[7:8, :]
        phi = 0.5 + 0.5 * lax.erf(u * 0.7071067811865476)
        gl = (u * phi).astype(BF)
        active[i] = gl
        pr[0, i] = matmul_nt(gl, w_down[...]).astype(BF)
        slope = phi + u * jnp.exp(-0.5 * u * u) * 0.3989422804014327
        du = (dg[i] * slope).astype(BF)
        du_full[i] = du
        up_sum[...] += jnp.sum(du.astype(F32), axis=0, keepdims=True)
        pr[1, i] = matmul_nt(du, w_up[...]).astype(BF)

    feed(mine)
    rows_core.wait()
    feed(beside)
    first = copy(pr.at[:, beside], got_two.at[:, t], core)
    rows_far.wait()
    rows_pass = copy(b_full.at[across], b_full.at[across], core)
    feed(across)
    rows_pass.wait()
    feed(both)
    second = copy(pr.at[:, both], got_two.at[:, 1 - t], core)
    second.wait()
    two = []
    for i in range(2):
        v = pr[i, across].astype(F32) + got_two[i, 1 - t].astype(F32)
        mid_two[i] = v.astype(BF)
        two.append(copy(mid_two.at[i], far_two.at[i], far))
    b_rows, du_rows = b_full[...].reshape(512, 768), du_full[...].reshape(512, 768)
    for i in range(2):
        cols = slice(i * 384, i * 384 + 384)
        g = matmul_tn(b_rows[:, cols], du_rows).astype(BF)
        g0[i] = matmul_tn(select[...], g).astype(BF).reshape(4, 4, 2, 16, 768)
    c_rows, a_rows = cot_full[...].reshape(512, 768), active[...].reshape(512, 768)
    for i in range(2):
        cols = slice(i * 384, i * 384 + 384)
        g = matmul_tn(c_rows[:, cols], a_rows).astype(BF)
        g1[i] = matmul_tn(select[...], g).astype(BF).reshape(4, 4, 2, 16, 768)
    over = spread_first(copy, g0, g1, b0, b1, x, y, xs, ys)
    first.wait()
    pair = []
    for i in range(2):
        v = pr[i, mine].astype(F32) + got_two[i, t].astype(F32)
        two[i].wait()
        pair.append(v + far_two[i].astype(F32))
    hidden = e1[...]
    output[...] = (hidden + pair[0] + vecs[5:6, :]).astype(BF)
    centred = hidden - jnp.mean(hidden, axis=-1, keepdims=True)
    scale = lax.rsqrt(jnp.mean(centred * centred, axis=-1, keepdims=True) + EPS)
    unit = centred * scale
    w = pair[1] * vecs[1:2, :]
    mean_w = jnp.mean(w, axis=-1, keepdims=True)
    mean_wu = jnp.mean(w * unit, axis=-1, keepdims=True)
    cot_f = cot[...].astype(F32)
    grad = cot_f + scale * (w - mean_w - unit * mean_wu)
    e1[...] = grad
    low_grad = grad.astype(BF)
    dr[...] = low_grad
    finish_rows = exchange_rows(copy, dr, dr_full, k, t, core, far)
    sums[0:1, :] = jnp.sum(pair[1] * unit, axis=0, keepdims=True)
    sums[1:2, :] = jnp.sum(low_grad.astype(F32), axis=0, keepdims=True)
    sums[2:3, :] = jnp.sum(pair[1], axis=0, keepdims=True)
    sums[3:4, :] = jnp.sum(cot_f, axis=0, keepdims=True)
    add_first(g0, g1, b0, b1, s0, s1, x, y, *over)
    over = spread_second(copy, s0, s1, a0, a1, x, y, xs, ys)
    finish_rows()
    add_second(s0, s1, a0, a1, u0, u1, x, y, *over)


def mid(p, f0, f1, cot, tok, vecs, select):
    rows = pltpu.VMEM((128, 768), BF)
    two = pltpu.VMEM((2, 128, 768), BF)
    four = pltpu.VMEM((4, 128, 768), BF)
    square = pltpu.VMEM((768, 768), BF)
    piece = pltpu.VMEM((2, 4, 4, 2, 16, 768), BF)
    return comm_call(
        mid_kernel,
        [
            jax.ShapeDtypeStruct((128, 768), BF),
            jax.ShapeDtypeStruct((128, 768), F32),
            jax.ShapeDtypeStruct((4, 128, 768), BF),
            jax.ShapeDtypeStruct((4, 768), F32),
            jax.ShapeDtypeStruct((1, 768), F32),
            jax.ShapeDtypeStruct((2, 2, 16, 768), BF),
            jax.ShapeDtypeStruct((2, 2, 16, 768), BF),
        ],
        [two, rows, rows, piece, piece, square, square, four, four]
        + [pltpu.VMEM((4, 128, 768), F32), four, four]
        + [pltpu.VMEM((2, 4, 128, 768), BF), pltpu.VMEM((2, 2, 128, 768), BF), two, two, rows]
        + [piece, piece]
        + [pltpu.VMEM((3, 2, 4, 2, 16, 768), BF)] * 2
        + [pltpu.VMEM((2, 4, 2, 16, 768), BF)] * 2
        + [pltpu.VMEM((3, 2, 2, 16, 768), BF)] * 2
        + [DMA((39,)), DMA((39,))],
        1,
        "mid",
        (p, f0, f1, cot, tok, vecs, select),
    )


def return_kernel(
    d, g, u0, u1, out, own, tile_out,
    got_core, v1, in1, e_send, got_far, r_send, got_ring,
    b0, b1, s0, s1, a0, a1, v_0, v_1, z_in0, z_in1, z_in2, z_in3, res, tile, send, recv,
):
    (z, y, x, k, t), xs, ys, core, far, low, ring = spots()
    copy = Copies(send, recv)
    greet(xs + ys + [core, far, low] + ring)
    mine, across = k * 2 + t, k * 2 + 1 - t
    near = (ring[4], ring[5])
    order = (4, 2, 5, 1, 6, 0, 3)
    to_core = {j: copy(d.at[j, pl.ds((1 - k) * 2, 2)], got_core.at[j], core) for j in order}
    g0, g1 = g.at[:, :, :, :, :, H0], g.at[:, :, :, :, :, H1]
    fc_z = [copy(u0.at[1 - z], z_in0, low), copy(u1.at[1 - z], z_in1, low)]
    hop1, to_far = [], []
    over = spread_first(copy, g0, g1, b0, b1, x, y, xs, ys)
    for i, j in enumerate((4, 2)):
        to_core[j].wait()
        v1[i] = (d[j, pl.ds(k * 2, 2)].astype(F32) + got_core[j].astype(F32)).astype(BF)
        hop1.append(copy(v1.at[i], in1.at[i], near[i]))
    for i, j in enumerate(order[2:6]):
        to_core[j].wait()
        e_send[i] = (d[j, across].astype(F32) + got_core[j, 1 - t].astype(F32)).astype(BF)
        to_far.append(copy(e_send.at[i], got_far.at[i], far))
    home = []

    def send_home(i):
        j = order[2 + i]
        to_far[i].wait()
        v = d[j, mine].astype(F32) + got_core[j, t].astype(F32) + got_far[i].astype(F32)
        r_send[i] = v.astype(BF)
        home.append(copy(r_send.at[i], got_ring.at[i], ring[i]))

    send_home(0)
    send_home(1)
    add_first(g0, g1, b0, b1, s0, s1, x, y, *over)
    over = spread_second(copy, s0, s1, a0, a1, x, y, xs, ys)
    to_core[3].wait()
    hop1[0].wait()
    hop1[1].wait()
    v = d[3, across].astype(F32) + got_core[3, 1 - t].astype(F32)
    v = v + in1[0, 1 - t].astype(F32) + in1[1, 1 - t].astype(F32)
    e_send[4] = v.astype(BF)
    last = copy(e_send.at[4], got_far.at[4], far)
    send_home(2)
    send_home(3)
    add_second(s0, s1, a0, a1, v_0, v_1, x, y, *over)
    attn_z = [copy(v_0.at[1 - z], z_in2, low), copy(v_1.at[1 - z], z_in3, low)]
    for c in fc_z:
        c.wait()
    res[:, :, 768:1536] = u0[z].astype(F32) + z_in0[...].astype(F32)
    res[:, :, 1536:2304] = u1[z].astype(F32) + z_in1[...].astype(F32)
    for c in attn_z:
        c.wait()
    res[:, :, H0] = v_0[z].astype(F32) + z_in2[...].astype(F32)
    res[:, :, H1] = v_1[z].astype(F32) + z_in3[...].astype(F32)
    swap = copy(res.at[1 - k], own.at[k], core)
    own[k] = res[k]
    total = d[3, mine].astype(F32) + got_core[3, t].astype(F32)
    total = total + in1[0, t].astype(F32) + in1[1, t].astype(F32)
    swap.wait()
    tile[...] = own[0, :, 0:128] + own[1, :, 0:128]
    c_tile = copy(tile, tile_out, far)
    for i in range(4):
        home[i].wait()
        total = total + got_ring[i].astype(F32)
    last.wait()
    out[...] = total + got_far[4].astype(F32)
    c_tile.wait()


def return_all(d, g, u0, u1):
    two = pltpu.VMEM((2, 2, 128, 768), BF)
    wide, slim = 512, 256
    return comm_call(
        return_kernel,
        [
            jax.ShapeDtypeStruct((128, 768), F32),
            jax.ShapeDtypeStruct((2, 16, 2304), F32),
            jax.ShapeDtypeStruct((16, 128), F32),
        ],
        [pltpu.VMEM((7, 2, 128, 768), BF), two, two]
        + [pltpu.VMEM((5, 128, 768), BF)] * 2
        + [pltpu.VMEM((4, 128, 768), BF)] * 2
        + [pltpu.VMEM((3, 2, 4, 2, 16, n), BF) for n in (wide, slim)]
        + [pltpu.VMEM((2, 4, 2, 16, n), BF) for n in (wide, slim)]
        + [pltpu.VMEM((3, 2, 2, 16, n), BF) for n in (wide, slim)]
        + [pltpu.VMEM((2, 2, 16, n), BF) for n in (wide, slim)]
        + [pltpu.VMEM((2, 16, n), BF) for n in (768, 768, wide, slim)]
        + [pltpu.VMEM((2, 16, 2304), F32), pltpu.VMEM((16, 128), F32), DMA((36,)), DMA((36,))],
        5,
        "return_all",
        (d, g, u0, u1),
    )


def layout_tables():
    d = np.arange(768)
    n64 = np.arange(64)[:, None]
    own = (d // 12 == n64).astype(np.float32)
    lane = d % 128
    high = d < 384
    column = np.where(high, lane - 64, lane)
    heads = ((column == n64) & (column >= 0) & (column < 64)).astype(np.float32)
    hidden = ((d % 256) // 4 == n64).astype(np.float32)
    spread = np.stack([own, heads, hidden])
    spot = 64 * ((d % 12) // 6) + d % 6
    head = (d % 384) // 128
    rows = [spot + 6 * p for p in range(6)]
    rows.append(np.where(high, 6, 0) + head)
    rows.append(12 + (d // 256) * 4 + d % 4)
    step = np.zeros((8, 768), np.int32)
    step[6], step[7] = 3, 12
    back = [12 * p + d % 12 for p in range(6)]
    back.append(72 + np.where(high, 3, 0) + head)
    back.append(78 + (d // 256) * 4 + d % 4)
    select = np.arange(512)[None, :] == (np.arange(384) // 12 * 16 + np.arange(384) % 12)[:, None]
    row12 = np.arange(512)[:, None] == np.arange(32)[None, :] * 16 + 12
    row13 = np.arange(512)[:, None] == np.arange(32)[None, :] * 16 + 13
    pads = np.arange(16)[:, None] == np.arange(12)[None, :]
    lane = np.arange(128)
    half = lane % 64
    six = half % 6 == np.arange(6)[:, None]
    four = lane % 4 == np.arange(4)[:, None]
    place = np.zeros((14, 128), np.float32)
    place[0:6], place[8:14] = six, lane // 4 == 3 + np.arange(6)[:, None]
    masks = [half // 6 == p for p in range(6)] + [lane // 6 == p for p in range(2)]
    masks += [(lane >= 12) & (lane < 36) & four[e] for e in range(4)]
    three = lane % 3 == np.arange(3)[:, None]
    ends = np.zeros((24, 128), np.float32)
    ends[0:6], ends[8:11], ends[19:22] = lane % 6 == np.arange(6)[:, None], three, three
    fours = (lane + 2) % 4 == np.arange(4)[:, None]
    return (
        spread,
        np.stack(rows).astype(np.int32),
        step,
        np.stack(back).astype(np.int32),
        select.astype(np.float32),
        np.stack([row12, row13]).astype(np.float32),
        pads.astype(np.float32),
        place,
        np.stack(masks).astype(np.float32),
        ends,
        fours.astype(np.float32),
    )


(
    SPREAD,
    FETCH,
    FETCH_STEP,
    PUT,
    SELECT,
    ROWS,
    PADS,
    PLACE,
    MASKS,
    ENDS,
    FOURS,
) = layout_tables()


def matmul(left, right):
    return jnp.dot(left, right, preferred_element_type=F32)


def matmul_nt(left, right):
    return lax.dot_general(left, right, NT, preferred_element_type=F32)


def matmul_tn(left, right):
    return lax.dot_general(left, right, TN, preferred_element_type=F32)


def allowed_pairs(clip, qb, j):
    pos = first_key() + j * 256 + lax.broadcasted_iota(jnp.int32, (256, 256), 0)
    return (pos >= clip[qb, 0:1, :]) & (pos < clip[qb, 1:2, :])


def first_key():
    return (lax.axis_index("dp") // 2 - 3) * 512


def key_blocks(ends, qb):
    first = (ends[qb, 0, 0] - first_key()) // 256
    return first, (ends[qb, 1, 255] - first_key() + 255) // 256


def front_kernel(
    ends, clip, w, small_rows, spread, fetch, step_k, select, tk,
    vecs, w_attn, unit, kv, q, of, lse, attn,
):
    line = lax.broadcasted_iota(jnp.int32, (128, 768), 0)
    k = lax.axis_index("dp") % 2
    row12, row13 = [
        jnp.concatenate([matmul_tn(small_rows[i], w[z, :, 0:128]) for z in range(2)]).astype(BF)
        for i in range(2)
    ]
    wide = matmul_tn(row12, spread[0])
    for p in range(6):
        hit = line == fetch[p : p + 1, :]
        vecs[p : p + 1, :] = jnp.sum(jnp.where(hit, wide, 0.0), axis=0, keepdims=True)
    for p in (6, 7):
        wide = matmul_tn(row13, spread[p - 5])
        hit = line == fetch[p : p + 1, :] + k * step_k[p : p + 1, :]
        vecs[p : p + 1, :] = jnp.sum(jnp.where(hit, wide, 0.0), axis=0, keepdims=True)
    for z in range(2):
        w_attn[z * 384 : z * 384 + 384, :] = matmul(select[...], w[z]).astype(BF)

    def norm_rows(j):
        v = tk[j].astype(F32)
        centred = v - jnp.mean(v, axis=-1, keepdims=True)
        spread_out = jnp.mean(centred * centred, axis=-1, keepdims=True)
        u = centred * lax.rsqrt(spread_out + EPS)
        return u, (u * vecs[0:1, :] + vecs[2:3, :]).astype(BF)

    bounds = [key_blocks(ends, qb) for qb in range(2)]

    @pl.loop(bounds[0][0], bounds[1][1])
    def _(j):
        u, a = norm_rows(j)
        unit[j] = u.astype(BF)
        kv[j] = (matmul(a, w_attn[:, 0:384]) + vecs[6:7, 0:384]).astype(BF)

    low = (lax.broadcasted_iota(jnp.int32, (256, 384), 1) & 127) < 64
    for qb in range(2):
        _, a = norm_rows(6 + qb)
        v = (matmul(a, w_attn[:, 384:768]) + vecs[6:7, 384:768]).astype(BF).astype(F32)
        q[qb * 256 : qb * 256 + 256, :] = jnp.where(low, v * SCORE_SCALE, 0.0).astype(BF)

    lane = lax.broadcasted_iota(jnp.int32, (256, 128), 1)
    for qb in range(2):
        rows = slice(qb * 256, qb * 256 + 256)

        def step(j, carry):
            ok = allowed_pairs(clip, qb, j)
            new = []
            for h in range(3):
                m, l, acc = carry[h]
                cols = slice(h * 128, h * 128 + 128)
                keys = kv[j, :, cols]
                s = jnp.where(ok, matmul_nt(keys, q[rows, cols]), NEGATIVE)
                top = jnp.maximum(m, jnp.max(s, axis=0, keepdims=True))
                p = jnp.exp(s - top)
                fade = jnp.exp(m - top)
                l = l * fade + jnp.sum(p, axis=0, keepdims=True)
                acc = acc * fade + matmul_tn(keys, p.astype(BF))
                new.append((top, l, acc))
            return tuple(new)

        start = tuple(
            (
                jnp.full((1, 256), NEGATIVE, F32),
                jnp.zeros((1, 256), F32),
                jnp.zeros((128, 256), F32),
            )
            for _ in range(3)
        )
        final = lax.fori_loop(bounds[qb][0], bounds[qb][1], step, start)
        for h in range(3):
            m, l, acc = final[h]
            o = (acc / l).T
            of[rows, h * 128 : h * 128 + 128] = jnp.where(lane >= 64, o, 0.0)
            lse[h : h + 1, rows] = m + jnp.log(l)
        attn[rows, :] = matmul_nt(of[rows, :].astype(BF), w_attn[:, 384:768]).astype(BF)


def front(*args):
    return pl.pallas_call(
        front_kernel,
        out_shape=[
            jax.ShapeDtypeStruct((8, 768), F32),
            jax.ShapeDtypeStruct((768, 768), BF),
            jax.ShapeDtypeStruct((14, 256, 768), BF),
            jax.ShapeDtypeStruct((14, 256, 384), BF),
            jax.ShapeDtypeStruct((512, 384), BF),
            jax.ShapeDtypeStruct((512, 384), F32),
            jax.ShapeDtypeStruct((3, 512), F32),
            jax.ShapeDtypeStruct((512, 768), BF),
        ],
        in_specs=[SM] + [VM] * 8,
        out_specs=[VM] * 8,
        compiler_params=pltpu.CompilerParams(vmem_limit_bytes=LIMIT),
        name="front",
    )(*args)


def back_kernel(
    ends, clip, q, dr, of, kv, lse, unit, w_attn, vecs, sums, up_sum, spread, put, select, row12,
    d_out, grad, total, dox, delta, dq, ug,
):
    bounds = [key_blocks(ends, qb) for qb in range(2)]
    lane = lax.broadcasted_iota(jnp.int32, (256, 128), 1)
    high = (lax.broadcasted_iota(jnp.int32, (256, 384), 1) & 127) >= 64

    @pl.loop(0, 14)
    def _(j):
        total[j] = jnp.zeros((256, 384), F32)
        d_out[j] = jnp.zeros((256, 768), BF)

    for qb in range(2):
        rows = slice(qb * 256, qb * 256 + 256)
        g = jnp.where(high, matmul(dr[rows, :], w_attn[:, 384:768]), 0.0).astype(BF)
        dox[rows, :] = g
        prod = g.astype(F32) * of[rows, :]
        for h in range(3):
            part = prod[:, h * 128 : h * 128 + 128].T
            delta[h : h + 1, rows] = jnp.sum(part, axis=0, keepdims=True)

    for qb in range(2):
        rows = slice(qb * 256, qb * 256 + 256)

        def step(j, carry):
            ok = allowed_pairs(clip, qb, j)
            new = []
            for h in range(3):
                cols = slice(h * 128, h * 128 + 128)
                keys = kv[j, :, cols]
                qh, dh = q[rows, cols], dox[rows, cols]
                s = jnp.where(ok, matmul_nt(keys, qh), NEGATIVE)
                p = jnp.exp(s - lse[h : h + 1, rows])
                ds = (p * (matmul_nt(keys, dh) - delta[h : h + 1, rows])).astype(BF)
                new.append(carry[h] + matmul_tn(keys, ds))
                total[j, :, cols] += matmul(ds, qh) + matmul(p.astype(BF), dh)
            return tuple(new)

        start = tuple(jnp.zeros((128, 256), F32) for _ in range(3))
        final = lax.fori_loop(bounds[qb][0], bounds[qb][1], step, start)
        for h in range(3):
            part = jnp.where(lane < 64, SCORE_SCALE * final[h].T, 0.0)
            dq[rows, h * 128 : h * 128 + 128] = part.astype(BF)

    ug[...] = jnp.zeros((768, 768), F32)

    def chunk(j, kv_sum):
        z = total[j].astype(BF)
        d_out[j] = matmul_nt(z, w_attn[:, 0:384]).astype(BF)
        ug[:, 0:384] += matmul_tn(unit[j], z)
        return kv_sum + jnp.sum(z.astype(F32), axis=0, keepdims=True)

    kv_sum = lax.fori_loop(bounds[0][0], bounds[1][1], chunk, jnp.zeros((1, 384), F32))
    for qb in range(2):
        rows = slice(qb * 256, qb * 256 + 256)
        own = matmul_nt(total[6 + qb].astype(BF), w_attn[:, 0:384])
        d_out[6 + qb] = (own + matmul_nt(dq[rows, :], w_attn[:, 384:768])).astype(BF)
        ug[:, 384:768] += matmul_tn(unit[6 + qb], dq[rows, :])
    q_sum = jnp.sum(dq[...].astype(F32), axis=0, keepdims=True)
    z_sum = jnp.concatenate([kv_sum, q_sum], axis=1)

    line = lax.broadcasted_iota(jnp.int32, (128, 768), 0)

    def place(p, row):
        return jnp.where(line == put[p : p + 1, :], row, 0.0)

    columns = vecs[...].T
    gain_col, offset_col = columns[:, 0:1], columns[:, 2:3]
    w_full = w_attn[...].astype(F32)
    gain_sum = jnp.sum(ug[...] * w_full, axis=1, keepdims=True)
    offset_sum = jnp.sum(w_full * z_sum, axis=1, keepdims=True)
    flip = lax.broadcasted_iota(jnp.int32, (768, 128), 1)
    both = jnp.where(flip == 0, gain_sum, jnp.where(flip == 1, offset_sum, 0.0)).T
    own = place(0, both[0:1, :]) + place(2, both[1:2, :])
    for i, p in enumerate((1, 3, 4, 5)):
        own = own + place(p, sums[i : i + 1, :])
    small = matmul_nt(spread[0], own.astype(BF))
    small += matmul_nt(spread[1], place(6, z_sum).astype(BF))
    small += matmul_nt(spread[2], place(7, up_sum[...]).astype(BF))
    small = small.astype(BF)

    ug[...] = ug[...] * gain_col + offset_col * z_sum
    ug[:, 384:768] += matmul_tn(dr[...], of[...].astype(BF))
    for i in range(2):
        g = matmul_tn(select[...], ug[i * 384 : i * 384 + 384, :].astype(BF))
        grad[i] = g.astype(BF)
        extra = matmul(row12[...], small[i * 32 : i * 32 + 32, :])
        grad[i, :, 0:128] = (g[:, 0:128] + extra).astype(BF)


def back(*args):
    return pl.pallas_call(
        back_kernel,
        out_shape=[
            jax.ShapeDtypeStruct((14, 256, 768), BF),
            jax.ShapeDtypeStruct((2, 512, 768), BF),
        ],
        in_specs=[SM] + [VM] * (len(args) - 1),
        out_specs=[VM, VM],
        scratch_shapes=[
            pltpu.VMEM((14, 256, 384), F32),
            pltpu.VMEM((512, 384), BF),
            pltpu.VMEM((3, 512), F32),
            pltpu.VMEM((512, 384), BF),
            pltpu.VMEM((768, 768), F32),
        ],
        compiler_params=pltpu.CompilerParams(vmem_limit_bytes=LIMIT),
        name="back",
    )(*args)


def finish_kernel(
    own, far, back_one, e1, tok, vecs, ends, fours,
    tokens, g_in, g_qv, g_out, g_up, g_fc, g_down, g_gain, g_row,
):
    t = lax.axis_index("tensor")
    hidden = tok[...].astype(F32)
    centred = hidden - jnp.mean(hidden, axis=-1, keepdims=True)
    scale = lax.rsqrt(jnp.mean(centred * centred, axis=-1, keepdims=True) + EPS)
    unit = centred * scale
    w = back_one[...] * vecs[0:1, :]
    mean_w = jnp.mean(w, axis=-1, keepdims=True)
    mean_wu = jnp.mean(w * unit, axis=-1, keepdims=True)
    tokens[...] = e1[...] + scale * (w - mean_w - unit * mean_wu)

    exact = dict(precision=lax.Precision.HIGHEST, preferred_element_type=F32)
    for n in range(3):
        cols = slice(n * 128, n * 128 + 128)
        parts = []
        for head in (2 * n, 2 * n + 1):
            q, h = head // 3, head % 3
            parts.append(
                (own[q, :, 384 + h * 128 : 512 + h * 128], own[q, :, h * 128 : h * 128 + 128])
            )
        (qo_a, kv_a), (qo_b, kv_b) = parts
        g_in[0, :, 0, cols] = jnp.concatenate([qo_a[:, 0:64], qo_b[:, 0:64]], axis=1)[0:12]
        g_in[1, :, 0, cols] = jnp.concatenate([kv_a[:, 0:64], kv_b[:, 0:64]], axis=1)[0:12]
        g_in[2, :, 0, cols] = jnp.concatenate([kv_a[:, 64:128], kv_b[:, 64:128]], axis=1)[0:12]
        mixed = jnp.concatenate([qo_a[:, 64:128], qo_b[:, 64:128]], axis=1)
        g_out[:, 0, cols] = mixed[0:12]
    for q in range(2):
        cols = slice(q * 768, q * 768 + 768)
        g_up[:, 0, cols] = own[q, 0:12, 768:1536]
        g_down[:, 0, cols] = own[q, 0:12, 1536:2304]
    row0, row1 = own[0, 12:13, 0:128], own[1, 12:13, 0:128]
    vec = row0 + row1 + far[12:13, :]
    lane = lax.broadcasted_iota(jnp.int32, (8, 128), 1)
    line = lax.broadcasted_iota(jnp.int32, (8, 128), 0)

    def pick(row, start, width, stride):
        begin = start + line * stride
        return jnp.where((lane >= begin) & (lane < begin + width), row, 0.0)

    norms = lax.dot_general(pick(vec, 6 * t, 6, 12), ends[0:6, :], NT, **exact)
    g_gain[...] = norms[0:2]
    g_row[...] = norms[2:6]
    heads = lax.dot_general(pick(row0, 72, 3, 3), ends[8:14, :], NT, **exact)
    heads += lax.dot_general(pick(row1, 72, 3, 3), ends[16:22, :], NT, **exact)
    g_qv[...] = heads[0:2]
    hidden_rows = jnp.where(line < 3, pick(row0, 78, 4, 4), pick(row1, 66, 4, 4))
    g_fc[...] = lax.dot_general(fours[...], hidden_rows, NT, **exact)[:, 0:6]


def finish(*args):
    return pl.pallas_call(
        finish_kernel,
        out_shape=[
            jax.ShapeDtypeStruct(dims, F32)
            for dims in (
                (128, 768),
                (3, 12, 1, 384),
                (2, 6),
                (12, 1, 384),
                (12, 1, 1536),
                (4, 6),
                (12, 1, 1536),
                (2, 6),
                (4, 6),
            )
        ],
        in_specs=[VM] * len(args),
        out_specs=[VM] * 9,
        compiler_params=pltpu.CompilerParams(vmem_limit_bytes=LIMIT),
        name="finish",
    )(*args)


def body(
    tokens,
    clip_bounds,
    attn_in,
    qv_bias,
    out_proj,
    fc_in,
    fc_bias,
    fc_out,
    ln_gain,
    row_bias,
    cotangent,
):
    spread, select, small_rows = [jnp.asarray(v, BF) for v in (SPREAD, SELECT, ROWS)]
    w, f0, f1, clip, near_tokens = gather_all(
        clip_bounds,
        tokens,
        attn_in[0],
        out_proj[0].T,
        fc_in[0],
        fc_out[0].T,
        ln_gain[0],
        row_bias[0],
        qv_bias.reshape(2, 6),
        fc_bias[0].T,
        jnp.asarray(PADS, BF),
        jnp.asarray(PLACE, BF),
        jnp.asarray(MASKS),
    )
    vecs, w_attn, unit, near, query, mixed, lse, attn = front(
        clip,
        clip,
        w.reshape(2, 512, 768),
        small_rows,
        spread,
        jnp.asarray(FETCH),
        jnp.asarray(FETCH_STEP),
        select,
        near_tokens.reshape(14, 256, 768),
    )
    output, grad_hidden_one, full_attn, sums, up_sum, u0, u1 = mid(
        attn.reshape(4, 128, 768), f0, f1, cotangent, tokens, vecs, select
    )
    near_back, grad_w = back(
        clip,
        clip,
        query,
        full_attn.reshape(512, 768),
        mixed,
        near,
        lse,
        unit,
        w_attn,
        vecs,
        sums,
        up_sum,
        spread,
        jnp.asarray(PUT),
        select,
        small_rows[0],
    )
    back_one, own, far = return_all(
        near_back.reshape(7, 4, 128, 768), grad_w.reshape(2, 4, 4, 2, 16, 768), u0, u1
    )
    grads = finish(
        own, far, back_one, grad_hidden_one, tokens, vecs, jnp.asarray(ENDS), jnp.asarray(FOURS)
    )
    grad_tokens, g_in, g_qv, g_out, g_up, g_fc, g_down, g_gain, g_row = grads
    return (
        output,
        grad_tokens,
        g_in.reshape(1, 3, 12, 384),
        g_qv.reshape(1, 2, 6, 1),
        g_out.reshape(12, 384).T[None],
        g_up.reshape(1, 12, 1536),
        g_fc.T[None],
        g_down.reshape(12, 1536).T[None],
        g_gain[None],
        g_row[None],
    )


def solution(mesh):
    return jax.shard_map(
        body,
        mesh=mesh,
        in_specs=(
            P(("dp", "tensor"), None),
            P(None, "dp"),
            P(None, None, "dp", "tensor"),
            P(None, None, "tensor", "dp"),
            P(None, "tensor", "dp"),
            P(None, "dp", "tensor"),
            P(None, "tensor", "dp"),
            P(None, "tensor", "dp"),
            P(None, None, ("dp", "tensor")),
            P(None, None, ("dp", "tensor")),
            P(("dp", "tensor"), None),
        ),
        out_specs=(
            P(("dp", "tensor"), None),
            P(("dp", "tensor"), None),
            P(None, None, "dp", "tensor"),
            P(None, None, "tensor", "dp"),
            P(None, "tensor", "dp"),
            P(None, "dp", "tensor"),
            P(None, "tensor", "dp"),
            P(None, "tensor", "dp"),
            P(None, None, ("dp", "tensor")),
            P(None, None, ("dp", "tensor")),
        ),
        check_vma=False,
    )
```

```python
import jax
import jax.numpy as jnp
import numpy as np
from jax import lax
import jax.experimental.pallas as pl
import jax.experimental.pallas.tpu as pltpu
from jax.sharding import PartitionSpec as P

EPS = 1e-05
NEGATIVE = -1e30
SCORE_SCALE = 0.125
BF = jnp.bfloat16
F32 = jnp.float32
MESH = pl.DeviceIdType.MESH
VM = pl.BlockSpec(memory_space=pltpu.VMEM)
SM = pl.BlockSpec(memory_space=pltpu.SMEM)
DMA = pltpu.SemaphoreType.DMA
NT = (((1,), (1,)), ((), ()))
TN = (((0,), (0,)), ((), ()))


def coords():
    dp = lax.axis_index("dp")
    return dp // 32, (dp // 8) % 4, (dp // 2) % 4, dp % 2, lax.axis_index("tensor")


def device(z, y, x, k, t):
    return (((z * 4 + y) * 4 + x) * 2 + k, t)


def chip(c, k, t):
    return (c * 2 + k, t)


def greet(peers):
    bar = pltpu.get_barrier_semaphore()
    for peer in peers:
        pl.semaphore_signal(bar, inc=1, device_id=peer, device_id_type=MESH)
    pl.semaphore_wait(bar, len(peers))


def remote(src, dst, sems, index, peer):
    send, recv = sems
    return pltpu.make_async_remote_copy(
        src, dst, send.at[index], recv.at[index], device_id=peer, device_id_type=MESH
    )


def comm_call(kernel, out_shape, scratch, cid, name, args, room, place=VM):
    single = not isinstance(out_shape, (list, tuple))
    return pl.pallas_call(
        kernel,
        out_shape=out_shape,
        in_specs=[place] * len(args),
        out_specs=VM if single else [VM] * len(out_shape),
        scratch_shapes=scratch,
        compiler_params=pltpu.CompilerParams(
            collective_id=cid, has_side_effects=True, vmem_limit_bytes=room * 2**20
        ),
        name=name,
    )(*args)


def neighbours():
    z, y, x, k, t = coords()
    xs = [device(z, y, (x + d) % 4, k, t) for d in (1, 2, 3)]
    ys = [device(z, (y + d) % 4, x, k, t) for d in (1, 2, 3)]
    core = device(z, y, x, 1 - k, t)
    far = device(z, y, x, k, 1 - t)
    low = device(1 - z, y, x, k, t)
    ring = [chip(((z * 4 + y) * 4 + x + d) % 32, k, t) for d in RING]
    return (z, y, x, k, t), xs, ys, core, far, low, ring


RING = (2, -2, 3, -3, 1, -1)


class Copies:
    def __init__(self, send, recv):
        self.sems, self.count = (send, recv), 0

    def __call__(self, src, dst, peer):
        made = remote(src, dst, self.sems, self.count, peer)
        self.count += 1
        made.start()
        return made


def build_small(gain, row, qv, fc, first, t, tile):
    place = first[0:14, :].astype(BF)
    masks = first[16:28, :]

    norms = jnp.sum(matmul(gain[...], place[0:6, :]) * masks[0:2, :], axis=0, keepdims=True)
    norms += jnp.sum(matmul(row[...], place[0:6, :]) * masks[2:6, :], axis=0, keepdims=True)
    lane = lax.broadcasted_iota(jnp.int32, (16, 128), 1)
    line = lax.broadcasted_iota(jnp.int32, (16, 128), 0)
    others = jnp.sum(matmul(qv[...], place[0:6, :]) * masks[6:8, :], axis=0, keepdims=True)
    others += jnp.sum(matmul(fc[...], place[8:14, :]) * masks[8:12, :], axis=0, keepdims=True)
    mine = (line == 12) & (lane >= 64 * t) & (lane < 64 * t + 64)
    small = jnp.where(mine, norms, 0.0)
    tile[...] = small.astype(BF)
    return small + jnp.where(line == 13, others, 0.0)


def build_rows(attn_w, proj, up, down, small, first, pay):
    pads = first[32:48, 0:12].astype(BF)

    def tall(v):
        return matmul(pads, v)

    query, keys, values = [tall(attn_w[i]) for i in range(3)]
    mixed, up_rows, down_rows = tall(proj[...]), tall(up[...]), tall(down[...])
    for q in range(2):
        for h in range(3):
            n = slice((q * 3 + h) * 64, (q * 3 + h) * 64 + 64)
            pair = jnp.concatenate([keys[:, n], values[:, n]], axis=1)
            if h == 0:
                pair = pair + small
            pay[q, :, h * 128 : h * 128 + 128] = pair.astype(BF)
            pair = jnp.concatenate([query[:, n], mixed[:, n]], axis=1)
            pay[q, :, 384 + h * 128 : 512 + h * 128] = pair.astype(BF)
        pay[q, :, 768:1536] = up_rows[:, q * 768 : q * 768 + 768].astype(BF)
        pay[q, :, 1536:2304] = down_rows[:, q * 768 : q * 768 + 768].astype(BF)


H0, H1 = pl.ds(0, 512), pl.ds(512, 256)


def gather_kernel(
    clip, tok, cot, attn_h, proj_h, up_h, down_h, gain_h, row_h, qv_h, fc_h, first_h,
    ones_h, spots_h, last_h,
    w, f0, f1, clip_out, tk, tok_out, cot_out, ones, spots, last,
    attn_w, proj, up, down, gain, row, qv, fc, first,
    pay_s, tile, tile_in, ws, send, recv, local,
):
    stages = []

    def stage(src, dst):
        stages.append(pltpu.make_async_copy(src, dst, local.at[len(stages)]))
        stages[-1].start()

    for src, dst in (
        (gain_h, gain), (row_h, row), (qv_h, qv), (fc_h, fc), (first_h, first),
        (attn_h, attn_w), (proj_h, proj), (up_h, up), (down_h, down),
    ):
        stage(src, dst)
    (z, y, x, k, t), xs, ys, core, far, low, ring = neighbours()
    copy = Copies(send, recv)
    mine, other = k * 2 + t, k * 2 + 1 - t
    greet(xs + ys + [core, far, low] + ring)
    own_far = copy(tok, tk.at[3, mine], far)
    order = (4, 5, 2, 3, 0, 1)
    pushes = {i: copy(tok, tk.at[3 - RING[i], mine], ring[i]) for i in order}
    done = [copy(tok, tk.at[3, mine], core), copy(clip, clip_out.at[k], core)]
    stage(tok, tk.at[3, mine])
    stage(clip, clip_out.at[k])
    for pair in ((tok, tok_out), (cot, cot_out), (ones_h, ones), (spots_h, spots), (last_h, last)):
        stage(*pair)
    for c in stages[0:9]:
        c.wait()
    small = build_small(gain, row, qv, fc, first, t, tile)
    c_tile = copy(tile, tile_in, far)
    build_rows(attn_w, proj, up, down, small, first, pay_s)
    to_far = {}

    def to_core(slot, which):
        done.append(copy(tk.at[slot, which], tk.at[slot, which], core))

    def pass_on(i):
        pushes[i].wait_recv()
        slot = 3 - RING[i]
        to_far[i] = copy(tk.at[slot, mine], tk.at[slot, mine], far)
        to_core(slot, mine)

    c_tile.wait()
    for q in range(2):
        pay_s[q, :, 0:128] = pay_s[q, :, 0:128] + tile_in[...]
    swap = copy(pay_s.at[1 - k], ws.at[z, k], core)
    ws[z, k] = pay_s[k]
    for i in (4, 5):
        pushes[i].wait_recv()
        to_core(3 - RING[i], mine)
    swap.wait()
    c_low = copy(ws.at[z], ws.at[z], low)
    pass_on(2)
    pass_on(3)
    c_low.wait()
    w[:, y, x] = ws[:, :, :, 0:768]
    f0[:, x] = ws[:, :, :, 768:1536]
    f1[:, y] = ws[:, :, :, 1536:2304]
    phase = []
    for i in range(3):
        phase.append(copy(ws.at[:, :, :, H0], w.at[:, y, x, :, :, H0], xs[i]))
        phase.append(copy(ws.at[:, :, :, H1], w.at[:, y, x, :, :, H1], ys[i]))
    pass_on(0)
    pass_on(1)
    own_far.wait_recv()
    beyond = []
    for i in (4, 5):
        slot = 3 - RING[i]
        beyond.append((slot, copy(tk.at[3, other], tk.at[slot, other], ring[i])))
    to_core(3, other)
    for c in phase:
        c.wait()
    rest = []
    for i in range(3):
        a = w.at[:, y, :, :, :, H0]
        rest.append(copy(a, a, ys[i]))
        b = w.at[:, :, x, :, :, H1]
        rest.append(copy(b, b, xs[i]))
    for i in range(3):
        rest.append(copy(ws.at[:, :, :, pl.ds(768, 768)], f0.at[:, x], xs[i]))
        rest.append(copy(ws.at[:, :, :, pl.ds(1536, 768)], f1.at[:, y], ys[i]))
    for i in (2, 3, 0, 1):
        to_far[i].wait_recv()
        to_core(3 - RING[i], other)
    for slot, c in beyond:
        c.wait_recv()
        to_core(slot, other)
        c.wait_send()
    for i in order:
        pushes[i].wait_send()
    for i in (2, 3, 0, 1):
        to_far[i].wait_send()
    own_far.wait_send()
    for c in rest + done + stages[9:]:
        c.wait()


def gather_all(*args):
    return comm_call(
        gather_kernel,
        [
            jax.ShapeDtypeStruct((2, 4, 4, 2, 16, 768), BF),
            jax.ShapeDtypeStruct((2, 4, 2, 16, 768), BF),
            jax.ShapeDtypeStruct((2, 4, 2, 16, 768), BF),
            jax.ShapeDtypeStruct((2, 2, 256), jnp.int32),
            jax.ShapeDtypeStruct((7, 4, 128, 768), BF),
            jax.ShapeDtypeStruct((128, 768), BF),
            jax.ShapeDtypeStruct((128, 768), BF),
            jax.ShapeDtypeStruct((640, 768), BF),
            jax.ShapeDtypeStruct((24, 768), jnp.int32),
            jax.ShapeDtypeStruct((32, 128), F32),
        ],
        [pltpu.VMEM(v.shape, v.dtype) for v in args[3:12]]
        + [
            pltpu.VMEM((2, 16, 2304), BF),
            pltpu.VMEM((16, 128), BF),
            pltpu.VMEM((16, 128), BF),
            pltpu.VMEM((2, 2, 16, 2304), BF),
            DMA((50,)),
            DMA((50,)),
            DMA((16,)),
        ],
        0,
        "gather_first",
        args,
        54,
        pl.BlockSpec(memory_space=pltpu.MemorySpace.HBM),
    )


def exchange_rows(copy, a, out, k, t, core, far):
    mine, other = k * 2 + t, k * 2 + 1 - t
    c_far = copy(a, out.at[mine], far)
    c_core = copy(a, out.at[mine], core)
    out[mine] = a[...]

    def finish():
        c_far.wait_recv()
        c_pass = copy(out.at[other], out.at[other], core)
        c_far.wait_send()
        c_core.wait()
        c_pass.wait()

    return finish


def spread_first(copy, g0, g1, b0, b1, x, y, xs, ys):
    over_y, over_x = [], []
    for i in range(3):
        over_y.append(copy(g0.at[:, (y + i + 1) % 4], b0.at[i], ys[i]))
        over_x.append(copy(g1.at[:, :, (x + i + 1) % 4], b1.at[i], xs[i]))
    return over_y, over_x


def add_first(g0, g1, b0, b1, s0, s1, x, y, over_y, over_x):
    for c in over_y:
        c.wait()

    @pl.loop(0, 8)
    def _(n):
        zz, m = n // 4, n % 4
        v = g0[zz, y, m].astype(F32)
        for i in range(3):
            v = v + b0[i, zz, m].astype(F32)
        s0[zz, m] = v.astype(BF)

    for c in over_x:
        c.wait()

    @pl.loop(0, 8)
    def _(n):
        zz, m = n // 4, n % 4
        v = g1[zz, m, x].astype(F32)
        for i in range(3):
            v = v + b1[i, zz, m].astype(F32)
        s1[zz, m] = v.astype(BF)


def spread_second(copy, s0, s1, a0, a1, x, y, xs, ys):
    over_x, over_y = [], []
    for i in range(3):
        over_x.append(copy(s0.at[:, (x + i + 1) % 4], a0.at[i], xs[i]))
        over_y.append(copy(s1.at[:, (y + i + 1) % 4], a1.at[i], ys[i]))
    return over_x, over_y


def add_second(s0, s1, a0, a1, u0, u1, x, y, over_x, over_y):
    for c in over_x + over_y:
        c.wait()
    for zz in range(2):
        v = s0[zz, x].astype(F32)
        v1 = s1[zz, y].astype(F32)
        for i in range(3):
            v = v + a0[i, zz].astype(F32)
            v1 = v1 + a1[i, zz].astype(F32)
        u0[zz] = v.astype(BF)
        u1[zz] = v1.astype(BF)


def mid_kernel(
    p, f0, f1, cot, tok, vecs, ones,
    output, e1, dr_full, sums, up_sum, s0, s1,
    got, mid, got_far, p0, p1, w_up, w_down, b_full, cot_full, dg, active, du_full,
    pr, got_two, mid_two, far_two, dr, g0, g1, b0, b1, send, recv,
):
    (z, y, x, k, t), xs, ys, core, far, low, ring = neighbours()
    copy = Copies(send, recv)
    greet(xs + ys + [core, far])
    mine, across, beside, both = k * 2 + t, k * 2 + 1 - t, 2 - 2 * k + t, 3 - 2 * k - t
    to_core = copy(p.at[pl.ds((1 - k) * 2, 2)], got, core)
    made = []
    for i in range(2):
        for j in range(3):
            made.append(copy(f0.at[i], p0.at[i, y], ys[j]))
            made.append(copy(f1.at[i], p1.at[i, :, x], xs[j]))
        p0[i, y] = f0[i]
        p1[i, :, x] = f1[i]
    to_core.wait()
    mid[...] = (p[across].astype(F32) + got[1 - t].astype(F32)).astype(BF)
    to_far = copy(mid, got_far, far)
    finish_cot = exchange_rows(copy, cot, cot_full, k, t, core, far)
    part = p[mine].astype(F32) + got[t].astype(F32) + tok[...].astype(F32) + vecs[3:4, :]
    to_far.wait()
    hidden = part + got_far[...].astype(F32)
    centred = hidden - jnp.mean(hidden, axis=-1, keepdims=True)
    scale = lax.rsqrt(jnp.mean(centred * centred, axis=-1, keepdims=True) + EPS)
    unit = centred * scale
    b_full[mine] = (unit * vecs[1:2, :] + vecs[4:5, :]).astype(BF)
    rows_far = copy(b_full.at[mine], b_full.at[mine], far)
    rows_core = copy(b_full.at[mine], b_full.at[mine], core)
    e1[...] = hidden
    finish_cot()
    for c in made:
        c.wait()
    for i in range(2):
        rows = slice(i * 384, i * 384 + 384)
        w_up[rows, :] = matmul(ones[SELECT], p0[i].reshape(512, 768)).astype(BF)
        w_down[rows, :] = matmul(ones[SELECT], p1[i].reshape(512, 768)).astype(BF)

    @pl.loop(0, 4)
    def _(i):
        dg[i] = matmul(cot_full[i], w_down[...])

    up_sum[...] = jnp.zeros((1, 768), F32)

    def feed(i):
        u = matmul(b_full[i], w_up[...]) + vecs[7:8, :]
        phi = 0.5 + 0.5 * lax.erf(u * 0.7071067811865476)
        gl = (u * phi).astype(BF)
        active[i] = gl
        pr[0, i] = matmul_nt(gl, w_down[...]).astype(BF)
        slope = phi + u * jnp.exp(-0.5 * u * u) * 0.3989422804014327
        du = (dg[i] * slope).astype(BF)
        du_full[i] = du
        up_sum[...] += jnp.sum(du.astype(F32), axis=0, keepdims=True)
        pr[1, i] = matmul_nt(du, w_up[...]).astype(BF)

    feed(mine)
    rows_core.wait()
    feed(beside)
    first = copy(pr.at[:, beside], got_two.at[:, t], core)
    rows_far.wait()
    rows_pass = copy(b_full.at[across], b_full.at[across], core)
    feed(across)
    rows_pass.wait()
    feed(both)
    second = copy(pr.at[:, both], got_two.at[:, 1 - t], core)
    second.wait()
    for i in range(2):
        v = pr[i, across].astype(F32) + got_two[i, 1 - t].astype(F32)
        mid_two[i] = v.astype(BF)
    two = {1: copy(mid_two.at[1], far_two.at[1], far)}
    b_rows, du_rows = b_full[...].reshape(512, 768), du_full[...].reshape(512, 768)
    for i in range(2):
        cols = slice(i * 384, i * 384 + 384)
        g = matmul_tn(b_rows[:, cols], du_rows).astype(BF)
        g0[i] = matmul_tn(ones[SELECT], g).astype(BF).reshape(4, 4, 2, 16, 768)
    c_rows, a_rows = cot_full[...].reshape(512, 768), active[...].reshape(512, 768)
    for i in range(2):
        cols = slice(i * 384, i * 384 + 384)
        g = matmul_tn(c_rows[:, cols], a_rows).astype(BF)
        g1[i] = matmul_tn(ones[SELECT], g).astype(BF).reshape(4, 4, 2, 16, 768)
    over = spread_first(copy, g0, g1, b0, b1, x, y, xs, ys)
    first.wait()

    def summed(i):
        v = pr[i, mine].astype(F32) + got_two[i, t].astype(F32)
        two[i].wait()
        return v + far_two[i].astype(F32)

    back_rows = summed(1)
    hidden = e1[...]
    centred = hidden - jnp.mean(hidden, axis=-1, keepdims=True)
    scale = lax.rsqrt(jnp.mean(centred * centred, axis=-1, keepdims=True) + EPS)
    unit = centred * scale
    w = back_rows * vecs[1:2, :]
    mean_w = jnp.mean(w, axis=-1, keepdims=True)
    mean_wu = jnp.mean(w * unit, axis=-1, keepdims=True)
    cot_f = cot[...].astype(F32)
    grad = cot_f + scale * (w - mean_w - unit * mean_wu)
    e1[...] = grad
    low_grad = grad.astype(BF)
    dr[...] = low_grad
    finish_rows = exchange_rows(copy, dr, dr_full, k, t, core, far)
    two[0] = copy(mid_two.at[0], far_two.at[0], far)
    sums[0:1, :] = jnp.sum(back_rows * unit, axis=0, keepdims=True)
    sums[1:2, :] = jnp.sum(low_grad.astype(F32), axis=0, keepdims=True)
    sums[2:3, :] = jnp.sum(back_rows, axis=0, keepdims=True)
    sums[3:4, :] = jnp.sum(cot_f, axis=0, keepdims=True)
    finish_rows()
    output[...] = (hidden + summed(0) + vecs[5:6, :]).astype(BF)
    add_first(g0, g1, b0, b1, s0, s1, x, y, *over)


def mid(p, f0, f1, cot, tok, vecs, ones):
    rows = pltpu.VMEM((128, 768), BF)
    two = pltpu.VMEM((2, 128, 768), BF)
    four = pltpu.VMEM((4, 128, 768), BF)
    square = pltpu.VMEM((768, 768), BF)
    piece = pltpu.VMEM((2, 4, 4, 2, 16, 768), BF)
    return comm_call(
        mid_kernel,
        [
            jax.ShapeDtypeStruct((128, 768), BF),
            jax.ShapeDtypeStruct((128, 768), F32),
            jax.ShapeDtypeStruct((4, 128, 768), BF),
            jax.ShapeDtypeStruct((4, 768), F32),
            jax.ShapeDtypeStruct((1, 768), F32),
            jax.ShapeDtypeStruct((2, 4, 2, 16, 768), BF),
            jax.ShapeDtypeStruct((2, 4, 2, 16, 768), BF),
        ],
        [two, rows, rows, piece, piece, square, square, four, four]
        + [pltpu.VMEM((4, 128, 768), F32), four, four]
        + [pltpu.VMEM((2, 4, 128, 768), BF), pltpu.VMEM((2, 2, 128, 768), BF), two, two, rows]
        + [piece, piece]
        + [pltpu.VMEM((3, 2, 4, 2, 16, 768), BF)] * 2
        + [DMA((33,)), DMA((33,))],
        1,
        "mid",
        (p, f0, f1, cot, tok, vecs, ones),
        26,
    )


def return_kernel(
    d, g, fs0, fs1, out, own, tile_out,
    got_core, v1, in1, e_send, got_far, r_send, got_ring,
    b0, b1, s0, s1, a0, a1, fa0, fa1, u0, u1, v_0, v_1, z_in0, z_in1, z_in2, z_in3, res, tile, send, recv,
):
    (z, y, x, k, t), xs, ys, core, far, low, ring = neighbours()
    copy = Copies(send, recv)
    greet(xs + ys + [core, far, low] + ring)
    mine, across = k * 2 + t, k * 2 + 1 - t
    near = (ring[4], ring[5])
    order = (4, 2, 5, 1, 6, 0, 3)
    to_core = {j: copy(d.at[j, pl.ds((1 - k) * 2, 2)], got_core.at[j], core) for j in order}
    g0, g1 = g.at[:, :, :, :, :, H0], g.at[:, :, :, :, :, H1]
    fc_over = spread_second(copy, fs0, fs1, fa0, fa1, x, y, xs, ys)
    hop1, to_far = [], []
    over = spread_first(copy, g0, g1, b0, b1, x, y, xs, ys)
    for i, j in enumerate((4, 2)):
        to_core[j].wait()
        v1[i] = (d[j, pl.ds(k * 2, 2)].astype(F32) + got_core[j].astype(F32)).astype(BF)
        hop1.append(copy(v1.at[i], in1.at[i], near[i]))
    for i, j in enumerate(order[2:6]):
        to_core[j].wait()
        e_send[i] = (d[j, across].astype(F32) + got_core[j, 1 - t].astype(F32)).astype(BF)
        to_far.append(copy(e_send.at[i], got_far.at[i], far))
    home = []

    def send_home(i):
        j = order[2 + i]
        to_far[i].wait()
        v = d[j, mine].astype(F32) + got_core[j, t].astype(F32) + got_far[i].astype(F32)
        r_send[i] = v.astype(BF)
        home.append(copy(r_send.at[i], got_ring.at[i], ring[i]))

    add_second(fs0, fs1, fa0, fa1, u0, u1, x, y, *fc_over)
    fc_z = [copy(u0.at[1 - z], z_in0, low), copy(u1.at[1 - z], z_in1, low)]
    send_home(0)
    send_home(1)
    add_first(g0, g1, b0, b1, s0, s1, x, y, *over)
    over = spread_second(copy, s0, s1, a0, a1, x, y, xs, ys)
    to_core[3].wait()
    hop1[0].wait()
    hop1[1].wait()
    v = d[3, across].astype(F32) + got_core[3, 1 - t].astype(F32)
    v = v + in1[0, 1 - t].astype(F32) + in1[1, 1 - t].astype(F32)
    e_send[4] = v.astype(BF)
    last = copy(e_send.at[4], got_far.at[4], far)
    send_home(2)
    send_home(3)
    add_second(s0, s1, a0, a1, v_0, v_1, x, y, *over)
    attn_z = [copy(v_0.at[1 - z], z_in2, low), copy(v_1.at[1 - z], z_in3, low)]
    for c in fc_z:
        c.wait()
    res[:, :, 768:1536] = u0[z].astype(F32) + z_in0[...].astype(F32)
    res[:, :, 1536:2304] = u1[z].astype(F32) + z_in1[...].astype(F32)
    for c in attn_z:
        c.wait()
    res[:, :, H0] = v_0[z].astype(F32) + z_in2[...].astype(F32)
    res[:, :, H1] = v_1[z].astype(F32) + z_in3[...].astype(F32)
    swap = copy(res.at[1 - k], own.at[k], core)
    own[k] = res[k]
    total = d[3, mine].astype(F32) + got_core[3, t].astype(F32)
    total = total + in1[0, t].astype(F32) + in1[1, t].astype(F32)
    swap.wait()
    tile[...] = own[0, :, 0:128] + own[1, :, 0:128]
    c_tile = copy(tile, tile_out, far)
    for i in range(4):
        home[i].wait()
        total = total + got_ring[i].astype(F32)
    last.wait()
    out[...] = total + got_far[4].astype(F32)
    c_tile.wait()


def return_all(d, g, s0, s1):
    two = pltpu.VMEM((2, 2, 128, 768), BF)
    wide, slim = 512, 256
    return comm_call(
        return_kernel,
        [
            jax.ShapeDtypeStruct((128, 768), F32),
            jax.ShapeDtypeStruct((2, 16, 2304), F32),
            jax.ShapeDtypeStruct((16, 128), F32),
        ],
        [pltpu.VMEM((7, 2, 128, 768), BF), two, two]
        + [pltpu.VMEM((5, 128, 768), BF)] * 2
        + [pltpu.VMEM((4, 128, 768), BF)] * 2
        + [pltpu.VMEM((3, 2, 4, 2, 16, n), BF) for n in (wide, slim)]
        + [pltpu.VMEM((2, 4, 2, 16, n), BF) for n in (wide, slim)]
        + [pltpu.VMEM((3, 2, 2, 16, n), BF) for n in (wide, slim)]
        + [pltpu.VMEM((3, 2, 2, 16, 768), BF)] * 2
        + [pltpu.VMEM((2, 2, 16, n), BF) for n in (768, 768, wide, slim)]
        + [pltpu.VMEM((2, 16, n), BF) for n in (768, 768, wide, slim)]
        + [pltpu.VMEM((2, 16, 2304), F32), pltpu.VMEM((16, 128), F32), DMA((42,)), DMA((42,))],
        5,
        "return_all",
        (d, g, s0, s1),
        24,
    )


def layout_tables():
    d = np.arange(768)
    n64 = np.arange(64)[:, None]
    own = (d // 12 == n64).astype(np.float32)
    lane = d % 128
    high = d < 384
    column = np.where(high, lane - 64, lane)
    heads = ((column == n64) & (column >= 0) & (column < 64)).astype(np.float32)
    hidden = ((d % 256) // 4 == n64).astype(np.float32)
    spread = np.stack([own, heads, hidden])
    spot = 64 * ((d % 12) // 6) + d % 6
    head = (d % 384) // 128
    rows = [spot + 6 * p for p in range(6)]
    rows.append(np.where(high, 6, 0) + head)
    rows.append(12 + (d // 256) * 4 + d % 4)
    step = np.zeros((8, 768), np.int32)
    step[6], step[7] = 3, 12
    back = [12 * p + d % 12 for p in range(6)]
    back.append(72 + np.where(high, 3, 0) + head)
    back.append(78 + (d // 256) * 4 + d % 4)
    select = np.arange(512)[None, :] == (np.arange(384) // 12 * 16 + np.arange(384) % 12)[:, None]
    row12 = np.arange(512)[:, None] == np.arange(32)[None, :] * 16 + 12
    row13 = np.arange(512)[:, None] == np.arange(32)[None, :] * 16 + 13
    pads = np.arange(16)[:, None] == np.arange(12)[None, :]
    lane = np.arange(128)
    half = lane % 64
    six = half % 6 == np.arange(6)[:, None]
    four = lane % 4 == np.arange(4)[:, None]
    place = np.zeros((14, 128), np.float32)
    place[0:6], place[8:14] = six, lane // 4 == 3 + np.arange(6)[:, None]
    masks = [half // 6 == p for p in range(6)] + [lane // 6 == p for p in range(2)]
    masks += [(lane >= 12) & (lane < 36) & four[e] for e in range(4)]
    three = lane % 3 == np.arange(3)[:, None]
    ends = np.zeros((24, 128), np.float32)
    ends[0:6], ends[8:11], ends[19:22] = lane % 6 == np.arange(6)[:, None], three, three
    fours = (lane + 2) % 4 == np.arange(4)[:, None]
    ones = np.zeros((640, 768), np.float32)
    ones[0:192] = spread.reshape(192, 768)
    ones[192:576, 0:512] = select
    ones[576:608, 0:512], ones[608:640, 0:512] = row12.T, row13.T
    spots = np.concatenate([np.stack(rows), step, np.stack(back)]).astype(np.int32)
    last = np.zeros((32, 128), np.float32)
    last[0:24], last[24:28] = ends, fours
    first = np.zeros((48, 128), np.float32)
    first[0:14], first[16:28], first[32:48, 0:12] = place, np.stack(masks), pads
    return ones, spots, last, first


ONES, SPOTS, LAST, FIRST = layout_tables()
SELECT = (slice(192, 576), slice(0, 512))


def spread_of(ones, i):
    return ones[64 * i : 64 * i + 64, :]


def matmul(left, right):
    return jnp.dot(left, right, preferred_element_type=F32)


def matmul_nt(left, right):
    return lax.dot_general(left, right, NT, preferred_element_type=F32)


def matmul_tn(left, right):
    return lax.dot_general(left, right, TN, preferred_element_type=F32)


def allowed_pairs(clip, qb, j):
    pos = first_key() + j * 512 + lax.broadcasted_iota(jnp.int32, (512, 256), 0)
    return (pos >= clip[qb, 0:1, :]) & (pos < clip[qb, 1:2, :])


def first_key():
    return (lax.axis_index("dp") // 2 - 3) * 512


def key_blocks(ends, qb):
    first = (ends[qb, 0, 0] - first_key()) // 512
    return first, (ends[qb, 1, 255] - first_key() + 511) // 512


def front_kernel(
    ends, clip, w, ones, spots, tk,
    vecs, w_attn, unit, kv, q, of, lse, attn,
):
    line = lax.broadcasted_iota(jnp.int32, (128, 768), 0)
    k = lax.axis_index("dp") % 2
    row12, row13 = [
        jnp.concatenate(
            [matmul(ones[576 + 32 * i : 608 + 32 * i, 0:512], w[z, :, 0:128]) for z in range(2)]
        ).astype(BF)
        for i in range(2)
    ]
    wide = matmul_tn(row12, spread_of(ones, 0))
    for p in range(6):
        hit = line == spots[p : p + 1, :]
        vecs[p : p + 1, :] = jnp.sum(jnp.where(hit, wide, 0.0), axis=0, keepdims=True)
    for p in (6, 7):
        wide = matmul_tn(row13, spread_of(ones, p - 5))
        hit = line == spots[p : p + 1, :] + k * spots[p + 8 : p + 9, :]
        vecs[p : p + 1, :] = jnp.sum(jnp.where(hit, wide, 0.0), axis=0, keepdims=True)
    for z in range(2):
        w_attn[z * 384 : z * 384 + 384, :] = matmul(ones[SELECT], w[z]).astype(BF)

    def norm_rows(j):
        v = tk[j].astype(F32)
        centred = v - jnp.mean(v, axis=-1, keepdims=True)
        spread_out = jnp.mean(centred * centred, axis=-1, keepdims=True)
        u = centred * lax.rsqrt(spread_out + EPS)
        return u, (u * vecs[0:1, :] + vecs[2:3, :]).astype(BF)

    bounds = [key_blocks(ends, qb) for qb in range(2)]

    @pl.loop(bounds[0][0], bounds[1][1])
    def _(j):
        u, a = norm_rows(j)
        unit[j] = u.astype(BF)
        kv[j] = (matmul(a, w_attn[:, 0:384]) + vecs[6:7, 0:384]).astype(BF)

    low = (lax.broadcasted_iota(jnp.int32, (512, 384), 1) & 127) < 64
    _, a = norm_rows(3)
    v = (matmul(a, w_attn[:, 384:768]) + vecs[6:7, 384:768]).astype(BF).astype(F32)
    q[...] = jnp.where(low, v * SCORE_SCALE, 0.0).astype(BF)

    lane = lax.broadcasted_iota(jnp.int32, (256, 128), 1)
    for qb in range(2):
        rows = slice(qb * 256, qb * 256 + 256)

        def step(j, carry):
            ok = allowed_pairs(clip, qb, j)
            keys = [kv[j, :, h * 128 : h * 128 + 128] for h in range(3)]
            scores = [
                jnp.where(ok, matmul_nt(keys[h], q[rows, h * 128 : h * 128 + 128]), NEGATIVE)
                for h in range(3)
            ]
            tops = [
                jnp.maximum(carry[h][0], jnp.max(scores[h], axis=0, keepdims=True))
                for h in range(3)
            ]
            probs = [jnp.exp(scores[h] - tops[h]) for h in range(3)]
            new = []
            for h in range(3):
                m, l, acc = carry[h]
                fade = jnp.exp(m - tops[h])
                l = l * fade + jnp.sum(probs[h], axis=0, keepdims=True)
                acc = acc * fade + matmul_tn(keys[h], probs[h].astype(BF))
                new.append((tops[h], l, acc))
            return tuple(new)

        start = tuple(
            (
                jnp.full((1, 256), NEGATIVE, F32),
                jnp.zeros((1, 256), F32),
                jnp.zeros((128, 256), F32),
            )
            for _ in range(3)
        )
        final = lax.fori_loop(bounds[qb][0], bounds[qb][1], step, start)
        for h in range(3):
            m, l, acc = final[h]
            o = (acc / l).T
            of[rows, h * 128 : h * 128 + 128] = jnp.where(lane >= 64, o, 0.0)
            lse[h : h + 1, rows] = m + jnp.log(l)
        attn[rows, :] = matmul_nt(of[rows, :].astype(BF), w_attn[:, 384:768]).astype(BF)


def front(*args):
    return pl.pallas_call(
        front_kernel,
        out_shape=[
            jax.ShapeDtypeStruct((8, 768), F32),
            jax.ShapeDtypeStruct((768, 768), BF),
            jax.ShapeDtypeStruct((7, 512, 768), BF),
            jax.ShapeDtypeStruct((7, 512, 384), BF),
            jax.ShapeDtypeStruct((512, 384), BF),
            jax.ShapeDtypeStruct((512, 384), F32),
            jax.ShapeDtypeStruct((3, 512), F32),
            jax.ShapeDtypeStruct((512, 768), BF),
        ],
        in_specs=[SM] + [VM] * 5,
        out_specs=[VM] * 8,
        compiler_params=pltpu.CompilerParams(vmem_limit_bytes=16 * 2**20),
        name="front",
    )(*args)


def back_kernel(
    ends, clip, q, dr, of, kv, lse, unit, w_attn, vecs, sums, up_sum, ones, spots,
    d_out, grad, total, dox, delta, dq, ug,
):
    bounds = [key_blocks(ends, qb) for qb in range(2)]
    lane = lax.broadcasted_iota(jnp.int32, (256, 128), 1)
    high = (lax.broadcasted_iota(jnp.int32, (256, 384), 1) & 127) >= 64

    @pl.loop(0, 7)
    def _(j):
        total[j] = jnp.zeros((512, 384), F32)
        d_out[j] = jnp.zeros((512, 768), BF)

    for qb in range(2):
        rows = slice(qb * 256, qb * 256 + 256)
        g = jnp.where(high, matmul(dr[rows, :], w_attn[:, 384:768]), 0.0).astype(BF)
        dox[rows, :] = g
        prod = g.astype(F32) * of[rows, :]
        for h in range(3):
            part = prod[:, h * 128 : h * 128 + 128].T
            delta[h : h + 1, rows] = jnp.sum(part, axis=0, keepdims=True)

    for qb in range(2):
        rows = slice(qb * 256, qb * 256 + 256)

        def step(j, carry):
            ok = allowed_pairs(clip, qb, j)
            cols = [slice(h * 128, h * 128 + 128) for h in range(3)]
            keys = [kv[j, :, n] for n in cols]
            scores = [jnp.where(ok, matmul_nt(keys[h], q[rows, cols[h]]), NEGATIVE) for h in range(3)]
            grads = [matmul_nt(keys[h], dox[rows, cols[h]]) for h in range(3)]
            probs = [jnp.exp(scores[h] - lse[h : h + 1, rows]) for h in range(3)]
            ds = [(probs[h] * (grads[h] - delta[h : h + 1, rows])).astype(BF) for h in range(3)]
            for h in range(3):
                total[j, :, cols[h]] += matmul(ds[h], q[rows, cols[h]]) + matmul(
                    probs[h].astype(BF), dox[rows, cols[h]]
                )
            return tuple(carry[h] + matmul_tn(keys[h], ds[h]) for h in range(3))

        start = tuple(jnp.zeros((128, 256), F32) for _ in range(3))
        final = lax.fori_loop(bounds[qb][0], bounds[qb][1], step, start)
        for h in range(3):
            part = jnp.where(lane < 64, SCORE_SCALE * final[h].T, 0.0)
            dq[rows, h * 128 : h * 128 + 128] = part.astype(BF)

    ug[...] = jnp.zeros((768, 768), F32)

    def chunk(j, kv_sum):
        z = total[j].astype(BF)
        d_out[j] = matmul_nt(z, w_attn[:, 0:384]).astype(BF)
        ug[:, 0:384] += matmul_tn(unit[j], z)
        return kv_sum + jnp.sum(z.astype(F32), axis=0, keepdims=True)

    kv_sum = lax.fori_loop(bounds[0][0], bounds[1][1], chunk, jnp.zeros((1, 384), F32))
    own = matmul_nt(total[3].astype(BF), w_attn[:, 0:384])
    d_out[3] = (own + matmul_nt(dq[...], w_attn[:, 384:768])).astype(BF)
    ug[:, 384:768] = matmul_tn(unit[3], dq[...])
    q_sum = jnp.sum(dq[...].astype(F32), axis=0, keepdims=True)
    z_sum = jnp.concatenate([kv_sum, q_sum], axis=1)

    line = lax.broadcasted_iota(jnp.int32, (128, 768), 0)

    def place(p, row):
        return jnp.where(line == spots[p + 16 : p + 17, :], row, 0.0)

    columns = vecs[...].T
    gain_col, offset_col = columns[:, 0:1], columns[:, 2:3]
    w_full = w_attn[...].astype(F32)
    gain_sum = jnp.sum(ug[...] * w_full, axis=1, keepdims=True)
    offset_sum = jnp.sum(w_full * z_sum, axis=1, keepdims=True)
    flip = lax.broadcasted_iota(jnp.int32, (768, 128), 1)
    both = jnp.where(flip == 0, gain_sum, jnp.where(flip == 1, offset_sum, 0.0)).T
    own = place(0, both[0:1, :]) + place(2, both[1:2, :])
    for i, p in enumerate((1, 3, 4, 5)):
        own = own + place(p, sums[i : i + 1, :])
    small = matmul_nt(spread_of(ones, 0), own.astype(BF))
    small += matmul_nt(spread_of(ones, 1), place(6, z_sum).astype(BF))
    small += matmul_nt(spread_of(ones, 2), place(7, up_sum[...]).astype(BF))
    small = small.astype(BF)

    ug[...] = ug[...] * gain_col + offset_col * z_sum
    ug[:, 384:768] += matmul_tn(dr[...], of[...].astype(BF))
    for i in range(2):
        g = matmul_tn(ones[SELECT], ug[i * 384 : i * 384 + 384, :].astype(BF))
        grad[i] = g.astype(BF)
        extra = matmul_tn(ones[576:608, 0:512], small[i * 32 : i * 32 + 32, :])
        grad[i, :, 0:128] = (g[:, 0:128] + extra).astype(BF)


def back(*args):
    return pl.pallas_call(
        back_kernel,
        out_shape=[
            jax.ShapeDtypeStruct((7, 512, 768), BF),
            jax.ShapeDtypeStruct((2, 512, 768), BF),
        ],
        in_specs=[SM] + [VM] * (len(args) - 1),
        out_specs=[VM, VM],
        scratch_shapes=[
            pltpu.VMEM((7, 512, 384), F32),
            pltpu.VMEM((512, 384), BF),
            pltpu.VMEM((3, 512), F32),
            pltpu.VMEM((512, 384), BF),
            pltpu.VMEM((768, 768), F32),
        ],
        compiler_params=pltpu.CompilerParams(vmem_limit_bytes=22 * 2**20),
        name="back",
    )(*args)


def finish_kernel(
    own, far, back_one, e1, tok, vecs, ends,
    tokens, g_in, g_qv, g_out, g_up, g_fc, g_down, g_gain, g_row,
):
    t = lax.axis_index("tensor")
    hidden = tok[...].astype(F32)
    centred = hidden - jnp.mean(hidden, axis=-1, keepdims=True)
    scale = lax.rsqrt(jnp.mean(centred * centred, axis=-1, keepdims=True) + EPS)
    unit = centred * scale
    w = back_one[...] * vecs[0:1, :]
    mean_w = jnp.mean(w, axis=-1, keepdims=True)
    mean_wu = jnp.mean(w * unit, axis=-1, keepdims=True)
    tokens[...] = e1[...] + scale * (w - mean_w - unit * mean_wu)

    exact = dict(precision=lax.Precision.HIGHEST, preferred_element_type=F32)
    for n in range(3):
        cols = slice(n * 128, n * 128 + 128)
        parts = []
        for head in (2 * n, 2 * n + 1):
            q, h = head // 3, head % 3
            parts.append(
                (own[q, :, 384 + h * 128 : 512 + h * 128], own[q, :, h * 128 : h * 128 + 128])
            )
        (qo_a, kv_a), (qo_b, kv_b) = parts
        g_in[0, :, 0, cols] = jnp.concatenate([qo_a[:, 0:64], qo_b[:, 0:64]], axis=1)[0:12]
        g_in[1, :, 0, cols] = jnp.concatenate([kv_a[:, 0:64], kv_b[:, 0:64]], axis=1)[0:12]
        g_in[2, :, 0, cols] = jnp.concatenate([kv_a[:, 64:128], kv_b[:, 64:128]], axis=1)[0:12]
        mixed = jnp.concatenate([qo_a[:, 64:128], qo_b[:, 64:128]], axis=1)
        g_out[:, 0, cols] = mixed[0:12]
    for q in range(2):
        cols = slice(q * 768, q * 768 + 768)
        g_up[:, 0, cols] = own[q, 0:12, 768:1536]
        g_down[:, 0, cols] = own[q, 0:12, 1536:2304]
    row0, row1 = own[0, 12:13, 0:128], own[1, 12:13, 0:128]
    vec = row0 + row1 + far[12:13, :]
    lane = lax.broadcasted_iota(jnp.int32, (8, 128), 1)
    line = lax.broadcasted_iota(jnp.int32, (8, 128), 0)

    def pick(row, start, width, stride):
        begin = start + line * stride
        return jnp.where((lane >= begin) & (lane < begin + width), row, 0.0)

    norms = lax.dot_general(pick(vec, 6 * t, 6, 12), ends[0:6, :], NT, **exact)
    g_gain[...] = norms[0:2]
    g_row[...] = norms[2:6]
    heads = lax.dot_general(pick(row0, 72, 3, 3), ends[8:14, :], NT, **exact)
    heads += lax.dot_general(pick(row1, 72, 3, 3), ends[16:22, :], NT, **exact)
    g_qv[...] = heads[0:2]
    hidden_rows = jnp.where(line < 3, pick(row0, 78, 4, 4), pick(row1, 66, 4, 4))
    g_fc[...] = lax.dot_general(ends[24:28, :], hidden_rows, NT, **exact)[:, 0:6]


def finish(*args):
    return pl.pallas_call(
        finish_kernel,
        out_shape=[
            jax.ShapeDtypeStruct(dims, F32)
            for dims in (
                (128, 768),
                (3, 12, 1, 384),
                (2, 6),
                (12, 1, 384),
                (12, 1, 1536),
                (4, 6),
                (12, 1, 1536),
                (2, 6),
                (4, 6),
            )
        ],
        in_specs=[VM] * len(args),
        out_specs=[VM] * 9,
        compiler_params=pltpu.CompilerParams(vmem_limit_bytes=16 * 2**20),
        name="finish",
    )(*args)


def body(
    tokens,
    clip_bounds,
    attn_in,
    qv_bias,
    out_proj,
    fc_in,
    fc_bias,
    fc_out,
    ln_gain,
    row_bias,
    cotangent,
):
    w, f0, f1, clip, near_tokens, tokens, cotangent, ones, spots, last = gather_all(
        clip_bounds,
        tokens,
        cotangent,
        attn_in[0],
        out_proj[0].T,
        fc_in[0],
        fc_out[0].T,
        ln_gain[0],
        row_bias[0],
        qv_bias.reshape(2, 6),
        fc_bias[0].T,
        jnp.asarray(FIRST),
        jnp.asarray(ONES, BF),
        jnp.asarray(SPOTS),
        jnp.asarray(LAST),
    )
    vecs, w_attn, unit, near, query, mixed, lse, attn = front(
        clip, clip, w.reshape(2, 512, 768), ones, spots, near_tokens.reshape(7, 512, 768)
    )
    output, grad_hidden_one, full_attn, sums, up_sum, s0, s1 = mid(
        attn.reshape(4, 128, 768), f0, f1, cotangent, tokens, vecs, ones
    )
    near_back, grad_w = back(
        clip,
        clip,
        query,
        full_attn.reshape(512, 768),
        mixed,
        near,
        lse,
        unit,
        w_attn,
        vecs,
        sums,
        up_sum,
        ones,
        spots,
    )
    back_one, own, far = return_all(
        near_back.reshape(7, 4, 128, 768), grad_w.reshape(2, 4, 4, 2, 16, 768), s0, s1
    )
    grads = finish(
        own, far, back_one, grad_hidden_one, tokens, vecs, last
    )
    grad_tokens, g_in, g_qv, g_out, g_up, g_fc, g_down, g_gain, g_row = grads
    return (
        output,
        grad_tokens,
        g_in.reshape(1, 3, 12, 384),
        g_qv.reshape(1, 2, 6, 1),
        g_out.reshape(12, 384).T[None],
        g_up.reshape(1, 12, 1536),
        g_fc.T[None],
        g_down.reshape(12, 1536).T[None],
        g_gain[None],
        g_row[None],
    )


def solution(mesh):
    return jax.shard_map(
        body,
        mesh=mesh,
        in_specs=(
            P(("dp", "tensor"), None),
            P(None, "dp"),
            P(None, None, "dp", "tensor"),
            P(None, None, "tensor", "dp"),
            P(None, "tensor", "dp"),
            P(None, "dp", "tensor"),
            P(None, "tensor", "dp"),
            P(None, "tensor", "dp"),
            P(None, None, ("dp", "tensor")),
            P(None, None, ("dp", "tensor")),
            P(("dp", "tensor"), None),
        ),
        out_specs=(
            P(("dp", "tensor"), None),
            P(("dp", "tensor"), None),
            P(None, None, "dp", "tensor"),
            P(None, None, "tensor", "dp"),
            P(None, "tensor", "dp"),
            P(None, "dp", "tensor"),
            P(None, "tensor", "dp"),
            P(None, "tensor", "dp"),
            P(None, None, ("dp", "tensor")),
            P(None, None, ("dp", "tensor")),
        ),
        check_vma=False,
    )
```

```python
import jax
import jax.numpy as jnp
import numpy as np
from jax import lax
import jax.experimental.pallas as pl
import jax.experimental.pallas.tpu as pltpu
from jax.sharding import PartitionSpec as P

EPS = 1e-05
NEGATIVE = -1e30
SCORE_SCALE = 0.125
BF = jnp.bfloat16
F32 = jnp.float32
MESH = pl.DeviceIdType.MESH
VM = pl.BlockSpec(memory_space=pltpu.VMEM)
SM = pl.BlockSpec(memory_space=pltpu.SMEM)
DMA = pltpu.SemaphoreType.DMA
NT = (((1,), (1,)), ((), ()))
TN = (((0,), (0,)), ((), ()))


def coords():
    dp = lax.axis_index("dp")
    return dp // 32, (dp // 8) % 4, (dp // 2) % 4, dp % 2, lax.axis_index("tensor")


def device(z, y, x, k, t):
    return (((z * 4 + y) * 4 + x) * 2 + k, t)


def chip(c, k, t):
    return (c * 2 + k, t)


def greet(peers):
    bar = pltpu.get_barrier_semaphore()
    for peer in peers:
        pl.semaphore_signal(bar, inc=1, device_id=peer, device_id_type=MESH)
    pl.semaphore_wait(bar, len(peers))


def remote(src, dst, sems, index, peer):
    send, recv = sems
    return pltpu.make_async_remote_copy(
        src, dst, send.at[index], recv.at[index], device_id=peer, device_id_type=MESH
    )


def comm_call(kernel, out_shape, scratch, cid, name, args, room, place=VM):
    single = not isinstance(out_shape, (list, tuple))
    return pl.pallas_call(
        kernel,
        out_shape=out_shape,
        in_specs=[place] * len(args),
        out_specs=VM if single else [VM] * len(out_shape),
        scratch_shapes=scratch,
        compiler_params=pltpu.CompilerParams(
            collective_id=cid, has_side_effects=True, vmem_limit_bytes=room * 2**20
        ),
        name=name,
    )(*args)


def neighbours():
    z, y, x, k, t = coords()
    xs = [device(z, y, (x + d) % 4, k, t) for d in (1, 2, 3)]
    ys = [device(z, (y + d) % 4, x, k, t) for d in (1, 2, 3)]
    core = device(z, y, x, 1 - k, t)
    far = device(z, y, x, k, 1 - t)
    low = device(1 - z, y, x, k, t)
    ring = [chip(((z * 4 + y) * 4 + x + d) % 32, k, t) for d in RING]
    return (z, y, x, k, t), xs, ys, core, far, low, ring


RING = (2, -2, 3, -3, 1, -1)


class Copies:
    def __init__(self, send, recv):
        self.sems, self.count = (send, recv), 0

    def __call__(self, src, dst, peer):
        made = remote(src, dst, self.sems, self.count, peer)
        self.count += 1
        made.start()
        return made


def build_small(gain, row, qv, fc, first, t, tile):
    place = first[0:14, :].astype(BF)
    masks = first[16:28, :]

    norms = jnp.sum(matmul(gain[...], place[0:6, :]) * masks[0:2, :], axis=0, keepdims=True)
    norms += jnp.sum(matmul(row[...], place[0:6, :]) * masks[2:6, :], axis=0, keepdims=True)
    lane = lax.broadcasted_iota(jnp.int32, (16, 128), 1)
    line = lax.broadcasted_iota(jnp.int32, (16, 128), 0)
    others = jnp.sum(matmul(qv[...], place[0:6, :]) * masks[6:8, :], axis=0, keepdims=True)
    others += jnp.sum(matmul(fc[...], place[8:14, :]) * masks[8:12, :], axis=0, keepdims=True)
    mine = (line == 12) & (lane >= 64 * t) & (lane < 64 * t + 64)
    small = jnp.where(mine, norms, 0.0)
    tile[...] = small.astype(BF)
    return small + jnp.where(line == 13, others, 0.0)


def build_rows(attn_w, proj, up, down, small, first, pay):
    pads = first[32:48, 0:12].astype(BF)

    def tall(v):
        return matmul(pads, v)

    query, keys, values = [tall(attn_w[i]) for i in range(3)]
    mixed, up_rows, down_rows = tall(proj[...]), tall(up[...]), tall(down[...])
    for q in range(2):
        for h in range(3):
            n = slice((q * 3 + h) * 64, (q * 3 + h) * 64 + 64)
            pair = jnp.concatenate([keys[:, n], values[:, n]], axis=1)
            if h == 0:
                pair = pair + small
            pay[q, :, h * 128 : h * 128 + 128] = pair.astype(BF)
            pair = jnp.concatenate([query[:, n], mixed[:, n]], axis=1)
            pay[q, :, 384 + h * 128 : 512 + h * 128] = pair.astype(BF)
        pay[q, :, 768:1536] = up_rows[:, q * 768 : q * 768 + 768].astype(BF)
        pay[q, :, 1536:2304] = down_rows[:, q * 768 : q * 768 + 768].astype(BF)


H0, H1 = pl.ds(0, 512), pl.ds(512, 256)


def gather_kernel(
    clip, tok, cot, attn_h, proj_h, up_h, down_h, gain_h, row_h, qv_h, fc_h, first_h,
    ones_h, spots_h, last_h,
    w, f0, f1, clip_out, tk, tok_out, cot_out, ones, spots, last,
    attn_w, proj, up, down, gain, row, qv, fc, first,
    pay_s, tile, tile_in, ws, send, recv, local,
):
    stages = []

    def stage(src, dst):
        stages.append(pltpu.make_async_copy(src, dst, local.at[len(stages)]))
        stages[-1].start()

    for src, dst in (
        (gain_h, gain), (row_h, row), (qv_h, qv), (fc_h, fc), (first_h, first),
        (attn_h, attn_w), (proj_h, proj), (up_h, up), (down_h, down),
    ):
        stage(src, dst)
    (z, y, x, k, t), xs, ys, core, far, low, ring = neighbours()
    copy = Copies(send, recv)
    mine, other = k * 2 + t, k * 2 + 1 - t
    both = device(z, y, x, 1 - k, 1 - t)
    greet(xs + ys + [core, far, both, low] + ring)
    own_far = copy(tok, tk.at[3, mine], far)
    order = (4, 5, 2, 3, 0, 1)
    pushes = {i: copy(tok, tk.at[3 - RING[i], mine], ring[i]) for i in order}
    done = [copy(tok, tk.at[3, mine], core), copy(clip, clip_out.at[k], core)]
    stage(tok, tk.at[3, mine])
    stage(clip, clip_out.at[k])
    for pair in ((tok, tok_out), (cot, cot_out), (ones_h, ones), (spots_h, spots), (last_h, last)):
        stage(*pair)
    for c in stages[0:9]:
        c.wait()
    small = build_small(gain, row, qv, fc, first, t, tile)
    c_tile = [copy(tile, tile_in.at[0], far), copy(tile, tile_in.at[1], both)]
    build_rows(attn_w, proj, up, down, small, first, pay_s)
    to_far = {}

    def to_core(slot, which):
        done.append(copy(tk.at[slot, which], tk.at[slot, which], core))

    def pass_on(i):
        pushes[i].wait_recv()
        slot = 3 - RING[i]
        to_far[i] = copy(tk.at[slot, mine], tk.at[slot, mine], far)
        to_core(slot, mine)

    swap = copy(pay_s.at[1 - k], ws.at[z, k], core)
    ws[z, k] = pay_s[k]
    for i in (4, 5):
        pushes[i].wait_recv()
        to_core(3 - RING[i], mine)
    swap.wait()
    for c in c_tile:
        c.wait()
    ws[z, k, :, 0:128] = ws[z, k, :, 0:128] + tile_in[0]
    ws[z, 1 - k, :, 0:128] = ws[z, 1 - k, :, 0:128] + tile_in[1]
    c_low = copy(ws.at[z], ws.at[z], low)
    pass_on(2)
    pass_on(3)
    c_low.wait()
    w[:, y, x] = ws[:, :, :, 0:768]
    f0[:, x] = ws[:, :, :, 768:1536]
    f1[:, y] = ws[:, :, :, 1536:2304]
    phase = []
    for i in range(3):
        phase.append(copy(ws.at[:, :, :, H0], w.at[:, y, x, :, :, H0], xs[i]))
        phase.append(copy(ws.at[:, :, :, H1], w.at[:, y, x, :, :, H1], ys[i]))
    pass_on(0)
    pass_on(1)
    own_far.wait_recv()
    beyond = []
    for i in (4, 5):
        slot = 3 - RING[i]
        beyond.append((slot, copy(tk.at[3, other], tk.at[slot, other], ring[i])))
    to_core(3, other)
    for c in phase:
        c.wait()
    rest = []
    for i in range(3):
        a = w.at[:, y, :, :, :, H0]
        rest.append(copy(a, a, ys[i]))
        b = w.at[:, :, x, :, :, H1]
        rest.append(copy(b, b, xs[i]))
    for i in range(3):
        rest.append(copy(ws.at[:, :, :, pl.ds(768, 768)], f0.at[:, x], xs[i]))
        rest.append(copy(ws.at[:, :, :, pl.ds(1536, 768)], f1.at[:, y], ys[i]))
    for i in (2, 3, 0, 1):
        to_far[i].wait_recv()
        to_core(3 - RING[i], other)
    for slot, c in beyond:
        c.wait_recv()
        to_core(slot, other)
        c.wait_send()
    for i in order:
        pushes[i].wait_send()
    for i in (2, 3, 0, 1):
        to_far[i].wait_send()
    own_far.wait_send()
    for c in rest + done + stages[9:]:
        c.wait()


def gather_all(*args):
    return comm_call(
        gather_kernel,
        [
            jax.ShapeDtypeStruct((2, 4, 4, 2, 16, 768), BF),
            jax.ShapeDtypeStruct((2, 4, 2, 16, 768), BF),
            jax.ShapeDtypeStruct((2, 4, 2, 16, 768), BF),
            jax.ShapeDtypeStruct((2, 2, 256), jnp.int32),
            jax.ShapeDtypeStruct((7, 4, 128, 768), BF),
            jax.ShapeDtypeStruct((128, 768), BF),
            jax.ShapeDtypeStruct((128, 768), BF),
            jax.ShapeDtypeStruct((640, 768), BF),
            jax.ShapeDtypeStruct((24, 768), jnp.int32),
            jax.ShapeDtypeStruct((32, 128), F32),
        ],
        [pltpu.VMEM(v.shape, v.dtype) for v in args[3:12]]
        + [
            pltpu.VMEM((2, 16, 2304), BF),
            pltpu.VMEM((16, 128), BF),
            pltpu.VMEM((2, 16, 128), BF),
            pltpu.VMEM((2, 2, 16, 2304), BF),
            DMA((50,)),
            DMA((50,)),
            DMA((16,)),
        ],
        0,
        "gather_first",
        args,
        54,
        pl.BlockSpec(memory_space=pltpu.MemorySpace.HBM),
    )


def exchange_rows(copy, a, out, k, t, core, far):
    mine, other = k * 2 + t, k * 2 + 1 - t
    c_far = copy(a, out.at[mine], far)
    c_core = copy(a, out.at[mine], core)
    out[mine] = a[...]

    def finish():
        c_far.wait_recv()
        c_pass = copy(out.at[other], out.at[other], core)
        c_far.wait_send()
        c_core.wait()
        c_pass.wait()

    return finish


def spread_over_y(copy, g0, b0, y, ys):
    return [copy(g0.at[:, (y + i + 1) % 4], b0.at[i], ys[i]) for i in range(3)]


def spread_over_x(copy, g1, b1, x, xs):
    return [copy(g1.at[:, :, (x + i + 1) % 4], b1.at[i], xs[i]) for i in range(3)]


def spread_first(copy, g0, g1, b0, b1, x, y, xs, ys):
    return spread_over_y(copy, g0, b0, y, ys), spread_over_x(copy, g1, b1, x, xs)


def add_first(g0, g1, b0, b1, s0, s1, x, y, over_y, over_x):
    for c in over_y:
        c.wait()

    @pl.loop(0, 8)
    def _(n):
        zz, m = n // 4, n % 4
        v = g0[zz, y, m].astype(F32)
        for i in range(3):
            v = v + b0[i, zz, m].astype(F32)
        s0[zz, m] = v.astype(BF)

    for c in over_x:
        c.wait()

    @pl.loop(0, 8)
    def _(n):
        zz, m = n // 4, n % 4
        v = g1[zz, m, x].astype(F32)
        for i in range(3):
            v = v + b1[i, zz, m].astype(F32)
        s1[zz, m] = v.astype(BF)


def spread_second(copy, s0, s1, a0, a1, x, y, xs, ys):
    over_x, over_y = [], []
    for i in range(3):
        over_x.append(copy(s0.at[:, (x + i + 1) % 4], a0.at[i], xs[i]))
        over_y.append(copy(s1.at[:, (y + i + 1) % 4], a1.at[i], ys[i]))
    return over_x, over_y


def add_second(s0, s1, a0, a1, u0, u1, x, y, over_x, over_y):
    for c in over_x + over_y:
        c.wait()
    for zz in range(2):
        v = s0[zz, x].astype(F32)
        v1 = s1[zz, y].astype(F32)
        for i in range(3):
            v = v + a0[i, zz].astype(F32)
            v1 = v1 + a1[i, zz].astype(F32)
        u0[zz] = v.astype(BF)
        u1[zz] = v1.astype(BF)


HALVES = (slice(0, 64), slice(64, 128))


def unit_rows(hidden):
    centred = hidden - jnp.mean(hidden, axis=-1, keepdims=True)
    scale = lax.rsqrt(jnp.mean(centred * centred, axis=-1, keepdims=True) + EPS)
    return centred * scale, scale


def mid_kernel(
    p, f0, f1, cot, tok, vecs, ones,
    output, e1, dr_full, sums, up_sum, s0, s1,
    got, mid, got_far, p0, p1, w_up, w_down, b_full, cot_full, dg, active, du_full,
    pr, got_two, mid_two, far_two, grad_one, g0, g1, b0, b1, send, recv,
):
    (z, y, x, k, t), xs, ys, core, far, low, ring = neighbours()
    copy = Copies(send, recv)
    greet(xs + ys + [core, far])
    mine, across, beside, both = k * 2 + t, k * 2 + 1 - t, 2 - 2 * k + t, 3 - 2 * k - t
    to_core = copy(p.at[pl.ds((1 - k) * 2, 2)], got, core)
    finish_cot = exchange_rows(copy, cot, cot_full, k, t, core, far)
    made = []
    for i in range(2):
        for j in range(3):
            made.append(copy(f0.at[i], p0.at[i, y], ys[j]))
            made.append(copy(f1.at[i], p1.at[i, :, x], xs[j]))
        p0[i, y] = f0[i]
        p1[i, :, x] = f1[i]
    to_core.wait()
    to_far, rows_far, rows_core = [], [], []
    for rows in HALVES:
        part = p[across, rows].astype(F32) + got[1 - t, rows].astype(F32)
        mid[rows] = part.astype(BF)
        to_far.append(copy(mid.at[rows], got_far.at[rows], far))
    for i, rows in enumerate(HALVES):
        part = p[mine, rows].astype(F32) + got[t, rows].astype(F32)
        part = part + tok[rows].astype(F32) + vecs[3:4, :]
        to_far[i].wait()
        hidden = part + got_far[rows].astype(F32)
        unit, _ = unit_rows(hidden)
        b_full[mine, rows] = (unit * vecs[1:2, :] + vecs[4:5, :]).astype(BF)
        here = b_full.at[mine, rows]
        rows_far.append(copy(here, here, far))
        rows_core.append(copy(here, here, core))
        e1[rows] = hidden
    finish_cot()
    for c in made:
        c.wait()
    for i in range(2):
        rows = slice(i * 384, i * 384 + 384)
        w_up[rows, :] = matmul(ones[SELECT], p0[i].reshape(512, 768)).astype(BF)
        w_down[rows, :] = matmul(ones[SELECT], p1[i].reshape(512, 768)).astype(BF)

    @pl.loop(0, 4)
    def _(i):
        dg[i] = matmul(cot_full[i], w_down[...])

    up_sum[...] = jnp.zeros((1, 768), F32)

    def feed(i):
        u = matmul(b_full[i], w_up[...]) + vecs[7:8, :]
        phi = 0.5 + 0.5 * lax.erf(u * 0.7071067811865476)
        gl = (u * phi).astype(BF)
        active[i] = gl
        pr[0, i] = matmul_nt(gl, w_down[...]).astype(BF)
        slope = phi + u * jnp.exp(-0.5 * u * u) * 0.3989422804014327
        du = (dg[i] * slope).astype(BF)
        du_full[i] = du
        up_sum[...] += jnp.sum(du.astype(F32), axis=0, keepdims=True)
        pr[1, i] = matmul_nt(du, w_up[...]).astype(BF)

    feed(mine)
    for c in rows_core:
        c.wait()
    feed(beside)
    first = copy(pr.at[:, beside], got_two.at[:, t], core)
    rows_pass = []
    for i, rows in enumerate(HALVES):
        rows_far[i].wait()
        rows_pass.append(copy(b_full.at[across, rows], b_full.at[across, rows], core))
    feed(across)
    for c in rows_pass:
        c.wait()
    feed(both)
    second = copy(pr.at[:, both], got_two.at[:, 1 - t], core)
    second.wait()
    for i in range(2):
        v = pr[i, across].astype(F32) + got_two[i, 1 - t].astype(F32)
        mid_two[i] = v.astype(BF)
    back_far = [copy(mid_two.at[1, rows], far_two.at[1, rows], far) for rows in HALVES]
    c_rows, a_rows = cot_full[...].reshape(512, 768), active[...].reshape(512, 768)
    for i in range(2):
        cols = slice(i * 384, i * 384 + 384)
        g = matmul_tn(c_rows[:, cols], a_rows).astype(BF)
        g1[i] = matmul_tn(ones[SELECT], g).astype(BF).reshape(4, 4, 2, 16, 768)
    over_x = spread_over_x(copy, g1, b1, x, xs)
    b_rows, du_rows = b_full[...].reshape(512, 768), du_full[...].reshape(512, 768)
    for i in range(2):
        cols = slice(i * 384, i * 384 + 384)
        g = matmul_tn(b_rows[:, cols], du_rows).astype(BF)
        g0[i] = matmul_tn(ones[SELECT], g).astype(BF).reshape(4, 4, 2, 16, 768)
    over = spread_over_y(copy, g0, b0, y, ys), over_x
    first.wait()

    sums[...] = jnp.zeros((4, 768), F32)
    dr_far, dr_core = [], []
    for i, rows in enumerate(HALVES):
        back_rows = pr[1, mine, rows].astype(F32) + got_two[1, t, rows].astype(F32)
        back_far[i].wait()
        back_rows = back_rows + far_two[1, rows].astype(F32)
        unit, scale = unit_rows(e1[rows])
        w = back_rows * vecs[1:2, :]
        mean_w = jnp.mean(w, axis=-1, keepdims=True)
        mean_wu = jnp.mean(w * unit, axis=-1, keepdims=True)
        cot_f = cot[rows].astype(F32)
        grad = cot_f + scale * (w - mean_w - unit * mean_wu)
        low_grad = grad.astype(BF)
        dr_full[mine, rows] = low_grad
        here = dr_full.at[mine, rows]
        dr_far.append(copy(here, here, far))
        dr_core.append(copy(here, here, core))
        grad_one[rows] = grad
        sums[0:1, :] += jnp.sum(back_rows * unit, axis=0, keepdims=True)
        sums[1:2, :] += jnp.sum(low_grad.astype(F32), axis=0, keepdims=True)
        sums[2:3, :] += jnp.sum(back_rows, axis=0, keepdims=True)
        sums[3:4, :] += jnp.sum(cot_f, axis=0, keepdims=True)
    out_far = copy(mid_two.at[0], far_two.at[0], far)
    dr_pass = []
    for i, rows in enumerate(HALVES):
        dr_far[i].wait()
        dr_pass.append(copy(dr_full.at[across, rows], dr_full.at[across, rows], core))
    part = e1[...] + pr[0, mine].astype(F32) + got_two[0, t].astype(F32) + vecs[5:6, :]
    e1[...] = grad_one[...]
    out_far.wait()
    output[...] = (part + far_two[0].astype(F32)).astype(BF)
    for c in dr_core + dr_pass:
        c.wait()
    add_first(g0, g1, b0, b1, s0, s1, x, y, *over)


def mid(p, f0, f1, cot, tok, vecs, ones):
    rows = pltpu.VMEM((128, 768), BF)
    two = pltpu.VMEM((2, 128, 768), BF)
    four = pltpu.VMEM((4, 128, 768), BF)
    square = pltpu.VMEM((768, 768), BF)
    piece = pltpu.VMEM((2, 4, 4, 2, 16, 768), BF)
    return comm_call(
        mid_kernel,
        [
            jax.ShapeDtypeStruct((128, 768), BF),
            jax.ShapeDtypeStruct((128, 768), F32),
            jax.ShapeDtypeStruct((4, 128, 768), BF),
            jax.ShapeDtypeStruct((4, 768), F32),
            jax.ShapeDtypeStruct((1, 768), F32),
            jax.ShapeDtypeStruct((2, 4, 2, 16, 768), BF),
            jax.ShapeDtypeStruct((2, 4, 2, 16, 768), BF),
        ],
        [two, rows, rows, piece, piece, square, square, four, four]
        + [pltpu.VMEM((4, 128, 768), F32), four, four]
        + [pltpu.VMEM((2, 4, 128, 768), BF), pltpu.VMEM((2, 2, 128, 768), BF), two, two]
        + [pltpu.VMEM((128, 768), F32)]
        + [piece, piece]
        + [pltpu.VMEM((3, 2, 4, 2, 16, 768), BF)] * 2
        + [DMA((41,)), DMA((41,))],
        1,
        "mid",
        (p, f0, f1, cot, tok, vecs, ones),
        26,
    )


def return_kernel(
    d, g, fs0, fs1, out, own, tile_out,
    got_core, v1, in1, e_send, got_far, r_send, got_ring,
    b0, b1, s0, s1, a0, a1, fa0, fa1, u0, u1, v_0, v_1, z_in0, z_in1, z_in2, z_in3, res, send, recv,
):
    (z, y, x, k, t), xs, ys, core, far, low, ring = neighbours()
    copy = Copies(send, recv)
    both = device(z, y, x, 1 - k, 1 - t)
    greet(xs + ys + [core, far, both, low] + ring)
    mine, across = k * 2 + t, k * 2 + 1 - t
    near = (ring[4], ring[5])
    order = (4, 2, 5, 1, 6, 0, 3)
    to_core = {j: copy(d.at[j, pl.ds((1 - k) * 2, 2)], got_core.at[j], core) for j in order}
    g0, g1 = g.at[:, :, :, :, :, H0], g.at[:, :, :, :, :, H1]
    fc_over = spread_second(copy, fs0, fs1, fa0, fa1, x, y, xs, ys)
    hop1, to_far = [], []
    over = spread_first(copy, g0, g1, b0, b1, x, y, xs, ys)
    for i, j in enumerate((4, 2)):
        to_core[j].wait()
        v1[i] = (d[j, pl.ds(k * 2, 2)].astype(F32) + got_core[j].astype(F32)).astype(BF)
        hop1.append(copy(v1.at[i], in1.at[i], near[i]))
    for i, j in enumerate(order[2:6]):
        to_core[j].wait()
        e_send[i] = (d[j, across].astype(F32) + got_core[j, 1 - t].astype(F32)).astype(BF)
        to_far.append(copy(e_send.at[i], got_far.at[i], far))
    home = []

    def send_home(i):
        j = order[2 + i]
        to_far[i].wait()
        v = d[j, mine].astype(F32) + got_core[j, t].astype(F32) + got_far[i].astype(F32)
        r_send[i] = v.astype(BF)
        home.append(copy(r_send.at[i], got_ring.at[i], ring[i]))

    add_second(fs0, fs1, fa0, fa1, u0, u1, x, y, *fc_over)
    fc_z = [copy(u0.at[1 - z], z_in0, low), copy(u1.at[1 - z], z_in1, low)]
    send_home(0)
    send_home(1)
    add_first(g0, g1, b0, b1, s0, s1, x, y, *over)
    over = spread_second(copy, s0, s1, a0, a1, x, y, xs, ys)
    to_core[3].wait()
    hop1[0].wait()
    hop1[1].wait()
    v = d[3, across].astype(F32) + got_core[3, 1 - t].astype(F32)
    v = v + in1[0, 1 - t].astype(F32) + in1[1, 1 - t].astype(F32)
    e_send[4] = v.astype(BF)
    last = copy(e_send.at[4], got_far.at[4], far)
    send_home(2)
    send_home(3)
    add_second(s0, s1, a0, a1, v_0, v_1, x, y, *over)
    attn_z = [copy(v_0.at[1 - z], z_in2, low), copy(v_1.at[1 - z], z_in3, low)]
    for c in fc_z:
        c.wait()
    res[:, :, 768:1536] = u0[z].astype(F32) + z_in0[...].astype(F32)
    res[:, :, 1536:2304] = u1[z].astype(F32) + z_in1[...].astype(F32)
    for c in attn_z:
        c.wait()
    res[:, :, H0] = v_0[z].astype(F32) + z_in2[...].astype(F32)
    res[:, :, H1] = v_1[z].astype(F32) + z_in3[...].astype(F32)
    swap = copy(res.at[1 - k], own.at[k], core)
    tiles = [
        copy(res.at[k, :, pl.ds(0, 128)], tile_out.at[0], far),
        copy(res.at[1 - k, :, pl.ds(0, 128)], tile_out.at[1], both),
    ]
    own[k] = res[k]
    total = d[3, mine].astype(F32) + got_core[3, t].astype(F32)
    total = total + in1[0, t].astype(F32) + in1[1, t].astype(F32)
    for i in range(4):
        home[i].wait()
        total = total + got_ring[i].astype(F32)
    last.wait()
    out[...] = total + got_far[4].astype(F32)
    swap.wait()
    for c in tiles:
        c.wait()


def return_all(d, g, s0, s1):
    two = pltpu.VMEM((2, 2, 128, 768), BF)
    wide, slim = 512, 256
    return comm_call(
        return_kernel,
        [
            jax.ShapeDtypeStruct((128, 768), F32),
            jax.ShapeDtypeStruct((2, 16, 2304), F32),
            jax.ShapeDtypeStruct((2, 16, 128), F32),
        ],
        [pltpu.VMEM((7, 2, 128, 768), BF), two, two]
        + [pltpu.VMEM((5, 128, 768), BF)] * 2
        + [pltpu.VMEM((4, 128, 768), BF)] * 2
        + [pltpu.VMEM((3, 2, 4, 2, 16, n), BF) for n in (wide, slim)]
        + [pltpu.VMEM((2, 4, 2, 16, n), BF) for n in (wide, slim)]
        + [pltpu.VMEM((3, 2, 2, 16, n), BF) for n in (wide, slim)]
        + [pltpu.VMEM((3, 2, 2, 16, 768), BF)] * 2
        + [pltpu.VMEM((2, 2, 16, n), BF) for n in (768, 768, wide, slim)]
        + [pltpu.VMEM((2, 16, n), BF) for n in (768, 768, wide, slim)]
        + [pltpu.VMEM((2, 16, 2304), F32), DMA((43,)), DMA((43,))],
        5,
        "return_all",
        (d, g, s0, s1),
        24,
    )


def layout_tables():
    d = np.arange(768)
    n64 = np.arange(64)[:, None]
    own = (d // 12 == n64).astype(np.float32)
    lane = d % 128
    high = d < 384
    column = np.where(high, lane - 64, lane)
    heads = ((column == n64) & (column >= 0) & (column < 64)).astype(np.float32)
    hidden = ((d % 256) // 4 == n64).astype(np.float32)
    spread = np.stack([own, heads, hidden])
    spot = 64 * ((d % 12) // 6) + d % 6
    head = (d % 384) // 128
    rows = [spot + 6 * p for p in range(6)]
    rows.append(np.where(high, 6, 0) + head)
    rows.append(12 + (d // 256) * 4 + d % 4)
    step = np.zeros((8, 768), np.int32)
    step[6], step[7] = 3, 12
    back = [12 * p + d % 12 for p in range(6)]
    back.append(72 + np.where(high, 3, 0) + head)
    back.append(78 + (d // 256) * 4 + d % 4)
    select = np.arange(512)[None, :] == (np.arange(384) // 12 * 16 + np.arange(384) % 12)[:, None]
    row12 = np.arange(512)[:, None] == np.arange(32)[None, :] * 16 + 12
    row13 = np.arange(512)[:, None] == np.arange(32)[None, :] * 16 + 13
    pads = np.arange(16)[:, None] == np.arange(12)[None, :]
    lane = np.arange(128)
    half = lane % 64
    six = half % 6 == np.arange(6)[:, None]
    four = lane % 4 == np.arange(4)[:, None]
    place = np.zeros((14, 128), np.float32)
    place[0:6], place[8:14] = six, lane // 4 == 3 + np.arange(6)[:, None]
    masks = [half // 6 == p for p in range(6)] + [lane // 6 == p for p in range(2)]
    masks += [(lane >= 12) & (lane < 36) & four[e] for e in range(4)]
    three = lane % 3 == np.arange(3)[:, None]
    ends = np.zeros((24, 128), np.float32)
    ends[0:6], ends[8:11], ends[19:22] = lane % 6 == np.arange(6)[:, None], three, three
    fours = (lane + 2) % 4 == np.arange(4)[:, None]
    ones = np.zeros((640, 768), np.float32)
    ones[0:192] = spread.reshape(192, 768)
    ones[192:576, 0:512] = select
    ones[576:608, 0:512], ones[608:640, 0:512] = row12.T, row13.T
    spots = np.concatenate([np.stack(rows), step, np.stack(back)]).astype(np.int32)
    last = np.zeros((32, 128), np.float32)
    last[0:24], last[24:28] = ends, fours
    first = np.zeros((48, 128), np.float32)
    first[0:14], first[16:28], first[32:48, 0:12] = place, np.stack(masks), pads
    return ones, spots, last, first


ONES, SPOTS, LAST, FIRST = layout_tables()
SELECT = (slice(192, 576), slice(0, 512))


def spread_of(ones, i):
    return ones[64 * i : 64 * i + 64, :]


def matmul(left, right):
    return jnp.dot(left, right, preferred_element_type=F32)


def matmul_nt(left, right):
    return lax.dot_general(left, right, NT, preferred_element_type=F32)


def matmul_tn(left, right):
    return lax.dot_general(left, right, TN, preferred_element_type=F32)


def allowed_pairs(clip, qb, j):
    pos = first_key() + j * 512 + lax.broadcasted_iota(jnp.int32, (512, 256), 0)
    return (pos >= clip[qb, 0:1, :]) & (pos < clip[qb, 1:2, :])


def first_key():
    return (lax.axis_index("dp") // 2 - 3) * 512


def key_blocks(ends, qb):
    first = (ends[qb, 0, 0] - first_key()) // 512
    return first, (ends[qb, 1, 255] - first_key() + 511) // 512


def front_kernel(
    ends, clip, w, ones, spots, tk,
    vecs, w_attn, unit, kv, q, of, lse, attn, held, sems,
):
    bounds = [key_blocks(ends, qb) for qb in range(2)]

    def fetch(j):
        return pltpu.make_async_copy(tk.at[j], held.at[j], sems.at[j])

    @pl.loop(bounds[0][0], bounds[1][1])
    def _(j):
        fetch(j).start()

    line = lax.broadcasted_iota(jnp.int32, (128, 768), 0)
    k = lax.axis_index("dp") % 2
    row12, row13 = [
        jnp.concatenate(
            [matmul(ones[576 + 32 * i : 608 + 32 * i, 0:512], w[z, :, 0:128]) for z in range(2)]
        ).astype(BF)
        for i in range(2)
    ]
    wide = matmul_tn(row12, spread_of(ones, 0))
    for p in range(6):
        hit = line == spots[p : p + 1, :]
        vecs[p : p + 1, :] = jnp.sum(jnp.where(hit, wide, 0.0), axis=0, keepdims=True)
    for p in (6, 7):
        wide = matmul_tn(row13, spread_of(ones, p - 5))
        hit = line == spots[p : p + 1, :] + k * spots[p + 8 : p + 9, :]
        vecs[p : p + 1, :] = jnp.sum(jnp.where(hit, wide, 0.0), axis=0, keepdims=True)
    for z in range(2):
        w_attn[z * 384 : z * 384 + 384, :] = matmul(ones[SELECT], w[z]).astype(BF)

    def norm_rows(j):
        v = held[j].astype(F32)
        centred = v - jnp.mean(v, axis=-1, keepdims=True)
        spread_out = jnp.mean(centred * centred, axis=-1, keepdims=True)
        u = centred * lax.rsqrt(spread_out + EPS)
        return u, (u * vecs[0:1, :] + vecs[2:3, :]).astype(BF)

    @pl.loop(bounds[0][0], bounds[1][1])
    def _(j):
        fetch(j).wait()
        u, a = norm_rows(j)
        unit[j] = u.astype(BF)
        kv[j] = (matmul(a, w_attn[:, 0:384]) + vecs[6:7, 0:384]).astype(BF)

    low = (lax.broadcasted_iota(jnp.int32, (512, 384), 1) & 127) < 64
    _, a = norm_rows(3)
    v = (matmul(a, w_attn[:, 384:768]) + vecs[6:7, 384:768]).astype(BF).astype(F32)
    q[...] = jnp.where(low, v * SCORE_SCALE, 0.0).astype(BF)

    lane = lax.broadcasted_iota(jnp.int32, (256, 128), 1)
    for qb in range(2):
        rows = slice(qb * 256, qb * 256 + 256)

        def step(j, carry):
            ok = allowed_pairs(clip, qb, j)
            keys = [kv[j, :, h * 128 : h * 128 + 128] for h in range(3)]
            scores = [
                jnp.where(ok, matmul_nt(keys[h], q[rows, h * 128 : h * 128 + 128]), NEGATIVE)
                for h in range(3)
            ]
            tops = [
                jnp.maximum(carry[h][0], jnp.max(scores[h], axis=0, keepdims=True))
                for h in range(3)
            ]
            probs = [jnp.exp(scores[h] - tops[h]) for h in range(3)]
            new = []
            for h in range(3):
                m, l, acc = carry[h]
                fade = jnp.exp(m - tops[h])
                l = l * fade + jnp.sum(probs[h], axis=0, keepdims=True)
                acc = acc * fade + matmul_tn(keys[h], probs[h].astype(BF))
                new.append((tops[h], l, acc))
            return tuple(new)

        start = tuple(
            (
                jnp.full((1, 256), NEGATIVE, F32),
                jnp.zeros((1, 256), F32),
                jnp.zeros((128, 256), F32),
            )
            for _ in range(3)
        )
        final = lax.fori_loop(bounds[qb][0], bounds[qb][1], step, start)
        for h in range(3):
            m, l, acc = final[h]
            o = (acc / l).T
            of[rows, h * 128 : h * 128 + 128] = jnp.where(lane >= 64, o, 0.0)
            lse[h : h + 1, rows] = m + jnp.log(l)
        attn[rows, :] = matmul_nt(of[rows, :].astype(BF), w_attn[:, 384:768]).astype(BF)


def front(*args):
    return pl.pallas_call(
        front_kernel,
        out_shape=[
            jax.ShapeDtypeStruct((8, 768), F32),
            jax.ShapeDtypeStruct((768, 768), BF),
            jax.ShapeDtypeStruct((7, 512, 768), BF),
            jax.ShapeDtypeStruct((7, 512, 384), BF),
            jax.ShapeDtypeStruct((512, 384), BF),
            jax.ShapeDtypeStruct((512, 384), F32),
            jax.ShapeDtypeStruct((3, 512), F32),
            jax.ShapeDtypeStruct((512, 768), BF),
        ],
        in_specs=[SM] + [VM] * 4 + [pl.BlockSpec(memory_space=pl.ANY)],
        out_specs=[VM] * 8,
        scratch_shapes=[pltpu.VMEM((7, 512, 768), BF), DMA((7,))],
        compiler_params=pltpu.CompilerParams(vmem_limit_bytes=38 * 2**20),
        name="front",
    )(*args)


def back_kernel(
    ends, clip, q, dr, of, kv, lse, unit, w_attn, vecs, sums, up_sum, ones, spots,
    d_out, grad, total, dox, delta, dq, ug,
):
    bounds = [key_blocks(ends, qb) for qb in range(2)]
    lane = lax.broadcasted_iota(jnp.int32, (256, 128), 1)
    high = (lax.broadcasted_iota(jnp.int32, (256, 384), 1) & 127) >= 64

    @pl.loop(0, 7)
    def _(j):
        total[j] = jnp.zeros((512, 384), F32)
        d_out[j] = jnp.zeros((512, 768), BF)

    for qb in range(2):
        rows = slice(qb * 256, qb * 256 + 256)
        g = jnp.where(high, matmul(dr[rows, :], w_attn[:, 384:768]), 0.0).astype(BF)
        dox[rows, :] = g
        prod = g.astype(F32) * of[rows, :]
        for h in range(3):
            part = prod[:, h * 128 : h * 128 + 128].T
            delta[h : h + 1, rows] = jnp.sum(part, axis=0, keepdims=True)

    for qb in range(2):
        rows = slice(qb * 256, qb * 256 + 256)

        def step(j, carry):
            ok = allowed_pairs(clip, qb, j)
            cols = [slice(h * 128, h * 128 + 128) for h in range(3)]
            keys = [kv[j, :, n] for n in cols]
            scores = [jnp.where(ok, matmul_nt(keys[h], q[rows, cols[h]]), NEGATIVE) for h in range(3)]
            grads = [matmul_nt(keys[h], dox[rows, cols[h]]) for h in range(3)]
            probs = [jnp.exp(scores[h] - lse[h : h + 1, rows]) for h in range(3)]
            ds = [(probs[h] * (grads[h] - delta[h : h + 1, rows])).astype(BF) for h in range(3)]
            for h in range(3):
                total[j, :, cols[h]] += matmul(ds[h], q[rows, cols[h]]) + matmul(
                    probs[h].astype(BF), dox[rows, cols[h]]
                )
            return tuple(carry[h] + matmul_tn(keys[h], ds[h]) for h in range(3))

        start = tuple(jnp.zeros((128, 256), F32) for _ in range(3))
        final = lax.fori_loop(bounds[qb][0], bounds[qb][1], step, start)
        for h in range(3):
            part = jnp.where(lane < 64, SCORE_SCALE * final[h].T, 0.0)
            dq[rows, h * 128 : h * 128 + 128] = part.astype(BF)

    ug[...] = jnp.zeros((768, 768), F32)

    def chunk(j, kv_sum):
        z = total[j].astype(BF)
        d_out[j] = matmul_nt(z, w_attn[:, 0:384]).astype(BF)
        ug[:, 0:384] += matmul_tn(unit[j], z)
        return kv_sum + jnp.sum(z.astype(F32), axis=0, keepdims=True)

    kv_sum = lax.fori_loop(bounds[0][0], bounds[1][1], chunk, jnp.zeros((1, 384), F32))
    own = matmul_nt(total[3].astype(BF), w_attn[:, 0:384])
    d_out[3] = (own + matmul_nt(dq[...], w_attn[:, 384:768])).astype(BF)
    ug[:, 384:768] = matmul_tn(unit[3], dq[...])
    q_sum = jnp.sum(dq[...].astype(F32), axis=0, keepdims=True)
    z_sum = jnp.concatenate([kv_sum, q_sum], axis=1)

    line = lax.broadcasted_iota(jnp.int32, (128, 768), 0)

    def place(p, row):
        return jnp.where(line == spots[p + 16 : p + 17, :], row, 0.0)

    columns = vecs[...].T
    gain_col, offset_col = columns[:, 0:1], columns[:, 2:3]
    w_full = w_attn[...].astype(F32)
    gain_sum = jnp.sum(ug[...] * w_full, axis=1, keepdims=True)
    offset_sum = jnp.sum(w_full * z_sum, axis=1, keepdims=True)
    flip = lax.broadcasted_iota(jnp.int32, (768, 128), 1)
    both = jnp.where(flip == 0, gain_sum, jnp.where(flip == 1, offset_sum, 0.0)).T
    own = place(0, both[0:1, :]) + place(2, both[1:2, :])
    for i, p in enumerate((1, 3, 4, 5)):
        own = own + place(p, sums[i : i + 1, :])
    small = matmul_nt(spread_of(ones, 0), own.astype(BF))
    small += matmul_nt(spread_of(ones, 1), place(6, z_sum).astype(BF))
    small += matmul_nt(spread_of(ones, 2), place(7, up_sum[...]).astype(BF))
    small = small.astype(BF)

    ug[...] = ug[...] * gain_col + offset_col * z_sum
    ug[:, 384:768] += matmul_tn(dr[...], of[...].astype(BF))
    for i in range(2):
        g = matmul_tn(ones[SELECT], ug[i * 384 : i * 384 + 384, :].astype(BF))
        grad[i] = g.astype(BF)
        extra = matmul_tn(ones[576:608, 0:512], small[i * 32 : i * 32 + 32, :])
        grad[i, :, 0:128] = (g[:, 0:128] + extra).astype(BF)


def back(*args):
    return pl.pallas_call(
        back_kernel,
        out_shape=[
            jax.ShapeDtypeStruct((7, 512, 768), BF),
            jax.ShapeDtypeStruct((2, 512, 768), BF),
        ],
        in_specs=[SM] + [VM] * (len(args) - 1),
        out_specs=[VM, VM],
        scratch_shapes=[
            pltpu.VMEM((7, 512, 384), F32),
            pltpu.VMEM((512, 384), BF),
            pltpu.VMEM((3, 512), F32),
            pltpu.VMEM((512, 384), BF),
            pltpu.VMEM((768, 768), F32),
        ],
        compiler_params=pltpu.CompilerParams(vmem_limit_bytes=22 * 2**20),
        name="back",
    )(*args)


def finish_kernel(
    own, far, back_one, e1, tok, vecs, ends,
    tokens, g_in, g_qv, g_out, g_up, g_fc, g_down, g_gain, g_row,
):
    t = lax.axis_index("tensor")
    hidden = tok[...].astype(F32)
    centred = hidden - jnp.mean(hidden, axis=-1, keepdims=True)
    scale = lax.rsqrt(jnp.mean(centred * centred, axis=-1, keepdims=True) + EPS)
    unit = centred * scale
    w = back_one[...] * vecs[0:1, :]
    mean_w = jnp.mean(w, axis=-1, keepdims=True)
    mean_wu = jnp.mean(w * unit, axis=-1, keepdims=True)
    tokens[...] = e1[...] + scale * (w - mean_w - unit * mean_wu)

    exact = dict(precision=lax.Precision.HIGHEST, preferred_element_type=F32)
    for n in range(3):
        cols = slice(n * 128, n * 128 + 128)
        parts = []
        for head in (2 * n, 2 * n + 1):
            q, h = head // 3, head % 3
            parts.append(
                (own[q, :, 384 + h * 128 : 512 + h * 128], own[q, :, h * 128 : h * 128 + 128])
            )
        (qo_a, kv_a), (qo_b, kv_b) = parts
        g_in[0, :, 0, cols] = jnp.concatenate([qo_a[:, 0:64], qo_b[:, 0:64]], axis=1)[0:12]
        g_in[1, :, 0, cols] = jnp.concatenate([kv_a[:, 0:64], kv_b[:, 0:64]], axis=1)[0:12]
        g_in[2, :, 0, cols] = jnp.concatenate([kv_a[:, 64:128], kv_b[:, 64:128]], axis=1)[0:12]
        mixed = jnp.concatenate([qo_a[:, 64:128], qo_b[:, 64:128]], axis=1)
        g_out[:, 0, cols] = mixed[0:12]
    for q in range(2):
        cols = slice(q * 768, q * 768 + 768)
        g_up[:, 0, cols] = own[q, 0:12, 768:1536]
        g_down[:, 0, cols] = own[q, 0:12, 1536:2304]
    row0, row1 = own[0, 12:13, 0:128], own[1, 12:13, 0:128]
    vec = row0 + row1 + far[0, 12:13, :] + far[1, 12:13, :]
    lane = lax.broadcasted_iota(jnp.int32, (8, 128), 1)
    line = lax.broadcasted_iota(jnp.int32, (8, 128), 0)

    def pick(row, start, width, stride):
        begin = start + line * stride
        return jnp.where((lane >= begin) & (lane < begin + width), row, 0.0)

    norms = lax.dot_general(pick(vec, 6 * t, 6, 12), ends[0:6, :], NT, **exact)
    g_gain[...] = norms[0:2]
    g_row[...] = norms[2:6]
    heads = lax.dot_general(pick(row0, 72, 3, 3), ends[8:14, :], NT, **exact)
    heads += lax.dot_general(pick(row1, 72, 3, 3), ends[16:22, :], NT, **exact)
    g_qv[...] = heads[0:2]
    hidden_rows = jnp.where(line < 3, pick(row0, 78, 4, 4), pick(row1, 66, 4, 4))
    g_fc[...] = lax.dot_general(ends[24:28, :], hidden_rows, NT, **exact)[:, 0:6]


def finish(*args):
    return pl.pallas_call(
        finish_kernel,
        out_shape=[
            jax.ShapeDtypeStruct(dims, F32)
            for dims in (
                (128, 768),
                (3, 12, 1, 384),
                (2, 6),
                (12, 1, 384),
                (12, 1, 1536),
                (4, 6),
                (12, 1, 1536),
                (2, 6),
                (4, 6),
            )
        ],
        in_specs=[VM] * len(args),
        out_specs=[VM] * 9,
        compiler_params=pltpu.CompilerParams(vmem_limit_bytes=16 * 2**20),
        name="finish",
    )(*args)


def body(
    tokens,
    clip_bounds,
    attn_in,
    qv_bias,
    out_proj,
    fc_in,
    fc_bias,
    fc_out,
    ln_gain,
    row_bias,
    cotangent,
):
    w, f0, f1, clip, near_tokens, tokens, cotangent, ones, spots, last = gather_all(
        clip_bounds,
        tokens,
        cotangent,
        attn_in[0],
        out_proj[0].T,
        fc_in[0],
        fc_out[0].T,
        ln_gain[0],
        row_bias[0],
        qv_bias.reshape(2, 6),
        fc_bias[0].T,
        jnp.asarray(FIRST),
        jnp.asarray(ONES, BF),
        jnp.asarray(SPOTS),
        jnp.asarray(LAST),
    )
    vecs, w_attn, unit, near, query, mixed, lse, attn = front(
        clip, clip, w.reshape(2, 512, 768), ones, spots, near_tokens.reshape(7, 512, 768)
    )
    output, grad_hidden_one, full_attn, sums, up_sum, s0, s1 = mid(
        attn.reshape(4, 128, 768), f0, f1, cotangent, tokens, vecs, ones
    )
    near_back, grad_w = back(
        clip,
        clip,
        query,
        full_attn.reshape(512, 768),
        mixed,
        near,
        lse,
        unit,
        w_attn,
        vecs,
        sums,
        up_sum,
        ones,
        spots,
    )
    back_one, own, far = return_all(
        near_back.reshape(7, 4, 128, 768), grad_w.reshape(2, 4, 4, 2, 16, 768), s0, s1
    )
    grads = finish(
        own, far, back_one, grad_hidden_one, tokens, vecs, last
    )
    grad_tokens, g_in, g_qv, g_out, g_up, g_fc, g_down, g_gain, g_row = grads
    return (
        output,
        grad_tokens,
        g_in.reshape(1, 3, 12, 384),
        g_qv.reshape(1, 2, 6, 1),
        g_out.reshape(12, 384).T[None],
        g_up.reshape(1, 12, 1536),
        g_fc.T[None],
        g_down.reshape(12, 1536).T[None],
        g_gain[None],
        g_row[None],
    )


def solution(mesh):
    return jax.shard_map(
        body,
        mesh=mesh,
        in_specs=(
            P(("dp", "tensor"), None),
            P(None, "dp"),
            P(None, None, "dp", "tensor"),
            P(None, None, "tensor", "dp"),
            P(None, "tensor", "dp"),
            P(None, "dp", "tensor"),
            P(None, "tensor", "dp"),
            P(None, "tensor", "dp"),
            P(None, None, ("dp", "tensor")),
            P(None, None, ("dp", "tensor")),
            P(("dp", "tensor"), None),
        ),
        out_specs=(
            P(("dp", "tensor"), None),
            P(("dp", "tensor"), None),
            P(None, None, "dp", "tensor"),
            P(None, None, "tensor", "dp"),
            P(None, "tensor", "dp"),
            P(None, "dp", "tensor"),
            P(None, "tensor", "dp"),
            P(None, "tensor", "dp"),
            P(None, None, ("dp", "tensor")),
            P(None, None, ("dp", "tensor")),
        ),
        check_vma=False,
    )
```

```python
import jax
import jax.numpy as jnp
import numpy as np
from jax import lax
import jax.experimental.pallas as pl
import jax.experimental.pallas.tpu as pltpu
from jax.sharding import PartitionSpec as P

EPS = 1e-05
NEGATIVE = -1e30
SCORE_SCALE = 0.125
BF = jnp.bfloat16
F32 = jnp.float32
MESH = pl.DeviceIdType.MESH
VM = pl.BlockSpec(memory_space=pltpu.VMEM)
SM = pl.BlockSpec(memory_space=pltpu.SMEM)
DMA = pltpu.SemaphoreType.DMA
NT = (((1,), (1,)), ((), ()))
TN = (((0,), (0,)), ((), ()))


def coords():
    dp = lax.axis_index("dp")
    return dp // 32, (dp // 8) % 4, (dp // 2) % 4, dp % 2, lax.axis_index("tensor")


def device(z, y, x, k, t):
    return (((z * 4 + y) * 4 + x) * 2 + k, t)


def chip(c, k, t):
    return (c * 2 + k, t)


def greet(peers):
    bar = pltpu.get_barrier_semaphore()
    for peer in peers:
        pl.semaphore_signal(bar, inc=1, device_id=peer, device_id_type=MESH)
    pl.semaphore_wait(bar, len(peers))


def remote(src, dst, sems, index, peer):
    send, recv = sems
    return pltpu.make_async_remote_copy(
        src, dst, send.at[index], recv.at[index], device_id=peer, device_id_type=MESH
    )


def comm_call(kernel, out_shape, scratch, cid, name, args, room, place=VM, outs=None):
    single = not isinstance(out_shape, (list, tuple))
    return pl.pallas_call(
        kernel,
        out_shape=out_shape,
        in_specs=[place] * len(args),
        out_specs=VM if single else outs or [VM] * len(out_shape),
        scratch_shapes=scratch,
        compiler_params=pltpu.CompilerParams(
            collective_id=cid, has_side_effects=True, vmem_limit_bytes=room * 2**20
        ),
        name=name,
    )(*args)


def neighbours():
    z, y, x, k, t = coords()
    xs = [device(z, y, (x + d) % 4, k, t) for d in (1, 2, 3)]
    ys = [device(z, (y + d) % 4, x, k, t) for d in (1, 2, 3)]
    core = device(z, y, x, 1 - k, t)
    far = device(z, y, x, k, 1 - t)
    low = device(1 - z, y, x, k, t)
    ring = [chip(((z * 4 + y) * 4 + x + d) % 32, k, t) for d in RING]
    return (z, y, x, k, t), xs, ys, core, far, low, ring


RING = (2, -2, 3, -3, 1, -1)


class Copies:
    def __init__(self, send, recv):
        self.sems, self.count = (send, recv), 0

    def __call__(self, src, dst, peer):
        made = remote(src, dst, self.sems, self.count, peer)
        self.count += 1
        made.start()
        return made


def build_small(gain, row, qv, fc, first, t, tile):
    place = first[0:14, :].astype(BF)
    masks = first[16:28, :]

    norms = jnp.sum(matmul(gain[...], place[0:6, :]) * masks[0:2, :], axis=0, keepdims=True)
    norms += jnp.sum(matmul(row[...], place[0:6, :]) * masks[2:6, :], axis=0, keepdims=True)
    lane = lax.broadcasted_iota(jnp.int32, (16, 128), 1)
    line = lax.broadcasted_iota(jnp.int32, (16, 128), 0)
    others = jnp.sum(matmul(qv[...], place[0:6, :]) * masks[6:8, :], axis=0, keepdims=True)
    others += jnp.sum(matmul(fc[...], place[8:14, :]) * masks[8:12, :], axis=0, keepdims=True)
    mine = (line == 12) & (lane >= 64 * t) & (lane < 64 * t + 64)
    small = jnp.where(mine, norms, 0.0)
    tile[...] = small.astype(BF)
    return small + jnp.where(line == 13, others, 0.0)


def build_rows(attn_w, proj, up, down, small, first, pay):
    pads = first[32:48, 0:12].astype(BF)

    def tall(v):
        return matmul(pads, v)

    query, keys, values = [tall(attn_w[i]) for i in range(3)]
    mixed, up_rows, down_rows = tall(proj[...]), tall(up[...]), tall(down[...])
    for q in range(2):
        for h in range(3):
            n = slice((q * 3 + h) * 64, (q * 3 + h) * 64 + 64)
            pair = jnp.concatenate([keys[:, n], values[:, n]], axis=1)
            if h == 0:
                pair = pair + small
            pay[q, :, h * 128 : h * 128 + 128] = pair.astype(BF)
            pair = jnp.concatenate([query[:, n], mixed[:, n]], axis=1)
            pay[q, :, 384 + h * 128 : 512 + h * 128] = pair.astype(BF)
        pay[q, :, 768:1536] = up_rows[:, q * 768 : q * 768 + 768].astype(BF)
        pay[q, :, 1536:2304] = down_rows[:, q * 768 : q * 768 + 768].astype(BF)


H0, H1 = pl.ds(0, 512), pl.ds(512, 256)


def gather_kernel(
    clip, tok, cot, attn_h, proj_h, up_h, down_h, gain_h, row_h, qv_h, fc_h, first_h,
    ones_h, spots_h, last_h,
    w, f0, f1, clip_out, tk, tok_out, cot_out, ones, spots, last,
    attn_w, proj, up, down, gain, row, qv, fc, first,
    pay_s, tile, tile_in, ws, send, recv, local,
):
    stages = []

    def stage(src, dst):
        stages.append(pltpu.make_async_copy(src, dst, local.at[len(stages)]))
        stages[-1].start()

    for src, dst in (
        (gain_h, gain), (row_h, row), (qv_h, qv), (fc_h, fc), (first_h, first),
        (attn_h, attn_w), (proj_h, proj), (up_h, up), (down_h, down),
    ):
        stage(src, dst)
    (z, y, x, k, t), xs, ys, core, far, low, ring = neighbours()
    copy = Copies(send, recv)
    mine, other = k * 2 + t, k * 2 + 1 - t
    both = device(z, y, x, 1 - k, 1 - t)
    greet(xs + ys + [core, far, both, low] + ring)
    own_far = copy(tok, tk.at[3, mine], far)
    order = (4, 5, 2, 3, 0, 1)
    pushes = {i: copy(tok, tk.at[3 - RING[i], mine], ring[i]) for i in order}
    done = [copy(tok, tk.at[3, mine], core), copy(clip, clip_out.at[k], core)]
    stage(tok, tk.at[3, mine])
    stage(clip, clip_out.at[k])
    for pair in ((tok, tok_out), (cot, cot_out), (ones_h, ones), (spots_h, spots), (last_h, last)):
        stage(*pair)
    for c in stages[0:9]:
        c.wait()
    small = build_small(gain, row, qv, fc, first, t, tile)
    c_tile = [copy(tile, tile_in.at[0], far), copy(tile, tile_in.at[1], both)]
    build_rows(attn_w, proj, up, down, small, first, pay_s)
    to_far = {}

    def to_core(slot, which):
        done.append(copy(tk.at[slot, which], tk.at[slot, which], core))

    def pass_on(i):
        pushes[i].wait_recv()
        slot = 3 - RING[i]
        to_far[i] = copy(tk.at[slot, mine], tk.at[slot, mine], far)
        to_core(slot, mine)

    swap = copy(pay_s.at[1 - k], ws.at[z, k], core)
    ws[z, k] = pay_s[k]
    for i in (4, 5):
        pushes[i].wait_recv()
        to_core(3 - RING[i], mine)
    swap.wait()
    for c in c_tile:
        c.wait()
    ws[z, k, :, 0:128] = ws[z, k, :, 0:128] + tile_in[0]
    ws[z, 1 - k, :, 0:128] = ws[z, 1 - k, :, 0:128] + tile_in[1]
    c_low = copy(ws.at[z], ws.at[z], low)
    pass_on(2)
    pass_on(3)
    c_low.wait()
    w[:, y, x] = ws[:, :, :, 0:768]
    f0[:, x] = ws[:, :, :, 768:1536]
    f1[:, y] = ws[:, :, :, 1536:2304]
    phase = []
    for i in range(3):
        phase.append(copy(ws.at[:, :, :, H0], w.at[:, y, x, :, :, H0], xs[i]))
        phase.append(copy(ws.at[:, :, :, H1], w.at[:, y, x, :, :, H1], ys[i]))
    pass_on(0)
    pass_on(1)
    own_far.wait_recv()
    beyond = []
    for i in (4, 5):
        slot = 3 - RING[i]
        beyond.append((slot, copy(tk.at[3, other], tk.at[slot, other], ring[i])))
    to_core(3, other)
    for c in phase:
        c.wait()
    rest = []
    for i in range(3):
        a = w.at[:, y, :, :, :, H0]
        rest.append(copy(a, a, ys[i]))
        b = w.at[:, :, x, :, :, H1]
        rest.append(copy(b, b, xs[i]))
    for i in range(3):
        rest.append(copy(ws.at[:, :, :, pl.ds(768, 768)], f0.at[:, x], xs[i]))
        rest.append(copy(ws.at[:, :, :, pl.ds(1536, 768)], f1.at[:, y], ys[i]))
    for i in (2, 3, 0, 1):
        to_far[i].wait_recv()
        to_core(3 - RING[i], other)
    for slot, c in beyond:
        c.wait_recv()
        to_core(slot, other)
        c.wait_send()
    for i in order:
        pushes[i].wait_send()
    for i in (2, 3, 0, 1):
        to_far[i].wait_send()
    own_far.wait_send()
    for c in rest + done + stages[9:]:
        c.wait()


def gather_all(*args):
    return comm_call(
        gather_kernel,
        [
            jax.ShapeDtypeStruct((2, 4, 4, 2, 16, 768), BF),
            jax.ShapeDtypeStruct((2, 4, 2, 16, 768), BF),
            jax.ShapeDtypeStruct((2, 4, 2, 16, 768), BF),
            jax.ShapeDtypeStruct((2, 2, 256), jnp.int32),
            jax.ShapeDtypeStruct((7, 4, 128, 768), BF),
            jax.ShapeDtypeStruct((128, 768), BF),
            jax.ShapeDtypeStruct((128, 768), BF),
            jax.ShapeDtypeStruct((640, 768), BF),
            jax.ShapeDtypeStruct((24, 768), jnp.int32),
            jax.ShapeDtypeStruct((32, 128), F32),
        ],
        [pltpu.VMEM(v.shape, v.dtype) for v in args[3:12]]
        + [
            pltpu.VMEM((2, 16, 2304), BF),
            pltpu.VMEM((16, 128), BF),
            pltpu.VMEM((2, 16, 128), BF),
            pltpu.VMEM((2, 2, 16, 2304), BF),
            DMA((50,)),
            DMA((50,)),
            DMA((16,)),
        ],
        0,
        "gather_first",
        args,
        54,
        pl.BlockSpec(memory_space=pltpu.MemorySpace.HBM),
        [VM] * 4 + [pl.BlockSpec(memory_space=pltpu.MemorySpace.HBM)] + [VM] * 5,
    )


def exchange_rows(copy, a, out, k, t, core, far):
    mine, other = k * 2 + t, k * 2 + 1 - t
    c_far = copy(a, out.at[mine], far)
    c_core = copy(a, out.at[mine], core)
    out[mine] = a[...]

    def finish():
        c_far.wait_recv()
        c_pass = copy(out.at[other], out.at[other], core)
        c_far.wait_send()
        c_core.wait()
        c_pass.wait()

    return finish


def spread_over_y(copy, g0, b0, y, ys):
    return [copy(g0.at[:, (y + i + 1) % 4], b0.at[i], ys[i]) for i in range(3)]


def spread_over_x(copy, g1, b1, x, xs):
    return [copy(g1.at[:, :, (x + i + 1) % 4], b1.at[i], xs[i]) for i in range(3)]


def spread_first(copy, g0, g1, b0, b1, x, y, xs, ys):
    return spread_over_y(copy, g0, b0, y, ys), spread_over_x(copy, g1, b1, x, xs)


def add_first(g0, g1, b0, b1, s0, s1, x, y, over_y, over_x):
    for c in over_y:
        c.wait()

    @pl.loop(0, 8)
    def _(n):
        zz, m = n // 4, n % 4
        v = g0[zz, y, m].astype(F32)
        for i in range(3):
            v = v + b0[i, zz, m].astype(F32)
        s0[zz, m] = v.astype(BF)

    for c in over_x:
        c.wait()

    @pl.loop(0, 8)
    def _(n):
        zz, m = n // 4, n % 4
        v = g1[zz, m, x].astype(F32)
        for i in range(3):
            v = v + b1[i, zz, m].astype(F32)
        s1[zz, m] = v.astype(BF)


def spread_second(copy, s0, s1, a0, a1, x, y, xs, ys):
    over_x, over_y = [], []
    for i in range(3):
        over_x.append(copy(s0.at[:, (x + i + 1) % 4], a0.at[i], xs[i]))
        over_y.append(copy(s1.at[:, (y + i + 1) % 4], a1.at[i], ys[i]))
    return over_x, over_y


def add_second(s0, s1, a0, a1, u0, u1, x, y, over_x, over_y):
    for c in over_x + over_y:
        c.wait()
    for zz in range(2):
        v = s0[zz, x].astype(F32)
        v1 = s1[zz, y].astype(F32)
        for i in range(3):
            v = v + a0[i, zz].astype(F32)
            v1 = v1 + a1[i, zz].astype(F32)
        u0[zz] = v.astype(BF)
        u1[zz] = v1.astype(BF)


HALVES = (slice(0, 64), slice(64, 128))


def unit_rows(hidden):
    centred = hidden - jnp.mean(hidden, axis=-1, keepdims=True)
    scale = lax.rsqrt(jnp.mean(centred * centred, axis=-1, keepdims=True) + EPS)
    return centred * scale, scale


def mid_kernel(
    p, f0, f1, cot, tok, vecs, ones,
    output, e1, dr_full, sums, up_sum, s0, s1,
    got, mid, got_far, p0, p1, w_up, w_down, b_full, cot_full, dg, active, du_full,
    pr, got_two, mid_two, far_two, grad_one, g0, g1, b0, b1, send, recv,
):
    (z, y, x, k, t), xs, ys, core, far, low, ring = neighbours()
    copy = Copies(send, recv)
    greet(xs + ys + [core, far])
    mine, across, beside, both = k * 2 + t, k * 2 + 1 - t, 2 - 2 * k + t, 3 - 2 * k - t
    to_core = copy(p.at[pl.ds((1 - k) * 2, 2)], got, core)
    finish_cot = exchange_rows(copy, cot, cot_full, k, t, core, far)
    made = []
    for i in range(2):
        for j in range(3):
            made.append(copy(f0.at[i], p0.at[i, y], ys[j]))
            made.append(copy(f1.at[i], p1.at[i, :, x], xs[j]))
        p0[i, y] = f0[i]
        p1[i, :, x] = f1[i]
    to_core.wait()
    to_far, rows_far, rows_core = [], [], []
    for rows in HALVES:
        part = p[across, rows].astype(F32) + got[1 - t, rows].astype(F32)
        mid[rows] = part.astype(BF)
        to_far.append(copy(mid.at[rows], got_far.at[rows], far))
    for i, rows in enumerate(HALVES):
        part = p[mine, rows].astype(F32) + got[t, rows].astype(F32)
        part = part + tok[rows].astype(F32) + vecs[3:4, :]
        to_far[i].wait()
        hidden = part + got_far[rows].astype(F32)
        unit, _ = unit_rows(hidden)
        b_full[mine, rows] = (unit * vecs[1:2, :] + vecs[4:5, :]).astype(BF)
        here = b_full.at[mine, rows]
        rows_far.append(copy(here, here, far))
        rows_core.append(copy(here, here, core))
        e1[rows] = hidden
    finish_cot()
    for c in made:
        c.wait()
    for i in range(2):
        rows = slice(i * 384, i * 384 + 384)
        w_up[rows, :] = matmul(ones[SELECT], p0[i].reshape(512, 768)).astype(BF)
        w_down[rows, :] = matmul(ones[SELECT], p1[i].reshape(512, 768)).astype(BF)

    @pl.loop(0, 4)
    def _(i):
        dg[i] = matmul(cot_full[i], w_down[...])

    up_sum[...] = jnp.zeros((1, 768), F32)

    def feed(i):
        u = matmul(b_full[i], w_up[...]) + vecs[7:8, :]
        phi = 0.5 + 0.5 * lax.erf(u * 0.7071067811865476)
        gl = (u * phi).astype(BF)
        active[i] = gl
        pr[0, i] = matmul_nt(gl, w_down[...]).astype(BF)
        slope = phi + u * jnp.exp(-0.5 * u * u) * 0.3989422804014327
        du = (dg[i] * slope).astype(BF)
        du_full[i] = du
        up_sum[...] += jnp.sum(du.astype(F32), axis=0, keepdims=True)
        pr[1, i] = matmul_nt(du, w_up[...]).astype(BF)

    feed(mine)
    for c in rows_core:
        c.wait()
    feed(beside)
    first = copy(pr.at[:, beside], got_two.at[:, t], core)
    rows_pass = []
    for i, rows in enumerate(HALVES):
        rows_far[i].wait()
        rows_pass.append(copy(b_full.at[across, rows], b_full.at[across, rows], core))
    feed(across)
    for c in rows_pass:
        c.wait()
    feed(both)
    second = copy(pr.at[:, both], got_two.at[:, 1 - t], core)
    second.wait()
    for i in range(2):
        v = pr[i, across].astype(F32) + got_two[i, 1 - t].astype(F32)
        mid_two[i] = v.astype(BF)
    back_far = [copy(mid_two.at[1, rows], far_two.at[1, rows], far) for rows in HALVES]
    c_rows, a_rows = cot_full[...].reshape(512, 768), active[...].reshape(512, 768)
    for i in range(2):
        cols = slice(i * 384, i * 384 + 384)
        g = matmul_tn(c_rows[:, cols], a_rows).astype(BF)
        g1[i] = matmul_tn(ones[SELECT], g).astype(BF).reshape(4, 4, 2, 16, 768)
    over_x = spread_over_x(copy, g1, b1, x, xs)
    b_rows, du_rows = b_full[...].reshape(512, 768), du_full[...].reshape(512, 768)
    for i in range(2):
        cols = slice(i * 384, i * 384 + 384)
        g = matmul_tn(b_rows[:, cols], du_rows).astype(BF)
        g0[i] = matmul_tn(ones[SELECT], g).astype(BF).reshape(4, 4, 2, 16, 768)
    over = spread_over_y(copy, g0, b0, y, ys), over_x
    first.wait()

    sums[...] = jnp.zeros((4, 768), F32)
    dr_far, dr_core = [], []
    for i, rows in enumerate(HALVES):
        back_rows = pr[1, mine, rows].astype(F32) + got_two[1, t, rows].astype(F32)
        back_far[i].wait()
        back_rows = back_rows + far_two[1, rows].astype(F32)
        unit, scale = unit_rows(e1[rows])
        w = back_rows * vecs[1:2, :]
        mean_w = jnp.mean(w, axis=-1, keepdims=True)
        mean_wu = jnp.mean(w * unit, axis=-1, keepdims=True)
        cot_f = cot[rows].astype(F32)
        grad = cot_f + scale * (w - mean_w - unit * mean_wu)
        low_grad = grad.astype(BF)
        dr_full[mine, rows] = low_grad
        here = dr_full.at[mine, rows]
        dr_far.append(copy(here, here, far))
        dr_core.append(copy(here, here, core))
        grad_one[rows] = grad
        sums[0:1, :] += jnp.sum(back_rows * unit, axis=0, keepdims=True)
        sums[1:2, :] += jnp.sum(low_grad.astype(F32), axis=0, keepdims=True)
        sums[2:3, :] += jnp.sum(back_rows, axis=0, keepdims=True)
        sums[3:4, :] += jnp.sum(cot_f, axis=0, keepdims=True)
    out_far = copy(mid_two.at[0], far_two.at[0], far)
    dr_pass = []
    for i, rows in enumerate(HALVES):
        dr_far[i].wait()
        dr_pass.append(copy(dr_full.at[across, rows], dr_full.at[across, rows], core))
    part = e1[...] + pr[0, mine].astype(F32) + got_two[0, t].astype(F32) + vecs[5:6, :]
    e1[...] = grad_one[...]
    out_far.wait()
    output[...] = (part + far_two[0].astype(F32)).astype(BF)
    for c in dr_core + dr_pass:
        c.wait()
    add_first(g0, g1, b0, b1, s0, s1, x, y, *over)


def mid(p, f0, f1, cot, tok, vecs, ones):
    rows = pltpu.VMEM((128, 768), BF)
    two = pltpu.VMEM((2, 128, 768), BF)
    four = pltpu.VMEM((4, 128, 768), BF)
    square = pltpu.VMEM((768, 768), BF)
    piece = pltpu.VMEM((2, 4, 4, 2, 16, 768), BF)
    return comm_call(
        mid_kernel,
        [
            jax.ShapeDtypeStruct((128, 768), BF),
            jax.ShapeDtypeStruct((128, 768), F32),
            jax.ShapeDtypeStruct((4, 128, 768), BF),
            jax.ShapeDtypeStruct((4, 768), F32),
            jax.ShapeDtypeStruct((1, 768), F32),
            jax.ShapeDtypeStruct((2, 4, 2, 16, 768), BF),
            jax.ShapeDtypeStruct((2, 4, 2, 16, 768), BF),
        ],
        [two, rows, rows, piece, piece, square, square, four, four]
        + [pltpu.VMEM((4, 128, 768), F32), four, four]
        + [pltpu.VMEM((2, 4, 128, 768), BF), pltpu.VMEM((2, 2, 128, 768), BF), two, two]
        + [pltpu.VMEM((128, 768), F32)]
        + [piece, piece]
        + [pltpu.VMEM((3, 2, 4, 2, 16, 768), BF)] * 2
        + [DMA((41,)), DMA((41,))],
        1,
        "mid",
        (p, f0, f1, cot, tok, vecs, ones),
        26,
    )


def return_kernel(
    d, g, fs0, fs1, out, own, tile_out,
    got_core, v1, in1, e_send, got_far, r_send, got_ring,
    b0, b1, s0, s1, a0, a1, fa0, fa1, u0, u1, v_0, v_1, z_in0, z_in1, z_in2, z_in3, res, send, recv,
):
    (z, y, x, k, t), xs, ys, core, far, low, ring = neighbours()
    copy = Copies(send, recv)
    both = device(z, y, x, 1 - k, 1 - t)
    greet(xs + ys + [core, far, both, low] + ring)
    mine, across = k * 2 + t, k * 2 + 1 - t
    near = (ring[4], ring[5])
    order = (4, 2, 5, 1, 6, 0, 3)
    to_core = {j: copy(d.at[j, pl.ds((1 - k) * 2, 2)], got_core.at[j], core) for j in order}
    g0, g1 = g.at[:, :, :, :, :, H0], g.at[:, :, :, :, :, H1]
    fc_over = spread_second(copy, fs0, fs1, fa0, fa1, x, y, xs, ys)
    hop1, to_far = [], []
    over = spread_first(copy, g0, g1, b0, b1, x, y, xs, ys)
    for i, j in enumerate((4, 2)):
        to_core[j].wait()
        v1[i] = (d[j, pl.ds(k * 2, 2)].astype(F32) + got_core[j].astype(F32)).astype(BF)
        hop1.append(copy(v1.at[i], in1.at[i], near[i]))
    for i, j in enumerate(order[2:6]):
        to_core[j].wait()
        e_send[i] = (d[j, across].astype(F32) + got_core[j, 1 - t].astype(F32)).astype(BF)
        to_far.append(copy(e_send.at[i], got_far.at[i], far))
    home = []

    def send_home(i):
        j = order[2 + i]
        to_far[i].wait()
        v = d[j, mine].astype(F32) + got_core[j, t].astype(F32) + got_far[i].astype(F32)
        r_send[i] = v.astype(BF)
        home.append(copy(r_send.at[i], got_ring.at[i], ring[i]))

    add_second(fs0, fs1, fa0, fa1, u0, u1, x, y, *fc_over)
    fc_z = [copy(u0.at[1 - z], z_in0, low), copy(u1.at[1 - z], z_in1, low)]
    send_home(0)
    send_home(1)
    add_first(g0, g1, b0, b1, s0, s1, x, y, *over)
    over = spread_second(copy, s0, s1, a0, a1, x, y, xs, ys)
    to_core[3].wait()
    hop1[0].wait()
    hop1[1].wait()
    v = d[3, across].astype(F32) + got_core[3, 1 - t].astype(F32)
    v = v + in1[0, 1 - t].astype(F32) + in1[1, 1 - t].astype(F32)
    e_send[4] = v.astype(BF)
    last = copy(e_send.at[4], got_far.at[4], far)
    send_home(2)
    send_home(3)
    add_second(s0, s1, a0, a1, v_0, v_1, x, y, *over)
    attn_z = [copy(v_0.at[1 - z], z_in2, low), copy(v_1.at[1 - z], z_in3, low)]
    for c in fc_z:
        c.wait()
    res[:, :, 768:1536] = u0[z].astype(F32) + z_in0[...].astype(F32)
    res[:, :, 1536:2304] = u1[z].astype(F32) + z_in1[...].astype(F32)
    for c in attn_z:
        c.wait()
    res[:, :, H0] = v_0[z].astype(F32) + z_in2[...].astype(F32)
    res[:, :, H1] = v_1[z].astype(F32) + z_in3[...].astype(F32)
    swap = copy(res.at[1 - k], own.at[k], core)
    tiles = [
        copy(res.at[k, :, pl.ds(0, 128)], tile_out.at[0], far),
        copy(res.at[1 - k, :, pl.ds(0, 128)], tile_out.at[1], both),
    ]
    own[k] = res[k]
    total = d[3, mine].astype(F32) + got_core[3, t].astype(F32)
    total = total + in1[0, t].astype(F32) + in1[1, t].astype(F32)
    for i in range(4):
        home[i].wait()
        total = total + got_ring[i].astype(F32)
    last.wait()
    out[...] = total + got_far[4].astype(F32)
    swap.wait()
    for c in tiles:
        c.wait()


def return_all(d, g, s0, s1):
    two = pltpu.VMEM((2, 2, 128, 768), BF)
    wide, slim = 512, 256
    return comm_call(
        return_kernel,
        [
            jax.ShapeDtypeStruct((128, 768), F32),
            jax.ShapeDtypeStruct((2, 16, 2304), F32),
            jax.ShapeDtypeStruct((2, 16, 128), F32),
        ],
        [pltpu.VMEM((7, 2, 128, 768), BF), two, two]
        + [pltpu.VMEM((5, 128, 768), BF)] * 2
        + [pltpu.VMEM((4, 128, 768), BF)] * 2
        + [pltpu.VMEM((3, 2, 4, 2, 16, n), BF) for n in (wide, slim)]
        + [pltpu.VMEM((2, 4, 2, 16, n), BF) for n in (wide, slim)]
        + [pltpu.VMEM((3, 2, 2, 16, n), BF) for n in (wide, slim)]
        + [pltpu.VMEM((3, 2, 2, 16, 768), BF)] * 2
        + [pltpu.VMEM((2, 2, 16, n), BF) for n in (768, 768, wide, slim)]
        + [pltpu.VMEM((2, 16, n), BF) for n in (768, 768, wide, slim)]
        + [pltpu.VMEM((2, 16, 2304), F32), DMA((43,)), DMA((43,))],
        5,
        "return_all",
        (d, g, s0, s1),
        24,
    )


def layout_tables():
    d = np.arange(768)
    n64 = np.arange(64)[:, None]
    own = (d // 12 == n64).astype(np.float32)
    lane = d % 128
    high = d < 384
    column = np.where(high, lane - 64, lane)
    heads = ((column == n64) & (column >= 0) & (column < 64)).astype(np.float32)
    hidden = ((d % 256) // 4 == n64).astype(np.float32)
    spread = np.stack([own, heads, hidden])
    spot = 64 * ((d % 12) // 6) + d % 6
    head = (d % 384) // 128
    rows = [spot + 6 * p for p in range(6)]
    rows.append(np.where(high, 6, 0) + head)
    rows.append(12 + (d // 256) * 4 + d % 4)
    step = np.zeros((8, 768), np.int32)
    step[6], step[7] = 3, 12
    back = [12 * p + d % 12 for p in range(6)]
    back.append(72 + np.where(high, 3, 0) + head)
    back.append(78 + (d // 256) * 4 + d % 4)
    select = np.arange(512)[None, :] == (np.arange(384) // 12 * 16 + np.arange(384) % 12)[:, None]
    row12 = np.arange(512)[:, None] == np.arange(32)[None, :] * 16 + 12
    row13 = np.arange(512)[:, None] == np.arange(32)[None, :] * 16 + 13
    pads = np.arange(16)[:, None] == np.arange(12)[None, :]
    lane = np.arange(128)
    half = lane % 64
    six = half % 6 == np.arange(6)[:, None]
    four = lane % 4 == np.arange(4)[:, None]
    place = np.zeros((14, 128), np.float32)
    place[0:6], place[8:14] = six, lane // 4 == 3 + np.arange(6)[:, None]
    masks = [half // 6 == p for p in range(6)] + [lane // 6 == p for p in range(2)]
    masks += [(lane >= 12) & (lane < 36) & four[e] for e in range(4)]
    three = lane % 3 == np.arange(3)[:, None]
    ends = np.zeros((24, 128), np.float32)
    ends[0:6], ends[8:11], ends[19:22] = lane % 6 == np.arange(6)[:, None], three, three
    fours = (lane + 2) % 4 == np.arange(4)[:, None]
    ones = np.zeros((640, 768), np.float32)
    ones[0:192] = spread.reshape(192, 768)
    ones[192:576, 0:512] = select
    ones[576:608, 0:512], ones[608:640, 0:512] = row12.T, row13.T
    spots = np.concatenate([np.stack(rows), step, np.stack(back)]).astype(np.int32)
    last = np.zeros((32, 128), np.float32)
    last[0:24], last[24:28] = ends, fours
    first = np.zeros((48, 128), np.float32)
    first[0:14], first[16:28], first[32:48, 0:12] = place, np.stack(masks), pads
    return ones, spots, last, first


ONES, SPOTS, LAST, FIRST = layout_tables()
SELECT = (slice(192, 576), slice(0, 512))


def spread_of(ones, i):
    return ones[64 * i : 64 * i + 64, :]


def matmul(left, right):
    return jnp.dot(left, right, preferred_element_type=F32)


def matmul_nt(left, right):
    return lax.dot_general(left, right, NT, preferred_element_type=F32)


def matmul_tn(left, right):
    return lax.dot_general(left, right, TN, preferred_element_type=F32)


def allowed_pairs(clip, qb, j):
    pos = first_key() + j * 512 + lax.broadcasted_iota(jnp.int32, (512, 256), 0)
    return (pos >= clip[qb, 0:1, :]) & (pos < clip[qb, 1:2, :])


def first_key():
    return (lax.axis_index("dp") // 2 - 3) * 512


def key_blocks(ends, qb):
    first = (ends[qb, 0, 0] - first_key()) // 512
    return first, (ends[qb, 1, 255] - first_key() + 511) // 512


def front_kernel(
    ends, clip, w, ones, spots, tk,
    vecs, w_attn, unit, kv, q, of, lse, attn, held, sems,
):
    bounds = [key_blocks(ends, qb) for qb in range(2)]

    def fetch(j):
        return pltpu.make_async_copy(tk.at[j], held.at[j], sems.at[j])

    @pl.loop(bounds[0][0], bounds[1][1])
    def _(j):
        fetch(j).start()

    line = lax.broadcasted_iota(jnp.int32, (128, 768), 0)
    k = lax.axis_index("dp") % 2
    row12, row13 = [
        jnp.concatenate(
            [matmul(ones[576 + 32 * i : 608 + 32 * i, 0:512], w[z, :, 0:128]) for z in range(2)]
        ).astype(BF)
        for i in range(2)
    ]
    wide = matmul_tn(row12, spread_of(ones, 0))
    for p in range(6):
        hit = line == spots[p : p + 1, :]
        vecs[p : p + 1, :] = jnp.sum(jnp.where(hit, wide, 0.0), axis=0, keepdims=True)
    for p in (6, 7):
        wide = matmul_tn(row13, spread_of(ones, p - 5))
        hit = line == spots[p : p + 1, :] + k * spots[p + 8 : p + 9, :]
        vecs[p : p + 1, :] = jnp.sum(jnp.where(hit, wide, 0.0), axis=0, keepdims=True)
    for z in range(2):
        w_attn[z * 384 : z * 384 + 384, :] = matmul(ones[SELECT], w[z]).astype(BF)

    def norm_rows(j):
        v = held[j].astype(F32)
        centred = v - jnp.mean(v, axis=-1, keepdims=True)
        spread_out = jnp.mean(centred * centred, axis=-1, keepdims=True)
        u = centred * lax.rsqrt(spread_out + EPS)
        return u, (u * vecs[0:1, :] + vecs[2:3, :]).astype(BF)

    @pl.loop(bounds[0][0], bounds[1][1])
    def _(j):
        fetch(j).wait()
        u, a = norm_rows(j)
        unit[j] = u.astype(BF)
        kv[j] = (matmul(a, w_attn[:, 0:384]) + vecs[6:7, 0:384]).astype(BF)

    low = (lax.broadcasted_iota(jnp.int32, (512, 384), 1) & 127) < 64
    _, a = norm_rows(3)
    v = (matmul(a, w_attn[:, 384:768]) + vecs[6:7, 384:768]).astype(BF).astype(F32)
    q[...] = jnp.where(low, v * SCORE_SCALE, 0.0).astype(BF)

    lane = lax.broadcasted_iota(jnp.int32, (256, 128), 1)
    for qb in range(2):
        rows = slice(qb * 256, qb * 256 + 256)

        def step(j, carry):
            ok = allowed_pairs(clip, qb, j)
            keys = [kv[j, :, h * 128 : h * 128 + 128] for h in range(3)]
            scores = [
                jnp.where(ok, matmul_nt(keys[h], q[rows, h * 128 : h * 128 + 128]), NEGATIVE)
                for h in range(3)
            ]
            tops = [
                jnp.maximum(carry[h][0], jnp.max(scores[h], axis=0, keepdims=True))
                for h in range(3)
            ]
            probs = [jnp.exp(scores[h] - tops[h]) for h in range(3)]
            new = []
            for h in range(3):
                m, l, acc = carry[h]
                fade = jnp.exp(m - tops[h])
                l = l * fade + jnp.sum(probs[h], axis=0, keepdims=True)
                acc = acc * fade + matmul_tn(keys[h], probs[h].astype(BF))
                new.append((tops[h], l, acc))
            return tuple(new)

        start = tuple(
            (
                jnp.full((1, 256), NEGATIVE, F32),
                jnp.zeros((1, 256), F32),
                jnp.zeros((128, 256), F32),
            )
            for _ in range(3)
        )
        final = lax.fori_loop(bounds[qb][0], bounds[qb][1], step, start)
        for h in range(3):
            m, l, acc = final[h]
            o = (acc / l).T
            of[rows, h * 128 : h * 128 + 128] = jnp.where(lane >= 64, o, 0.0)
            lse[h : h + 1, rows] = m + jnp.log(l)
        attn[rows, :] = matmul_nt(of[rows, :].astype(BF), w_attn[:, 384:768]).astype(BF)


def front(*args):
    return pl.pallas_call(
        front_kernel,
        out_shape=[
            jax.ShapeDtypeStruct((8, 768), F32),
            jax.ShapeDtypeStruct((768, 768), BF),
            jax.ShapeDtypeStruct((7, 512, 768), BF),
            jax.ShapeDtypeStruct((7, 512, 384), BF),
            jax.ShapeDtypeStruct((512, 384), BF),
            jax.ShapeDtypeStruct((512, 384), F32),
            jax.ShapeDtypeStruct((3, 512), F32),
            jax.ShapeDtypeStruct((512, 768), BF),
        ],
        in_specs=[SM] + [VM] * 4 + [pl.BlockSpec(memory_space=pl.ANY)],
        out_specs=[VM] * 8,
        scratch_shapes=[pltpu.VMEM((7, 512, 768), BF), DMA((7,))],
        compiler_params=pltpu.CompilerParams(vmem_limit_bytes=38 * 2**20),
        name="front",
    )(*args)


def back_kernel(
    ends, clip, q, dr, of, kv, lse, unit, w_attn, vecs, sums, up_sum, ones, spots,
    d_out, grad, total, dox, delta, dq, ug,
):
    bounds = [key_blocks(ends, qb) for qb in range(2)]
    lane = lax.broadcasted_iota(jnp.int32, (256, 128), 1)
    high = (lax.broadcasted_iota(jnp.int32, (256, 384), 1) & 127) >= 64

    @pl.loop(0, 7)
    def _(j):
        total[j] = jnp.zeros((512, 384), F32)
        d_out[j] = jnp.zeros((512, 768), BF)

    for qb in range(2):
        rows = slice(qb * 256, qb * 256 + 256)
        g = jnp.where(high, matmul(dr[rows, :], w_attn[:, 384:768]), 0.0).astype(BF)
        dox[rows, :] = g
        prod = g.astype(F32) * of[rows, :]
        for h in range(3):
            part = prod[:, h * 128 : h * 128 + 128].T
            delta[h : h + 1, rows] = jnp.sum(part, axis=0, keepdims=True)

    for qb in range(2):
        rows = slice(qb * 256, qb * 256 + 256)

        def step(j, carry):
            ok = allowed_pairs(clip, qb, j)
            cols = [slice(h * 128, h * 128 + 128) for h in range(3)]
            keys = [kv[j, :, n] for n in cols]
            scores = [jnp.where(ok, matmul_nt(keys[h], q[rows, cols[h]]), NEGATIVE) for h in range(3)]
            grads = [matmul_nt(keys[h], dox[rows, cols[h]]) for h in range(3)]
            probs = [jnp.exp(scores[h] - lse[h : h + 1, rows]) for h in range(3)]
            ds = [(probs[h] * (grads[h] - delta[h : h + 1, rows])).astype(BF) for h in range(3)]
            for h in range(3):
                total[j, :, cols[h]] += matmul(ds[h], q[rows, cols[h]]) + matmul(
                    probs[h].astype(BF), dox[rows, cols[h]]
                )
            return tuple(carry[h] + matmul_tn(keys[h], ds[h]) for h in range(3))

        start = tuple(jnp.zeros((128, 256), F32) for _ in range(3))
        final = lax.fori_loop(bounds[qb][0], bounds[qb][1], step, start)
        for h in range(3):
            part = jnp.where(lane < 64, SCORE_SCALE * final[h].T, 0.0)
            dq[rows, h * 128 : h * 128 + 128] = part.astype(BF)

    ug[...] = jnp.zeros((768, 768), F32)

    def chunk(j, kv_sum):
        z = total[j].astype(BF)
        d_out[j] = matmul_nt(z, w_attn[:, 0:384]).astype(BF)
        ug[:, 0:384] += matmul_tn(unit[j], z)
        return kv_sum + jnp.sum(z.astype(F32), axis=0, keepdims=True)

    kv_sum = lax.fori_loop(bounds[0][0], bounds[1][1], chunk, jnp.zeros((1, 384), F32))
    own = matmul_nt(total[3].astype(BF), w_attn[:, 0:384])
    d_out[3] = (own + matmul_nt(dq[...], w_attn[:, 384:768])).astype(BF)
    ug[:, 384:768] = matmul_tn(unit[3], dq[...])
    q_sum = jnp.sum(dq[...].astype(F32), axis=0, keepdims=True)
    z_sum = jnp.concatenate([kv_sum, q_sum], axis=1)

    line = lax.broadcasted_iota(jnp.int32, (128, 768), 0)

    def place(p, row):
        return jnp.where(line == spots[p + 16 : p + 17, :], row, 0.0)

    columns = vecs[...].T
    gain_col, offset_col = columns[:, 0:1], columns[:, 2:3]
    w_full = w_attn[...].astype(F32)
    gain_sum = jnp.sum(ug[...] * w_full, axis=1, keepdims=True)
    offset_sum = jnp.sum(w_full * z_sum, axis=1, keepdims=True)
    flip = lax.broadcasted_iota(jnp.int32, (768, 128), 1)
    both = jnp.where(flip == 0, gain_sum, jnp.where(flip == 1, offset_sum, 0.0)).T
    own = place(0, both[0:1, :]) + place(2, both[1:2, :])
    for i, p in enumerate((1, 3, 4, 5)):
        own = own + place(p, sums[i : i + 1, :])
    small = matmul_nt(spread_of(ones, 0), own.astype(BF))
    small += matmul_nt(spread_of(ones, 1), place(6, z_sum).astype(BF))
    small += matmul_nt(spread_of(ones, 2), place(7, up_sum[...]).astype(BF))
    small = small.astype(BF)

    ug[...] = ug[...] * gain_col + offset_col * z_sum
    ug[:, 384:768] += matmul_tn(dr[...], of[...].astype(BF))
    for i in range(2):
        g = matmul_tn(ones[SELECT], ug[i * 384 : i * 384 + 384, :].astype(BF))
        grad[i] = g.astype(BF)
        extra = matmul_tn(ones[576:608, 0:512], small[i * 32 : i * 32 + 32, :])
        grad[i, :, 0:128] = (g[:, 0:128] + extra).astype(BF)


def back(*args):
    return pl.pallas_call(
        back_kernel,
        out_shape=[
            jax.ShapeDtypeStruct((7, 512, 768), BF),
            jax.ShapeDtypeStruct((2, 512, 768), BF),
        ],
        in_specs=[SM] + [VM] * (len(args) - 1),
        out_specs=[VM, VM],
        scratch_shapes=[
            pltpu.VMEM((7, 512, 384), F32),
            pltpu.VMEM((512, 384), BF),
            pltpu.VMEM((3, 512), F32),
            pltpu.VMEM((512, 384), BF),
            pltpu.VMEM((768, 768), F32),
        ],
        compiler_params=pltpu.CompilerParams(vmem_limit_bytes=22 * 2**20),
        name="back",
    )(*args)


def finish_kernel(
    own, far, back_one, e1, tok, vecs, ends,
    tokens, g_in, g_qv, g_out, g_up, g_fc, g_down, g_gain, g_row,
):
    t = lax.axis_index("tensor")
    hidden = tok[...].astype(F32)
    centred = hidden - jnp.mean(hidden, axis=-1, keepdims=True)
    scale = lax.rsqrt(jnp.mean(centred * centred, axis=-1, keepdims=True) + EPS)
    unit = centred * scale
    w = back_one[...] * vecs[0:1, :]
    mean_w = jnp.mean(w, axis=-1, keepdims=True)
    mean_wu = jnp.mean(w * unit, axis=-1, keepdims=True)
    tokens[...] = e1[...] + scale * (w - mean_w - unit * mean_wu)

    exact = dict(precision=lax.Precision.HIGHEST, preferred_element_type=F32)
    for n in range(3):
        cols = slice(n * 128, n * 128 + 128)
        parts = []
        for head in (2 * n, 2 * n + 1):
            q, h = head // 3, head % 3
            parts.append(
                (own[q, :, 384 + h * 128 : 512 + h * 128], own[q, :, h * 128 : h * 128 + 128])
            )
        (qo_a, kv_a), (qo_b, kv_b) = parts
        g_in[0, :, 0, cols] = jnp.concatenate([qo_a[:, 0:64], qo_b[:, 0:64]], axis=1)[0:12]
        g_in[1, :, 0, cols] = jnp.concatenate([kv_a[:, 0:64], kv_b[:, 0:64]], axis=1)[0:12]
        g_in[2, :, 0, cols] = jnp.concatenate([kv_a[:, 64:128], kv_b[:, 64:128]], axis=1)[0:12]
        mixed = jnp.concatenate([qo_a[:, 64:128], qo_b[:, 64:128]], axis=1)
        g_out[:, 0, cols] = mixed[0:12]
    for q in range(2):
        cols = slice(q * 768, q * 768 + 768)
        g_up[:, 0, cols] = own[q, 0:12, 768:1536]
        g_down[:, 0, cols] = own[q, 0:12, 1536:2304]
    row0, row1 = own[0, 12:13, 0:128], own[1, 12:13, 0:128]
    vec = row0 + row1 + far[0, 12:13, :] + far[1, 12:13, :]
    lane = lax.broadcasted_iota(jnp.int32, (8, 128), 1)
    line = lax.broadcasted_iota(jnp.int32, (8, 128), 0)

    def pick(row, start, width, stride):
        begin = start + line * stride
        return jnp.where((lane >= begin) & (lane < begin + width), row, 0.0)

    norms = lax.dot_general(pick(vec, 6 * t, 6, 12), ends[0:6, :], NT, **exact)
    g_gain[...] = norms[0:2]
    g_row[...] = norms[2:6]
    heads = lax.dot_general(pick(row0, 72, 3, 3), ends[8:14, :], NT, **exact)
    heads += lax.dot_general(pick(row1, 72, 3, 3), ends[16:22, :], NT, **exact)
    g_qv[...] = heads[0:2]
    hidden_rows = jnp.where(line < 3, pick(row0, 78, 4, 4), pick(row1, 66, 4, 4))
    g_fc[...] = lax.dot_general(ends[24:28, :], hidden_rows, NT, **exact)[:, 0:6]


def finish(*args):
    return pl.pallas_call(
        finish_kernel,
        out_shape=[
            jax.ShapeDtypeStruct(dims, F32)
            for dims in (
                (128, 768),
                (3, 12, 1, 384),
                (2, 6),
                (12, 1, 384),
                (12, 1, 1536),
                (4, 6),
                (12, 1, 1536),
                (2, 6),
                (4, 6),
            )
        ],
        in_specs=[VM] * len(args),
        out_specs=[VM] * 9,
        compiler_params=pltpu.CompilerParams(vmem_limit_bytes=16 * 2**20),
        name="finish",
    )(*args)


def body(
    tokens,
    clip_bounds,
    attn_in,
    qv_bias,
    out_proj,
    fc_in,
    fc_bias,
    fc_out,
    ln_gain,
    row_bias,
    cotangent,
):
    w, f0, f1, clip, near_tokens, tokens, cotangent, ones, spots, last = gather_all(
        clip_bounds,
        tokens,
        cotangent,
        attn_in[0],
        out_proj[0].T,
        fc_in[0],
        fc_out[0].T,
        ln_gain[0],
        row_bias[0],
        qv_bias.reshape(2, 6),
        fc_bias[0].T,
        jnp.asarray(FIRST),
        jnp.asarray(ONES, BF),
        jnp.asarray(SPOTS),
        jnp.asarray(LAST),
    )
    vecs, w_attn, unit, near, query, mixed, lse, attn = front(
        clip, clip, w.reshape(2, 512, 768), ones, spots, near_tokens.reshape(7, 512, 768)
    )
    output, grad_hidden_one, full_attn, sums, up_sum, s0, s1 = mid(
        attn.reshape(4, 128, 768), f0, f1, cotangent, tokens, vecs, ones
    )
    near_back, grad_w = back(
        clip,
        clip,
        query,
        full_attn.reshape(512, 768),
        mixed,
        near,
        lse,
        unit,
        w_attn,
        vecs,
        sums,
        up_sum,
        ones,
        spots,
    )
    back_one, own, far = return_all(
        near_back.reshape(7, 4, 128, 768), grad_w.reshape(2, 4, 4, 2, 16, 768), s0, s1
    )
    grads = finish(
        own, far, back_one, grad_hidden_one, tokens, vecs, last
    )
    grad_tokens, g_in, g_qv, g_out, g_up, g_fc, g_down, g_gain, g_row = grads
    return (
        output,
        grad_tokens,
        g_in.reshape(1, 3, 12, 384),
        g_qv.reshape(1, 2, 6, 1),
        g_out.reshape(12, 384).T[None],
        g_up.reshape(1, 12, 1536),
        g_fc.T[None],
        g_down.reshape(12, 1536).T[None],
        g_gain[None],
        g_row[None],
    )


def solution(mesh):
    return jax.shard_map(
        body,
        mesh=mesh,
        in_specs=(
            P(("dp", "tensor"), None),
            P(None, "dp"),
            P(None, None, "dp", "tensor"),
            P(None, None, "tensor", "dp"),
            P(None, "tensor", "dp"),
            P(None, "dp", "tensor"),
            P(None, "tensor", "dp"),
            P(None, "tensor", "dp"),
            P(None, None, ("dp", "tensor")),
            P(None, None, ("dp", "tensor")),
            P(("dp", "tensor"), None),
        ),
        out_specs=(
            P(("dp", "tensor"), None),
            P(("dp", "tensor"), None),
            P(None, None, "dp", "tensor"),
            P(None, None, "tensor", "dp"),
            P(None, "tensor", "dp"),
            P(None, "dp", "tensor"),
            P(None, "tensor", "dp"),
            P(None, "tensor", "dp"),
            P(None, None, ("dp", "tensor")),
            P(None, None, ("dp", "tensor")),
        ),
        check_vma=False,
    )
```
